32 devices in a mesh: crop: 2 (over x), row: 16 (over z, y, core).
Axes of the slice: x: 2, y: 2, z: 4, core: 2. Of those that a mesh axis runs over, the one named last changes fastest.
Arguments:
- pair_feats: bfloat16 [256, 2, 256, 128], P('row', 'crop'), may hold values from -6 to 6
- node_feats: bfloat16 [256, 2, 256], P('row', 'crop'), may hold values from -6 to 6
- chain_ids: int32 [2, 256], P('crop'), may hold values from 0 to 3, never falling along the last dimension, each value on 1 to 192 neighbouring positions
- out_grad: bfloat16 [256, 2, 256, 128], P('row', 'crop'), may hold values from -6 to 6
- node_out_grad: bfloat16 [256, 2, 256], P('row', 'crop'), may hold values from -6 to 6
- w_attend: float32 [256, 1024], replicated, may hold values from -0.375 to 0.375
- w_pairbias: float32 [128, 8], replicated, may hold values from -0.5 to 0.5
- w_attout: float32 [256, 256], replicated, may hold values from -1 to 1
- w_nodeup: float32 [256, 1024], replicated, may hold values from -0.375 to 0.375
- w_nodedown: float32 [1024, 256], replicated, may hold values from -0.1875 to 0.1875
- w_node: float32 [256, 64], replicated, may hold values from -0.375 to 0.375
- w_outer: float32 [1024, 128], replicated, may hold values from -0.1875 to 0.1875
- w_in: float32 [128, 1152], replicated, may hold values from -0.5 to 0.5
- w_z: float32 [256, 128], replicated, may hold values from -0.375 to 0.375
- w_up: float32 [128, 512], replicated, may hold values from -0.5 to 0.5
- w_down: float32 [512, 128], replicated, may hold values from -0.25 to 0.25
- ln_gains: float32 [1408], replicated, may hold values from 0.5 to 1.5
- m_attend: float32 [256, 1024], replicated
- m_pairbias: float32 [128, 8], replicated
- m_attout: float32 [256, 256], replicated
- m_nodeup: float32 [256, 1024], replicated
- m_nodedown: float32 [1024, 256], replicated
- m_node: float32 [256, 64], replicated
- m_outer: float32 [1024, 128], replicated
- m_in: float32 [128, 1152], replicated
- m_z: float32 [256, 128], replicated
- m_up: float32 [128, 512], replicated
- m_down: float32 [512, 128], replicated
- m_gains: float32 [1408], replicated
- v_attend: float32 [256, 1024], replicated, as said below
- v_pairbias: float32 [128, 8], replicated, as said below
- v_attout: float32 [256, 256], replicated, as said below
- v_nodeup: float32 [256, 1024], replicated, as said below
- v_nodedown: float32 [1024, 256], replicated, as said below
- v_node: float32 [256, 64], replicated, as said below
- v_outer: float32 [1024, 128], replicated, as said below
- v_in: float32 [128, 1152], replicated, as said below
- v_z: float32 [256, 128], replicated, as said below
- v_up: float32 [128, 512], replicated, as said below
- v_down: float32 [512, 128], replicated, as said below
- v_gains: float32 [1408], replicated, as said below
Outputs:
- pair_out: bfloat16 [256, 2, 256, 128], P('row', 'crop')
- node_out: bfloat16 [256, 2, 256], P('row', 'crop')
- pair_grad: float32 [256, 2, 256, 128], P('row', 'crop')
- node_grad: float32 [256, 2, 256], P('row', 'crop')
- attend_first: float32 [256, 1024], replicated
- attend_second: float32 [256, 1024], replicated
- attend_master: float32 [256, 1024], replicated
- pairbias_first: float32 [128, 8], replicated
- pairbias_second: float32 [128, 8], replicated
- pairbias_master: float32 [128, 8], replicated
- attout_first: float32 [256, 256], replicated
- attout_second: float32 [256, 256], replicated
- attout_master: float32 [256, 256], replicated
- nodeup_first: float32 [256, 1024], replicated
- nodeup_second: float32 [256, 1024], replicated
- nodeup_master: float32 [256, 1024], replicated
- nodedown_first: float32 [1024, 256], replicated
- nodedown_second: float32 [1024, 256], replicated
- nodedown_master: float32 [1024, 256], replicated
- node_first: float32 [256, 64], replicated
- node_second: float32 [256, 64], replicated
- node_master: float32 [256, 64], replicated
- outer_first: float32 [1024, 128], replicated
- outer_second: float32 [1024, 128], replicated
- outer_master: float32 [1024, 128], replicated
- inproj_first: float32 [128, 1152], replicated
- inproj_second: float32 [128, 1152], replicated
- inproj_master: float32 [128, 1152], replicated
- zproj_first: float32 [256, 128], replicated
- zproj_second: float32 [256, 128], replicated
- zproj_master: float32 [256, 128], replicated
- upproj_first: float32 [128, 512], replicated
- upproj_second: float32 [128, 512], replicated
- upproj_master: float32 [128, 512], replicated
- downproj_first: float32 [512, 128], replicated
- downproj_second: float32 [512, 128], replicated
- downproj_master: float32 [512, 128], replicated
- gains_first: float32 [1408], replicated
- gains_second: float32 [1408], replicated
- gains_master: float32 [1408], replicated
The draws below stay inside these ranges and needn't reach their ends.
Inputs may be any that keep to these rules, and one draw needn't show every extreme that they name: `chain_ids`: along each crop the chain index never falls; each chain has at most 192 residues and one has exactly that many. `v_attend`: positive. `v_pairbias`: positive. `v_attout`: positive. `v_nodeup`: positive. `v_nodedown`: positive. `v_node`: positive. `v_outer`: positive. `v_in`: positive. `v_z`: positive. `v_up`: positive. `v_down`: positive. `v_gains`: positive.
All inputs are finite; a program needn't handle non-finite values.
Results may differ from the reference program's by a relative error of at most 0.017.
Values may be sent and summed in bfloat16 or wider, within the bound.
No kernel may reach another device: no remote copies, remote signals or barrier semaphores. Data moves between devices by JAX's collectives and lax.ppermute only.
A program may use at most 256 MiB of HBM per device.

```python
import math
import jax
import jax.numpy as jnp
import numpy as np
from jax import lax

CS = 256
HEADS = 8
NFF = 1024
CZ = 128
OP = 32
HID = 128
FF = 512
NRES = 256
CHAINS = 4
ADAM_STEP = 4
CROPS = 2
GAINS = 1408


def grad_level(factor):
    return factor * math.sqrt(CROPS * NRES * NRES)


def first_draw(key, label, arr_dims, factor):
    own_key = jax.random.fold_in(key, label)
    return grad_level(factor) / 9.0 * jax.random.truncated_normal(own_key, -4.0, 4.0, arr_dims, jnp.float32)


def second_draw(key, label, arr_dims, factor):
    own_key = jax.random.fold_in(key, label)
    level_now = grad_level(factor)
    spread_vals = jnp.exp(jax.random.uniform(own_key, arr_dims, jnp.float32, 0.0, math.log(4.0)))
    return 0.001 / 0.999 * level_now * level_now * spread_vals


def draw_m_attend(key, part):
    return first_draw(key, 101, (CS, 4 * CS), 1.0)


def draw_m_pairbias(key, part):
    return first_draw(key, 102, (CZ, HEADS), 3.0)


def draw_m_attout(key, part):
    return first_draw(key, 103, (CS, CS), 0.25)


def draw_m_nodeup(key, part):
    return first_draw(key, 104, (CS, NFF), 0.4)


def draw_m_nodedown(key, part):
    return first_draw(key, 105, (NFF, CS), 0.7)


def draw_m_node(key, part):
    return first_draw(key, 106, (CS, 2 * OP), 2.0)


def draw_m_outer(key, part):
    return first_draw(key, 107, (OP * OP, CZ), 1.0)


def draw_m_in(key, part):
    return first_draw(key, 108, (CZ, 8 * HID + CZ), 0.5)


def draw_m_z(key, part):
    return first_draw(key, 109, (2 * HID, CZ), 0.5)


def draw_m_up(key, part):
    return first_draw(key, 110, (CZ, FF), 0.7)


def draw_m_down(key, part):
    return first_draw(key, 111, (FF, CZ), 0.6)


def draw_m_gains(key, part):
    return first_draw(key, 112, (GAINS,), 1.0)


def draw_v_attend(key, part):
    return second_draw(key, 201, (CS, 4 * CS), 1.0)


def draw_v_pairbias(key, part):
    return second_draw(key, 202, (CZ, HEADS), 3.0)


def draw_v_attout(key, part):
    return second_draw(key, 203, (CS, CS), 0.25)


def draw_v_nodeup(key, part):
    return second_draw(key, 204, (CS, NFF), 0.4)


def draw_v_nodedown(key, part):
    return second_draw(key, 205, (NFF, CS), 0.7)


def draw_v_node(key, part):
    return second_draw(key, 206, (CS, 2 * OP), 2.0)


def draw_v_outer(key, part):
    return second_draw(key, 207, (OP * OP, CZ), 1.0)


def draw_v_in(key, part):
    return second_draw(key, 208, (CZ, 8 * HID + CZ), 0.5)


def draw_v_z(key, part):
    return second_draw(key, 209, (2 * HID, CZ), 0.5)


def draw_v_up(key, part):
    return second_draw(key, 210, (CZ, FF), 0.7)


def draw_v_down(key, part):
    return second_draw(key, 211, (FF, CZ), 0.6)


def draw_v_gains(key, part):
    return second_draw(key, 212, (GAINS,), 1.0)


def shard_levels(key, shape, shards, low, high):
    def one(position, shards_of):
        steps = jax.random.uniform(jax.random.fold_in(jax.random.fold_in(key, 6), position), (shards_of,), jnp.float32, low / len(shards), high / len(shards))
        return jnp.repeat(jnp.exp(steps), shape[position] // shards_of).reshape((-1,) + (1,) * (len(shape) - position - 1))

    gain = one(*shards[0])
    for cut in shards[1:]:
        gain = gain * one(*cut)
    return gain


def length_profile(number_of, total, reach, slope):
    loads = [(1 << 20) // math.isqrt(standing ** slope) + 1 for standing in range(2, number_of + 1)]
    spare, counts = total - reach - (number_of - 1), [1] * (number_of - 1)
    while spare > 0:
        movable = [i for i in range(number_of - 1) if counts[i] < reach]
        pool, budget = sum([loads[i] for i in movable]), spare
        for i in movable:
            more = min(reach - counts[i], max(1, budget * loads[i] // pool), spare)
            counts[i] = counts[i] + more
            spare = spare - more
    return np.array([reach] + counts)


def ragged(rng, count, total, most, skew):
    if count == 2:
        one = jax.random.randint(rng, (), max(1, total - most), min(most, total - 1) + 1)
        return jnp.stack([one, total - one])
    tallies = jnp.asarray(length_profile(count, total, most, skew), jnp.int32)
    pairs = (count - 1) // 2
    donor, sink = tallies[1:1 + 2 * pairs:2], tallies[2:2 + 2 * pairs:2]
    room = jnp.minimum(donor - 1, most - sink)
    shifted = jax.random.randint(jax.random.fold_in(rng, 1), (pairs,), 0, 1 << 20) % (room + 1)
    tallies = tallies.at[1:1 + 2 * pairs:2].set(donor - shifted).at[2:2 + 2 * pairs:2].set(sink + shifted)
    return tallies[jax.random.permutation(jax.random.fold_in(rng, 2), count)]


def scatter_about(rng, extent, deviation, bound, pieces=(), kind=jnp.bfloat16):
    level = shard_levels(rng, extent, pieces, -0.22, 0.18) if pieces else 1.0
    drawn = jax.random.normal(rng, extent, jnp.float32) * deviation * level
    return jnp.minimum(jnp.maximum(drawn, -bound), bound).astype(kind)


def setup_inputs(seed: int = 0) -> dict:
    seeds = jax.random.split(jax.random.key(seed), 42)
    return {
        "pair_feats": scatter_about(seeds[0], (NRES, CROPS, NRES, CZ), 1.0, 6.0, ((0, 16), (1, 2))),
        "node_feats": scatter_about(seeds[1], (NRES, CROPS, CS), 1.0, 6.0, ((0, 16), (1, 2))),
        "chain_ids": jax.vmap(lambda own: jnp.searchsorted(jnp.cumsum(ragged(own, CHAINS, NRES, NRES * 3 // 4, 1)), jnp.arange(NRES), side="right"))(jax.random.split(seeds[2], CROPS)).reshape((CROPS, NRES)).astype(jnp.int32),
        "out_grad": scatter_about(seeds[3], (NRES, CROPS, NRES, CZ), 1.0, 6.0, ((0, 16), (1, 2))),
        "node_out_grad": scatter_about(seeds[4], (NRES, CROPS, CS), 1.0, 6.0, ((0, 16), (1, 2))),
        "w_attend": scatter_about(seeds[5], (CS, 4 * CS), CS ** -0.5, 0.375, (), jnp.float32),
        "w_pairbias": scatter_about(seeds[6], (CZ, HEADS), CZ ** -0.5, 0.5, (), jnp.float32),
        "w_attout": scatter_about(seeds[7], (CS, CS), (CS // 8) ** -0.5, 1.0, (), jnp.float32),
        "w_nodeup": scatter_about(seeds[8], (CS, NFF), CS ** -0.5, 0.375, (), jnp.float32),
        "w_nodedown": scatter_about(seeds[9], (NFF, CS), NFF ** -0.5, 0.1875, (), jnp.float32),
        "w_node": scatter_about(seeds[10], (CS, 2 * OP), CS ** -0.5, 0.375, (), jnp.float32),
        "w_outer": scatter_about(seeds[11], (OP * OP, CZ), (OP * OP) ** -0.5, 0.1875, (), jnp.float32),
        "w_in": scatter_about(seeds[12], (CZ, 8 * HID + CZ), CZ ** -0.5, 0.5, (), jnp.float32),
        "w_z": scatter_about(seeds[13], (2 * HID, CZ), (2 * HID) ** -0.5, 0.375, (), jnp.float32),
        "w_up": scatter_about(seeds[14], (CZ, FF), CZ ** -0.5, 0.5, (), jnp.float32),
        "w_down": scatter_about(seeds[15], (FF, CZ), FF ** -0.5, 0.25, (), jnp.float32),
        "ln_gains": jnp.clip(1.0 + 0.1 * jax.random.normal(seeds[16], (GAINS,), jnp.float32), 0.5, 1.5),
        "m_attend": draw_m_attend(jax.random.fold_in(seeds[41], 71), 0),
        "m_pairbias": draw_m_pairbias(jax.random.fold_in(seeds[41], 71), 0),
        "m_attout": draw_m_attout(jax.random.fold_in(seeds[41], 71), 0),
        "m_nodeup": draw_m_nodeup(jax.random.fold_in(seeds[41], 71), 0),
        "m_nodedown": draw_m_nodedown(jax.random.fold_in(seeds[41], 71), 0),
        "m_node": draw_m_node(jax.random.fold_in(seeds[41], 71), 0),
        "m_outer": draw_m_outer(jax.random.fold_in(seeds[41], 71), 0),
        "m_in": draw_m_in(jax.random.fold_in(seeds[41], 71), 0),
        "m_z": draw_m_z(jax.random.fold_in(seeds[41], 71), 0),
        "m_up": draw_m_up(jax.random.fold_in(seeds[41], 71), 0),
        "m_down": draw_m_down(jax.random.fold_in(seeds[41], 71), 0),
        "m_gains": draw_m_gains(jax.random.fold_in(seeds[41], 71), 0),
        "v_attend": draw_v_attend(jax.random.fold_in(seeds[41], 71), 0),
        "v_pairbias": draw_v_pairbias(jax.random.fold_in(seeds[41], 71), 0),
        "v_attout": draw_v_attout(jax.random.fold_in(seeds[41], 71), 0),
        "v_nodeup": draw_v_nodeup(jax.random.fold_in(seeds[41], 71), 0),
        "v_nodedown": draw_v_nodedown(jax.random.fold_in(seeds[41], 71), 0),
        "v_node": draw_v_node(jax.random.fold_in(seeds[41], 71), 0),
        "v_outer": draw_v_outer(jax.random.fold_in(seeds[41], 71), 0),
        "v_in": draw_v_in(jax.random.fold_in(seeds[41], 71), 0),
        "v_z": draw_v_z(jax.random.fold_in(seeds[41], 71), 0),
        "v_up": draw_v_up(jax.random.fold_in(seeds[41], 71), 0),
        "v_down": draw_v_down(jax.random.fold_in(seeds[41], 71), 0),
        "v_gains": draw_v_gains(jax.random.fold_in(seeds[41], 71), 0),
    }


@jax.custom_vjp
def low(v):
    return lax.optimization_barrier(v.astype(jnp.bfloat16)).astype(jnp.float32)

@jax.custom_vjp
def low_back(v):
    return v

def low_keep(v):
    return (low(v), None)

def low_pass(kept, grad):
    return (grad,)

def back_keep(v):
    return (v, None)

def back_low(kept, grad):
    return (low(grad),)
low.defvjp(low_keep, low_pass)
low_back.defvjp(back_keep, back_low)
exact_mode = lax.Precision.HIGHEST

def layer_norm(values, gain_vec):
    centred = values - lax.optimization_barrier(jnp.mean(values, axis=-1, keepdims=True))
    spread = lax.optimization_barrier(jnp.mean(centred * centred, axis=-1, keepdims=True))
    return centred * lax.rsqrt(spread + 1e-05) * gain_vec

def matmul_full(left, right):
    return jnp.dot(left, right, precision=exact_mode, preferred_element_type=jnp.float32)

def crop_forward(params, pair_in, node_in, chain_row):
    w_attend, w_pairbias, w_attout, w_nodeup, w_nodedown, w_node, w_outer, w_in, w_z, w_up, w_down, ln_gains = params
    width_s = node_in.shape[-1]
    width_z = pair_in.shape[-1]
    residues = node_in.shape[0]
    head_count = w_pairbias.shape[1]
    head_dim = width_s // head_count
    score_scale = 1.0 / head_dim ** 0.5
    outer_dim = w_node.shape[1] // 2
    hidden = (w_in.shape[1] - width_z) // 8
    offset_b = width_s
    offset_n = offset_b + width_z
    offset_s = offset_n + width_s
    offset_x = offset_s + width_s
    offset_t = offset_x + width_z
    offset_h = offset_t + 2 * hidden
    gain_a = ln_gains[:offset_b]
    gain_b = ln_gains[offset_b:offset_n]
    gain_n = ln_gains[offset_n:offset_s]
    gain_s = ln_gains[offset_s:offset_x]
    gain_x = ln_gains[offset_x:offset_t]
    gain_t = ln_gains[offset_t:offset_h]
    gain_h = ln_gains[offset_h:]
    same_chain = chain_row[:, None] == chain_row[None, :]
    pair_mask = same_chain.astype(jnp.float32)[..., None]
    att_norm = low(layer_norm(node_in, gain_a))
    qkvg = low_back(matmul_full(att_norm, low(w_attend)))
    query = low(qkvg[:, :width_s]).reshape(residues, head_count, head_dim)
    key_vec = low(qkvg[:, width_s:2 * width_s]).reshape(residues, head_count, head_dim)
    value_vec = low(qkvg[:, 2 * width_s:3 * width_s]).reshape(residues, head_count, head_dim)
    att_gate = jax.nn.sigmoid(qkvg[:, 3 * width_s:])
    bias_norm = low(layer_norm(pair_in, gain_b))
    pair_bias = matmul_full(bias_norm, low(w_pairbias))
    raw_scores = jnp.einsum('ihd,jhd->hij', query, key_vec, precision=exact_mode) * score_scale + jnp.transpose(pair_bias, (2, 0, 1))
    scores = low_back(jnp.where(same_chain[None], raw_scores, -1000000000.0))
    weights = low(jax.nn.softmax(scores, axis=-1))
    attn = low_back(jnp.einsum('hij,jhd->ihd', weights, value_vec, precision=exact_mode)).reshape(residues, width_s)
    gated = low(att_gate * attn)
    node_mid = node_in + low_back(matmul_full(gated, low(w_attout)))
    trans_node = low(layer_norm(node_mid, gain_n))
    node_upv = low_back(matmul_full(trans_node, low(w_nodeup)))
    node_act = low(jax.nn.gelu(node_upv, approximate=True))
    node_next = node_mid + low_back(matmul_full(node_act, low(w_nodedown)))
    node_w = low(w_node)
    outer_w = low(w_outer).reshape(outer_dim, outer_dim * width_z)
    in_w = low(w_in)
    z_w = low(w_z)
    up_w = low(w_up)
    down_w = low(w_down)
    node_norm = low(layer_norm(node_next, gain_s))
    node_proj = low_back(low(matmul_full(node_norm, node_w)))
    left_vec = node_proj[:, :outer_dim]
    right_vec = node_proj[:, outer_dim:]
    outer_mix = low_back(low(matmul_full(left_vec, outer_w))).reshape(-1, outer_dim, width_z)
    outer_out = low_back(jnp.einsum('jb,ibc->ijc', right_vec, outer_mix, precision=exact_mode))
    first_sum = pair_in + outer_out
    pair_norm = low(layer_norm(first_sum, gain_x))
    projected = low_back(matmul_full(pair_norm, in_w))
    gated_acts = low_back(low(jax.nn.sigmoid(projected[..., 4 * hidden:8 * hidden]) * projected[..., :4 * hidden] * pair_mask))
    left_out = gated_acts[..., :hidden]
    right_out = gated_acts[..., hidden:2 * hidden]
    left_in = gated_acts[..., 2 * hidden:3 * hidden]
    right_in = gated_acts[..., 3 * hidden:]
    tri_out = jnp.einsum('ikh,jkh->ijh', left_out, right_out, precision=exact_mode)
    tri_in = jnp.einsum('kih,kjh->ijh', left_in, right_in, precision=exact_mode)
    combined = low_back(jnp.concatenate([tri_out, tri_in], axis=-1))
    tri_norm = low(layer_norm(combined, gain_t))
    tri_proj = low_back(matmul_full(tri_norm, z_w))
    second_sum = first_sum + jax.nn.sigmoid(projected[..., 8 * hidden:]) * tri_proj * pair_mask
    trans_in = low(layer_norm(second_sum, gain_h))
    up_proj = low_back(matmul_full(trans_in, up_w))
    activated = low(jax.nn.gelu(up_proj, approximate=True))
    down_proj = low_back(matmul_full(activated, down_w))
    return (second_sum + down_proj, node_next)

def adam_step(master, first_old, second_old, grad_total, rate, decay):
    first_new = 0.9 * first_old + 0.1 * grad_total
    second_new = 0.999 * second_old + 0.001 * grad_total * grad_total
    first_hat = first_new / (1.0 - 0.9 ** ADAM_STEP)
    second_hat = second_new / (1.0 - 0.999 ** ADAM_STEP)
    master_new = master - rate * (first_hat / (jnp.sqrt(second_hat) + 1e-08) + decay * master)
    return (first_new, second_new, master_new)

def reference(pair_feats, node_feats, chain_ids, out_grad, node_out_grad, w_attend, w_pairbias, w_attout, w_nodeup, w_nodedown, w_node, w_outer, w_in, w_z, w_up, w_down, ln_gains, m_attend, m_pairbias, m_attout, m_nodeup, m_nodedown, m_node, m_outer, m_in, m_z, m_up, m_down, m_gains, v_attend, v_pairbias, v_attout, v_nodeup, v_nodedown, v_node, v_outer, v_in, v_z, v_up, v_down, v_gains):
    params = (w_attend, w_pairbias, w_attout, w_nodeup, w_nodedown, w_node, w_outer, w_in, w_z, w_up, w_down, ln_gains)
    pair_crops = jnp.transpose(pair_feats.astype(jnp.float32), (1, 0, 2, 3))
    node_crops = jnp.transpose(node_feats.astype(jnp.float32), (1, 0, 2))
    checked = jax.checkpoint(crop_forward)

    def forward(param_set, pair_all, node_all):
        return lax.map(lambda crop_args: checked(param_set, crop_args[0], crop_args[1], crop_args[2]), (pair_all, node_all, chain_ids))
    outputs, pull_back = jax.vjp(forward, params, pair_crops, node_crops)
    pair_cot_in = jnp.transpose(out_grad.astype(jnp.float32), (1, 0, 2, 3))
    node_cot_in = jnp.transpose(node_out_grad.astype(jnp.float32), (1, 0, 2))
    param_grads, pair_cot, node_cot = pull_back((pair_cot_in, node_cot_in))
    pair_out = jnp.transpose(outputs[0], (1, 0, 2, 3)).astype(jnp.bfloat16)
    node_out = jnp.transpose(outputs[1], (1, 0, 2)).astype(jnp.bfloat16)
    pair_grad = jnp.transpose(pair_cot, (1, 0, 2, 3))
    node_grad = jnp.transpose(node_cot, (1, 0, 2))
    firsts = (m_attend, m_pairbias, m_attout, m_nodeup, m_nodedown, m_node, m_outer, m_in, m_z, m_up, m_down, m_gains)
    seconds = (v_attend, v_pairbias, v_attout, v_nodeup, v_nodedown, v_node, v_outer, v_in, v_z, v_up, v_down, v_gains)
    results = [pair_out, node_out, pair_grad, node_grad]
    for index in range(12):
        rate = 1.0 if index == 11 else 0.1
        decay = 0.0 if index == 11 else 0.1
        first_new, second_new, master_new = adam_step(params[index], firsts[index], seconds[index], param_grads[index], rate, decay)
        results.append(first_new)
        results.append(second_new)
        results.append(master_new)
    return tuple(results)
```

```python
import functools
import jax
import jax.numpy as jnp
from jax import lax
from jax.experimental import pallas as pl
from jax.experimental.pallas import tpu as pltpu
from jax.sharding import PartitionSpec as P

ADAM_STEP = 4
EPS = 1e-05
BF = jnp.bfloat16
F32 = jnp.float32
LANES = 128
HALF = 64
BOTH = ("crop", "row")
NN = (((1,), (0,)), ((), ()))
NT = (((1,), (1,)), ((), ()))
TN = (((0,), (0,)), ((), ()))


def mm(left, right, dims=NN):
    return lax.dot_general(left, right, dims, preferred_element_type=F32)


def layer_norm(values, gain_vec):
    centred = values - jnp.mean(values, axis=-1, keepdims=True)
    spread = jnp.mean(centred * centred, axis=-1, keepdims=True)
    return centred * lax.rsqrt(spread + EPS) * gain_vec


def gelu_tanh(values):
    return jax.nn.gelu(values, approximate=True)


def back_dot(left, weight):
    return mm(left, weight, NT)


def cross_sum(left, right):
    return mm(left, right, TN)


def adam_step(master, first_old, second_old, grad_total, rate, decay):
    first_new = 0.9 * first_old + 0.1 * grad_total
    second_new = 0.999 * second_old + 0.001 * grad_total * grad_total
    first_hat = first_new / (1.0 - 0.9**ADAM_STEP)
    second_hat = second_new / (1.0 - 0.999**ADAM_STEP)
    master_new = master - rate * (first_hat / (jnp.sqrt(second_hat) + 1e-08) + decay * master)
    return (first_new, second_new, master_new)


def gather_all(part, row_devices):
    every = 2 * row_devices
    groups = [[d for d in range(every) if d % 2 == k] for k in range(2)]
    spread = jnp.broadcast_to(part[None], (every // 2,) + part.shape)
    got = lax.all_to_all(
        spread, BOTH, split_axis=0, concat_axis=0, tiled=True, axis_index_groups=groups
    )
    other = lax.ppermute(got, "row", [(d, d ^ 1) for d in range(row_devices)])
    odd = lax.axis_index("row") % 2 == 1
    pair = [jnp.where(odd, other, got), jnp.where(odd, got, other)]
    return jnp.stack(pair, axis=1).reshape((every,) + part.shape)


def scatter_sum(flat, row_devices):
    every = 2 * row_devices
    unit = every * 16 * LANES
    sent = jnp.pad(flat, (0, -flat.shape[0] % unit)).astype(BF).reshape(every, -1, LANES)
    parts = lax.all_to_all(sent, BOTH, split_axis=0, concat_axis=0, tiled=True)
    return jnp.sum(parts.astype(F32), axis=0).astype(BF)


def after(value, event):
    return lax.optimization_barrier((value, event))[0]


def join_flat(parts):
    return jnp.concatenate([part.reshape(-1) for part in parts])


def split_flat(flat, parts):
    found, start = [], 0
    for part in parts:
        found.append(flat[start : start + part.size].reshape(part.shape))
        start = start + part.size
    return found


def lanes_sum(acc):
    return jnp.sum(acc, axis=1)


def norm_rows(values):
    centred = values - jnp.mean(values, axis=0, keepdims=True)
    inv = lax.rsqrt(jnp.mean(centred * centred, axis=0, keepdims=True) + EPS)
    return centred * inv, inv


def norm_rows_back(scaled, hat, inv):
    return inv * (
        scaled
        - jnp.mean(scaled, axis=0, keepdims=True)
        - hat * jnp.mean(scaled * hat, axis=0, keepdims=True)
    )


def turn(values):
    return pltpu.roll(values, HALF, values.ndim - 1)


def low_lanes(shape):
    return lax.broadcasted_iota(jnp.int32, shape, len(shape) - 1) < HALF


def fold_pair(first, second):
    low = low_lanes((first.shape[0], LANES))
    f_lo, f_hi = first[:, :LANES], first[:, LANES:]
    s_lo, s_hi = second[:, :LANES], second[:, LANES:]
    f_turn, s_turn = turn(f_hi), turn(s_hi)
    main_f = f_lo + jnp.where(low, f_turn, 0.0)
    main_s = s_lo + jnp.where(low, s_turn, 0.0)
    return main_f, main_s, jnp.where(low, f_hi, s_turn)


def unfold_pair(main_f, main_s, tail):
    low = low_lanes(tail.shape)
    first = jnp.concatenate([main_f, jnp.where(low, tail, turn(main_f))], axis=1)
    second = jnp.concatenate([main_s, jnp.where(low, turn(tail), turn(main_s))], axis=1)
    return first, second


def put_tile(stage_ref, tile, row, rows, values):
    high = values.shape[0]
    stage_ref[pl.ds(tile * high * rows + row, high, stride=rows), :] = values


def get_tile(stage_ref, tile, row, rows, high):
    return stage_ref[pl.ds(tile * high * rows + row, high, stride=rows), :]


def ship(stage_ref, send_ref, tiles, share, rows):
    devices = send_ref.shape[0]
    span = share * rows
    for t in range(tiles):
        block = stage_ref[t * devices * span : (t + 1) * devices * span]
        send_ref[:, t * span : (t + 1) * span] = block.reshape(devices, span, LANES).astype(BF)


def unship(got_ref, stage_ref, tiles, share, rows):
    devices = got_ref.shape[0]
    span = share * rows
    for t in range(tiles):
        block = got_ref[:, t * span : (t + 1) * span].astype(F32)
        stage_ref[t * devices * span : (t + 1) * devices * span] = block.reshape(-1, LANES)


def bias_kernel(x_ref, gain_ref, weight_ref, xt_ref, bias_ref):
    for r in range(x_ref.shape[0]):
        xt = x_ref[r].astype(F32).T
        xt_ref[r] = xt.astype(BF)
        hat, _ = norm_rows(xt)
        bias_ref[r] = mm(weight_ref[...], (hat * gain_ref[...]).astype(BF))


def first_kernel(
    share, rows, xt_ref, mix_ref, right_ref, mask_ref, gain_ref, weight_ref, ride_ref,
    sum_ref, send_ref, *stage,
):
    hidden = weight_ref.shape[0] // 9
    for r in range(xt_ref.shape[0]):
        row = pl.program_id(0) * xt_ref.shape[0] + r
        total = xt_ref[r].astype(F32) + mm(mix_ref[r], right_ref[...], TN)
        sum_ref[r] = total
        hat, _ = norm_rows(total)
        norm = (hat * gain_ref[...]).astype(BF)
        mask = mask_ref[r]
        acts = []
        for block in range(4):
            value = mm(weight_ref[block * hidden : (block + 1) * hidden], norm)
            gate = mm(weight_ref[(block + 4) * hidden : (block + 5) * hidden], norm)
            acts.append(jax.nn.sigmoid(gate) * value * mask)
        for pair in range(2):
            tiles = fold_pair(acts[2 * pair], acts[2 * pair + 1])
            for t in range(3):
                if stage:
                    put_tile(stage[0], 3 * pair + t, row, rows, tiles[t])
                else:
                    send_ref[r, 3 * pair + t] = tiles[t].astype(BF)
    if stage:

        @pl.when(pl.program_id(0) == pl.num_programs(0) - 1)
        def _():
            ship(stage[0], send_ref, 6, share, rows)
            send_ref[:, 6 * share * rows :] = ride_ref[...]


def chain_mask(col_ref, row_ref):
    return col_ref[...] == row_ref[...]


def channel_rows(dims, tile):
    share, rows = dims
    return pl.ds(pl.multiple_of((tile * share + pl.program_id(0)) * rows, rows), rows)


def flat_rows(ref, tile, dims):
    block = ref[:, channel_rows(dims, tile)] if dims else ref[:, tile, 0]
    return block.reshape(-1, block.shape[-1])


def slot_operands(ref, pair, dims):
    main_f, main_s, tail = (flat_rows(ref, 3 * pair + t, dims).astype(F32) for t in range(3))
    low = low_lanes(tail.shape)
    zero = jnp.zeros_like(tail)
    first = jnp.concatenate([main_f, jnp.where(low, tail, zero)], axis=1).astype(BF)
    second = jnp.concatenate([main_s, jnp.where(low, turn(tail), zero)], axis=1).astype(BF)
    return first, second


def raw_columns(slots, same):
    values = slots.astype(F32)
    main, tail = values[:, :LANES], values[:, LANES:]
    wide = jnp.concatenate(
        [main, jnp.where(low_lanes(tail.shape), tail, turn(main))], axis=1
    )
    return jnp.where(same, wide, 0.0).astype(BF)


def store_tiles(out_ref, pair, dims, tiles):
    for t in range(3):
        block = tiles[t].astype(BF).reshape(out_ref.shape[0], -1, LANES)
        if dims:
            out_ref[:, channel_rows(dims, 3 * pair + t)] = block
        else:
            out_ref[:, 3 * pair + t, 0] = block


def tri_kernel(dims, col_ref, row_ref, acts_ref, out_ref):
    same = chain_mask(col_ref, row_ref)
    left_out, right_out = slot_operands(acts_ref, 0, dims)
    left_in, right_in = slot_operands(acts_ref, 1, dims)
    outgoing = jnp.where(same, mm(left_out, right_out, NT), 0.0)
    incoming = mm(raw_columns(left_in, same), right_in, TN)
    low = low_lanes((outgoing.shape[0], LANES))
    o_lo, o_hi = outgoing[:, :LANES], outgoing[:, LANES:]
    main_o = o_lo + jnp.where(low, turn(o_hi), 0.0)
    tail = jnp.where(low, o_hi, turn(incoming[:, LANES:]))
    store_tiles(out_ref, 0, dims, (main_o, incoming[:, :LANES], tail))


def tri_back_kernel(dims, col_ref, row_ref, acts_ref, grad_ref, out_ref):
    same = chain_mask(col_ref, row_ref)
    left_out, right_out = slot_operands(acts_ref, 0, dims)
    left_in, right_in = slot_operands(acts_ref, 1, dims)
    grad_out, grad_in = slot_operands(grad_ref, 0, dims)
    raw_out = raw_columns(grad_out, same)
    d_left = mm(raw_out, right_out)
    d_right = mm(raw_out, left_out, TN)
    low = low_lanes((d_left.shape[0], LANES))
    tail = jnp.where(low, d_left[:, LANES:], turn(d_right[:, LANES:]))
    store_tiles(out_ref, 0, dims, (d_left[:, :LANES], d_right[:, :LANES], tail))
    d_left = jnp.where(same, mm(right_in, grad_in, NT), 0.0)
    d_right = mm(raw_columns(left_in, same), grad_in)
    l_lo, l_hi = d_left[:, :LANES], d_left[:, LANES:]
    main_l = l_lo + jnp.where(low, turn(l_hi), 0.0)
    tail = jnp.where(low, l_hi, turn(d_right[:, LANES:]))
    store_tiles(out_ref, 1, dims, (main_l, d_right[:, :LANES], tail))


def second_kernel(
    share, rows, sum_ref, tri_ref, grad_ref, mask_ref, gx_ref, gt_ref, gh_ref,
    wgate_ref, wzt_ref, wz_ref, wut_ref, wu_ref, wdt_ref, wd_ref,
    out_ref, ds_ref, dlogit_ref, send_ref, gd_ref, gu_ref, gz_ref, gaint_ref, gainh_ref,
    *stage,
):
    @pl.when(pl.program_id(0) == 0)
    def _():
        for acc in (gd_ref, gu_ref, gz_ref, gaint_ref, gainh_ref):
            acc[...] = jnp.zeros_like(acc)
        if stage:
            unship(tri_ref, stage[0], 3, share, rows)

    for r in range(sum_ref.shape[0]):
        row = pl.program_id(0) * sum_ref.shape[0] + r
        total = sum_ref[r]
        mask = mask_ref[r]
        hat_x, _ = norm_rows(total)
        norm = (hat_x * gx_ref[...]).astype(BF)
        out_gate = jax.nn.sigmoid(mm(wgate_ref[...], norm))
        if stage:
            tiles = [get_tile(stage[0], t, row, rows, total.shape[0]) for t in range(3)]
        else:
            tiles = [tri_ref[r, t].astype(F32) for t in range(3)]
        tri_out, tri_in = unfold_pair(*tiles)
        hat_t, inv_t = norm_rows(jnp.concatenate([tri_out, tri_in], axis=0))
        tri_norm = (hat_t * gt_ref[...]).astype(BF)
        tri_proj = mm(wzt_ref[...], tri_norm)
        second = total + out_gate * tri_proj * mask
        hat_h, inv_h = norm_rows(second)
        trans_in = (hat_h * gh_ref[...]).astype(BF)
        up = mm(wut_ref[...], trans_in)
        square = up * up
        curve = jnp.tanh(0.7978845608 * up * (1.0 + 0.044715 * square))
        half = 0.5 * (1.0 + curve)
        act = (up * half).astype(BF)
        slope = half + up * (1.0 - curve * curve) * (0.3989422804 + 0.05351611220 * square)
        out_ref[r] = (second + mm(wdt_ref[...], act)).T.astype(BF)
        grad_low = grad_ref[r].astype(F32).T.astype(BF)
        gd_ref[...] += mm(act, grad_low, NT)
        d_up = (mm(wd_ref[...], grad_low) * slope).astype(BF)
        gu_ref[...] += mm(d_up, trans_in, NT)
        back = mm(wu_ref[...], d_up)
        gainh_ref[...] += back * hat_h
        d_second = grad_low.astype(F32) + norm_rows_back(back * gh_ref[...], hat_h, inv_h)
        ds_ref[r] = d_second
        gated = d_second * mask * out_gate
        d_tri = gated.astype(BF)
        dlogit_ref[r] = (gated * tri_proj * (1.0 - out_gate)).astype(BF)
        gz_ref[...] += mm(tri_norm, d_tri, NT)
        back = mm(wz_ref[...], d_tri)
        gaint_ref[...] += back * hat_t
        comb = norm_rows_back(back * gt_ref[...], hat_t, inv_t)
        hidden = comb.shape[0] // 2
        tiles = fold_pair(comb[:hidden], comb[hidden:])
        for t in range(3):
            if stage:
                put_tile(stage[1], t, row, rows, tiles[t])
            else:
                send_ref[r, t] = tiles[t].astype(BF)
    if stage:

        @pl.when(pl.program_id(0) == pl.num_programs(0) - 1)
        def _():
            ship(stage[1], send_ref, 3, share, rows)
            at = 3 * share * rows
            for acc in (gd_ref, gu_ref, gz_ref):
                part = acc.shape[0] // send_ref.shape[0]
                block = acc[...].reshape(send_ref.shape[0], part, LANES)
                send_ref[:, at : at + part] = block.astype(BF)
                at = at + part


def third_kernel(
    share, rows, sum_ref, acts_ref, ds_ref, dlogit_ref, mask_ref, mix_ref, right_ref, gx_ref, wt_ref, w_ref,
    fg_ref, dmix_ref, dright_ref, gin_ref, gainx_ref, dproj_ref, *stage,
):
    @pl.when(pl.program_id(0) == 0)
    def _():
        for acc in (dright_ref, gin_ref, gainx_ref):
            acc[...] = jnp.zeros_like(acc)
        if stage:
            unship(acts_ref, stage[0], 6, share, rows)

    hidden = wt_ref.shape[0] // 9
    for r in range(sum_ref.shape[0]):
        row = pl.program_id(0) * sum_ref.shape[0] + r
        hat, inv = norm_rows(sum_ref[r])
        norm = (hat * gx_ref[...]).astype(BF)
        mask = mask_ref[r]
        for pair in range(2):
            tiles = range(3 * pair, 3 * pair + 3)
            if stage:
                tiles = [get_tile(stage[0], t, row, rows, hidden) for t in tiles]
            else:
                tiles = [acts_ref[r, t].astype(F32) for t in tiles]
            both = unfold_pair(*tiles)
            for side in range(2):
                block = 2 * pair + side
                value = mm(wt_ref[block * hidden : (block + 1) * hidden], norm)
                gate = mm(wt_ref[(block + 4) * hidden : (block + 5) * hidden], norm)
                sig = jax.nn.sigmoid(gate)
                d_value = both[side] * mask * sig
                d_gate = d_value * value * (1.0 - sig)
                dproj_ref[block * hidden : (block + 1) * hidden] = d_value.astype(BF)
                dproj_ref[(block + 4) * hidden : (block + 5) * hidden] = d_gate.astype(BF)
        dproj_ref[8 * hidden :] = dlogit_ref[r]
        d_proj = dproj_ref[...]
        gin_ref[...] += mm(d_proj, norm, NT)
        back = mm(w_ref[...], d_proj)
        gainx_ref[...] += back * hat
        first = ds_ref[r] + norm_rows_back(back * gx_ref[...], hat, inv)
        fg_ref[r] = first
        low = first.astype(BF)
        dmix_ref[r] = mm(right_ref[...], low, NT).astype(BF)
        dright_ref[...] += mm(mix_ref[r], low)


def last_kernel(xt_ref, fg_ref, ds_ref, gain_ref, w_ref, out_ref, gw_ref, gainb_ref):
    @pl.when(pl.program_id(0) == 0)
    def _():
        for acc in (gw_ref, gainb_ref):
            acc[...] = jnp.zeros_like(acc)

    for r in range(xt_ref.shape[0]):
        hat, inv = norm_rows(xt_ref[r].astype(F32))
        norm = (hat * gain_ref[...]).astype(BF)
        d_bias = ds_ref[r]
        gw_ref[...] += mm(d_bias, norm, NT)
        back = mm(w_ref[...], d_bias)
        gainb_ref[...] += back * hat
        out_ref[r] = (fg_ref[r] + norm_rows_back(back * gain_ref[...], hat, inv)).T


def whole(shape):
    return pl.BlockSpec(shape, lambda i: (0,) * len(shape))


def by_row(step, shape):
    return pl.BlockSpec((step,) + shape, lambda i: (i,) + (0,) * len(shape))


def pair_call(kernel, steps, ins, outs, args, scratch=(), flops=0, moved=0):
    return pl.pallas_call(
        kernel,
        grid=(steps,),
        in_specs=ins,
        out_specs=[spec for spec, _ in outs],
        out_shape=[shape for _, shape in outs],
        scratch_shapes=list(scratch),
        compiler_params=pltpu.CompilerParams(vmem_limit_bytes=48 * 1024 * 1024),
        cost_estimate=pl.CostEstimate(flops=flops, bytes_accessed=moved, transcendentals=0),
    )(*args)


def shards(row_devices, *arrays):
    (pair_feats, node_feats, chain_ids, out_grad, node_out_grad) = arrays[:5]
    masters, firsts, seconds = arrays[5:17], arrays[17:29], arrays[29:41]
    w_attend, w_pairbias, w_attout, w_nodeup, w_nodedown = masters[:5]
    w_node, w_outer, w_in, w_z, w_up, w_down, ln_gains = masters[5:]
    count, _, residues, width_z = pair_feats.shape
    width_s = node_feats.shape[2]
    heads = w_pairbias.shape[1]
    depth = width_s // heads
    scale = 1.0 / depth**0.5
    outer_dim = w_node.shape[1] // 2
    hidden = (w_in.shape[1] - width_z) // 8
    expand = w_up.shape[1]
    every = 2 * row_devices
    shape_of = jax.ShapeDtypeStruct
    cuts = [width_s, width_z, width_s, width_s, width_z, 2 * hidden, width_z]
    gains, at = [], 0
    for cut in cuts:
        gains.append(ln_gains[at : at + cut])
        at = at + cut
    gain_a, gain_b, gain_n, gain_s, gain_x, gain_t, gain_h = gains
    column = lambda gain: gain.reshape(-1, 1)
    crop_index, row_index = lax.axis_index("crop"), lax.axis_index("row")
    first_row = row_index * count
    chains = chain_ids[0]
    own_chain = lax.dynamic_slice_in_dim(chains, first_row, count, 0)
    same_own = own_chain[:, None] == chains[None, :]
    mask = same_own.astype(F32)[:, None, :]
    chain_col, chain_row = chains.reshape(-1, 1), chains.reshape(1, -1)

    att_wb, attout_wb = w_attend.astype(BF), w_attout.astype(BF)
    nodeup_wb, nodedown_wb, node_wb = w_nodeup.astype(BF), w_nodedown.astype(BF), w_node.astype(BF)
    outer_wb = w_outer.astype(BF).reshape(outer_dim, outer_dim * width_z)
    bias_wb, in_wb, z_wb = w_pairbias.astype(BF), w_in.astype(BF), w_z.astype(BF)
    up_wb, down_wb = w_up.astype(BF), w_down.astype(BF)
    bias_wt, in_wt, z_wt, up_wt, down_wt = bias_wb.T, in_wb.T, z_wb.T, up_wb.T, down_wb.T

    step = 2 if count % 2 == 0 else 1
    steps = count // step
    pairs = count * residues

    node_both = jnp.concatenate([node_feats[:, 0], node_out_grad[:, 0]], axis=1)
    node_both = gather_all(node_both, row_devices).reshape(2 * residues, 2 * width_s)
    node_all, cot_all = node_both[:, :width_s], node_both[:, width_s:]
    node_f32 = node_all.astype(F32)

    pair_x = pair_feats[:, 0]
    xt, pair_bias = pair_call(
        bias_kernel, steps,
        [by_row(step, (residues, width_z)), whole((width_z, 1)), whole((heads, width_z))],
        [(by_row(step, (width_z, residues)), shape_of((count, width_z, residues), BF)),
         (by_row(step, (heads, residues)), shape_of((count, heads, residues), F32))],
        [pair_x, column(gain_b), bias_wt],
        flops=2 * pairs * width_z * heads, moved=4 * pairs * width_z,
    )

    def own_rows(values):
        return lax.dynamic_slice_in_dim(values, crop_index * residues + first_row, count, 0)

    def own_crop(values):
        return lax.dynamic_slice_in_dim(values, crop_index * residues, residues, 0)

    att_hat, att_back = jax.vjp(layer_norm, node_f32, gain_a)
    att_norm = att_hat.astype(BF)
    qkvg = mm(att_norm, att_wb)
    gate_all = jax.nn.sigmoid(qkvg[:, 3 * width_s :])
    qkv_crop = own_crop(qkvg[:, : 3 * width_s]).astype(BF)
    query_crop, keys, values = (
        qkv_crop[:, k * width_s : (k + 1) * width_s].reshape(residues, heads, depth)
        for k in range(3)
    )
    own_row_of = lambda v: lax.dynamic_slice_in_dim(v, first_row, count, 0)
    query = own_row_of(query_crop)
    raw_scores = jnp.einsum("ihd,jhd->ihj", query, keys, preferred_element_type=F32) * scale
    scores = jnp.where(same_own[:, None, :], raw_scores + pair_bias, -1000000000.0)
    att_weights = jax.nn.softmax(scores, axis=-1)
    weights_low = att_weights.astype(BF)
    attn = jnp.einsum("ihj,jhd->ihd", weights_low, values, preferred_element_type=F32)
    gated_own = (own_rows(gate_all) * attn.reshape(count, width_s)).astype(BF)
    gated = gather_all(gated_own, row_devices).reshape(2 * residues, width_s)

    node_mid = node_f32 + mm(gated, attout_wb)
    ntrans_hat, ntrans_back = jax.vjp(layer_norm, node_mid, gain_n)
    trans_node = ntrans_hat.astype(BF)
    node_upv = mm(trans_node, nodeup_wb)
    nact_val, nact_back = jax.vjp(gelu_tanh, node_upv)
    node_act = nact_val.astype(BF)
    node_next = node_mid + mm(node_act, nodedown_wb)
    node_out = own_rows(node_next).astype(BF)[:, None]
    node_hat, node_back = jax.vjp(layer_norm, node_next, gain_s)
    node_norm = node_hat.astype(BF)
    node_proj = mm(node_norm, node_wb).astype(BF)
    left_vec = own_rows(node_proj[:, :outer_dim])
    right_t = own_crop(node_proj[:, outer_dim:]).T
    outer_mix = mm(left_vec, outer_wb).astype(BF).reshape(count, outer_dim, width_z)

    share = hidden // row_devices
    direct = count % 16 == 0
    dims = (share, count) if direct else None
    weights_cut = weights_low.reshape(count, heads, row_devices, count).transpose(2, 0, 1, 3)

    def sent_block(tiles, extra=0):
        if direct:
            shape = (row_devices, tiles * share * count + extra, LANES)
            return whole(shape), shape_of(shape, BF)
        return by_row(step, (tiles, hidden, LANES)), shape_of((count, tiles, hidden, LANES), BF)

    def stage(tiles):
        return [pltpu.VMEM((tiles * hidden * count, LANES), F32)] if direct else []

    def swap(block):
        return lax.all_to_all(block, "row", split_axis=0, concat_axis=0, tiled=True)

    def to_channels(block):
        if direct:
            return swap(block)
        tiles = block.shape[1]
        cut = block.reshape(count, tiles, row_devices, share, LANES)
        sent = swap(cut.transpose(2, 1, 3, 0, 4))
        return sent.transpose(1, 2, 0, 3, 4).reshape(1, tiles, share, residues, LANES)

    def to_rows(block):
        if direct:
            return swap(block)
        tiles = block.shape[1]
        cut = block.reshape(tiles, share, row_devices, count, LANES)
        got = swap(cut.transpose(2, 0, 1, 3, 4))
        return got.transpose(3, 1, 0, 2, 4).reshape(count, tiles, hidden, LANES)

    def tri_block(tiles, extra=0):
        if direct:
            return sent_block(tiles, extra)
        shape = (1, tiles, share, residues, LANES)
        spec = pl.BlockSpec((1, tiles, 1, residues, LANES), lambda i: (0, 0, i, 0, 0))
        return spec, shape_of(shape, BF)

    ride = weights_cut.reshape(row_devices, -1, LANES) if direct else jnp.zeros((1, 1, LANES), BF)
    extra = ride.shape[1]
    first_sum, acts_own = pair_call(
        functools.partial(first_kernel, share, count), steps,
        [by_row(step, (width_z, residues)), by_row(step, (outer_dim, width_z)),
         whole((outer_dim, residues)), by_row(step, (1, residues)), whole((width_z, 1)),
         whole(in_wt.shape), whole(ride.shape)],
        [(by_row(step, (width_z, residues)), shape_of((count, width_z, residues), F32)),
         sent_block(6, extra)],
        [xt, outer_mix, right_t, mask, column(gain_x), in_wt, ride],
        scratch=stage(6),
        flops=16 * pairs * width_z * hidden, moved=12 * pairs * width_z,
    )

    chain_specs = [whole((residues, 1)), whole((1, residues))]
    product = 2 * share * residues**3
    acts = to_channels(acts_own)
    if direct:
        weights_col = acts[:, 6 * share * count :].reshape(residues, heads, count)
    else:
        weights_col = swap(weights_cut).reshape(residues, heads, count)
    (tri,) = pair_call(
        functools.partial(tri_kernel, dims), share, chain_specs + [tri_block(6, extra)[0]],
        [tri_block(3)], [chain_col, chain_row, acts],
        flops=2 * product, moved=share * residues * 9 * 256,
    )
    tri_rows = to_rows(tri)

    slab = by_row(step, (width_z, residues))
    second_args = [
        (by_row(step, (width_z, residues)), first_sum),
        (sent_block(3)[0], tri_rows),
        (by_row(step, (residues, width_z)), out_grad[:, 0]),
        (by_row(step, (1, residues)), mask),
    ]
    second_args += [
        (whole(v.shape), v)
        for v in (
            column(gain_x), column(gain_t), column(gain_h),
            in_wt[8 * hidden :], z_wt, z_wb, up_wt, up_wb, down_wt, down_wb,
        )
    ]
    grad_rows = 2 * expand + 2 * hidden
    carried = grad_rows // row_devices if direct else 0
    acc_shapes = [
        (expand, width_z), (expand, width_z), (2 * hidden, width_z),
        (2 * hidden, residues), (width_z, residues),
    ]
    pair_out, d_second, d_logit, dtri_own, g_down, g_up_t, g_z, gain_t_acc, gain_h_acc = pair_call(
        functools.partial(second_kernel, share, count), steps,
        [spec for spec, _ in second_args],
        [(by_row(step, (residues, width_z)), shape_of((count, residues, width_z), BF)),
         (slab, shape_of((count, width_z, residues), F32)),
         (slab, shape_of((count, width_z, residues), BF)),
         sent_block(3, carried)]
        + [(whole(s), shape_of(s, F32)) for s in acc_shapes],
        [arg for _, arg in second_args],
        scratch=stage(3) + stage(3),
        flops=12 * pairs * width_z * expand, moved=20 * pairs * width_z,
    )

    dtri = to_channels(dtri_own)
    if direct:
        grad_parts = dtri[:, 3 * share * count :]
    else:
        cut = lambda g: g.reshape(row_devices, -1, LANES)
        grad_parts = swap(jnp.concatenate([cut(g) for g in (g_down, g_up_t, g_z)], 1).astype(BF))
    row_sum = jnp.sum(grad_parts.astype(F32), axis=0)
    half_rows = row_sum.shape[0] // 2
    lower, upper = row_sum[:half_rows], row_sum[half_rows:]
    low_crop = crop_index == 0
    theirs = lax.ppermute(jnp.where(low_crop, upper, lower), "crop", [(0, 1), (1, 0)])
    pair_own = (jnp.where(low_crop, lower, upper) + theirs).astype(BF)
    (dacts,) = pair_call(
        functools.partial(tri_back_kernel, dims), share,
        chain_specs + [tri_block(6, extra)[0], tri_block(3, carried)[0]],
        [tri_block(6)], [chain_col, chain_row, acts, dtri],
        flops=4 * product, moved=share * residues * 15 * 256,
    )
    dacts_rows = to_rows(dacts)

    first_grad, d_mix, d_right, g_in_t, gain_x_acc = pair_call(
        functools.partial(third_kernel, share, count), steps,
        [slab, sent_block(6)[0], slab, slab, by_row(step, (1, residues)),
         by_row(step, (outer_dim, width_z)), whole((outer_dim, residues)), whole((width_z, 1)),
         whole(in_wt.shape), whole(in_wb.shape)],
        [(slab, shape_of((count, width_z, residues), F32)),
         (by_row(step, (outer_dim, width_z)), shape_of((count, outer_dim, width_z), BF)),
         (whole((outer_dim, residues)), shape_of((outer_dim, residues), F32)),
         (whole(in_wt.shape), shape_of(in_wt.shape, F32)),
         (whole((width_z, residues)), shape_of((width_z, residues), F32))],
        [first_sum, dacts_rows, d_second, d_logit, mask, outer_mix, right_t, column(gain_x),
         in_wt, in_wb],
        scratch=[pltpu.VMEM((9 * hidden, residues), BF)] + stage(6),
        flops=54 * pairs * width_z * hidden, moved=20 * pairs * width_z,
    )

    mix_flat = d_mix.reshape(count, outer_dim * width_z)
    d_left = back_dot(mix_flat, outer_wb)
    packed = jnp.concatenate([d_right.reshape(-1), d_left.reshape(-1)]).astype(BF)
    size = packed.shape[0]
    unit = 16 * LANES
    packed = jnp.pad(packed, (0, -size % unit)).reshape(-1, LANES)
    got = gather_all(packed, row_devices)
    g_outer = cross_sum(left_vec, mix_flat)
    gain_accs = [gain_x_acc, gain_t_acc, gain_h_acc]
    late_flat = join_flat([g_in_t, g_outer] + [lanes_sum(acc) for acc in gain_accs])
    late_own = scatter_sum(after(late_flat, got), row_devices)
    got = got.reshape(2, row_devices, -1)[:, :, :size].astype(F32)
    right_sum = jnp.sum(got[:, :, : outer_dim * residues], axis=1)
    right_sum = right_sum.reshape(2, outer_dim, residues).transpose(0, 2, 1)
    left_all = got[:, :, outer_dim * residues :].reshape(2, residues, outer_dim)
    proj_grad = jnp.concatenate([left_all, right_sum], axis=-1).astype(BF)
    proj_grad = proj_grad.reshape(2 * residues, 2 * outer_dim)

    g_node = cross_sum(node_norm, proj_grad)
    outer_node_grad, gain_s_grad = node_back(back_dot(proj_grad, node_wb))
    grad_next = cot_all.astype(F32) + outer_node_grad
    next_low = grad_next.astype(BF)
    g_nodedown = cross_sum(node_act, next_low)
    (nact_grad,) = nact_back(back_dot(next_low, nodedown_wb))
    nodeup_low = nact_grad.astype(BF)
    g_nodeup = cross_sum(trans_node, nodeup_low)
    ntrans_grad, gain_n_grad = ntrans_back(back_dot(nodeup_low, nodeup_wb))
    grad_mid = grad_next + ntrans_grad
    mid_low = grad_mid.astype(BF)
    g_attout = cross_sum(gated, mid_low)
    gated_grad = back_dot(mid_low, attout_wb)
    attn_grad = (gated_grad * gate_all).astype(BF)
    gate_grad = (gated_grad * gated.astype(F32) * (1.0 - gate_all)).astype(BF)

    attn_grad_crop = own_crop(attn_grad).reshape(residues, heads, depth)
    attn_grad_own = own_row_of(attn_grad_crop)
    weight_grad = jnp.einsum("ihd,jhd->ihj", attn_grad_own, values, preferred_element_type=F32)
    inner = jnp.sum(weight_grad * att_weights, axis=-1, keepdims=True)
    score_grad = (att_weights * (weight_grad - inner)).astype(BF)
    query_grad = jnp.einsum("ihj,jhd->ihd", score_grad, keys, preferred_element_type=F32) * scale

    values_own = own_row_of(values)
    inner_crop = jnp.sum(
        (own_crop(gated_grad) * own_crop(gated).astype(F32)).reshape(residues, heads, depth),
        axis=-1, keepdims=True,
    )
    weight_grad_col = jnp.einsum(
        "ihd,jhd->ihj", attn_grad_crop, values_own, preferred_element_type=F32
    )
    score_grad_col = (weights_col.astype(F32) * (weight_grad_col - inner_crop)).astype(BF)
    key_grad = (
        jnp.einsum("ihj,ihd->jhd", score_grad_col, query_crop, preferred_element_type=F32) * scale
    )
    value_grad = jnp.einsum("ihj,ihd->jhd", weights_col, attn_grad_crop, preferred_element_type=F32)
    qkv_grad = jnp.concatenate(
        [v.reshape(count, width_s) for v in (query_grad, key_grad, value_grad)], axis=-1
    ).astype(BF)

    pair_grad, g_bias_t, gain_b_acc = pair_call(
        last_kernel, steps,
        [slab, slab, by_row(step, (heads, residues)), whole((width_z, 1)), whole((width_z, heads))],
        [(by_row(step, (residues, width_z)), shape_of((count, residues, width_z), F32)),
         (whole((heads, width_z)), shape_of((heads, width_z), F32)),
         (whole((width_z, residues)), shape_of((width_z, residues), F32))],
        [xt, first_grad, score_grad, column(gain_b), bias_wb],
        flops=4 * pairs * width_z * heads, moved=10 * pairs * width_z,
    )

    bias_flat = join_flat([g_bias_t, lanes_sum(gain_b_acc)]).astype(BF)
    pieces = [qkv_grad.reshape(-1, LANES), late_own, pair_own, bias_flat.reshape(-1, LANES)]
    highs = [piece.shape[0] for piece in pieces]
    tail = jnp.zeros((-sum(highs) % 16, LANES), BF)
    last = gather_all(jnp.concatenate(pieces + [tail]), row_devices)
    ends = [sum(highs[: k + 1]) for k in range(len(highs))]
    qkv_grad_all = last[:, : ends[0]].reshape(2 * residues, 3 * width_s)
    late_sums = last[:, ends[0] : ends[1]].reshape(-1).astype(F32)
    pair_sums = last[:, ends[1] : ends[2]].astype(F32).reshape(2, row_devices, -1, LANES)
    bias_parts = last[:, ends[2] : ends[3]].astype(F32)
    qkvg_grad = jnp.concatenate([qkv_grad_all, gate_grad], axis=-1)
    g_attend = cross_sum(att_norm, qkvg_grad)
    att_in_grad, gain_a_grad = att_back(back_dot(qkvg_grad, att_wb))
    node_grad = own_rows(grad_mid + att_in_grad)[:, None]

    g_in_t, g_outer, gain_x_grad, gain_t_grad, gain_h_grad = split_flat(
        late_sums, [g_in_t, w_outer, gain_x, gain_t, gain_h]
    )
    g_bias_t, gain_b_grad = split_flat(jnp.sum(bias_parts, axis=0).reshape(-1), [g_bias_t, gain_b])
    pair_sums = pair_sums.transpose(1, 0, 2, 3).reshape(row_devices, 2 * half_rows, LANES)
    found, start = [], 0
    for total in (g_down, g_up_t, g_z):
        part = total.shape[0] // row_devices
        found.append(pair_sums[:, start : start + part].reshape(total.shape))
        start = start + part
    g_down, g_up_t, g_z = found
    gain_grad = jnp.concatenate(
        [gain_a_grad, gain_b_grad, gain_n_grad, gain_s_grad, gain_x_grad, gain_t_grad, gain_h_grad]
    )
    grads = [
        g_attend, g_bias_t.T, g_attout, g_nodeup, g_nodedown, g_node, g_outer, g_in_t.T, g_z,
        g_up_t.T, g_down, gain_grad,
    ]
    results = [pair_out[:, None], node_out, pair_grad[:, None], node_grad]
    rates = [0.1] * 11 + [1.0]
    decays = [0.1] * 11 + [0.0]
    for master, first_old, second_old, grad, rate, decay in zip(
        masters, firsts, seconds, grads, rates, decays
    ):
        results.extend(adam_step(master, first_old, second_old, grad, rate, decay))
    return tuple(results)


def solution(mesh):
    rows4, rows3 = P("row", "crop", None, None), P("row", "crop", None)
    return jax.shard_map(
        functools.partial(shards, mesh.shape["row"]),
        mesh=mesh,
        in_specs=(rows4, rows3, P("crop", None), rows4, rows3) + (P(),) * 36,
        out_specs=(rows4, rows3, rows4, rows3) + (P(),) * 36,
        check_vma=False,
    )
```

```python
import functools
import jax
import jax.numpy as jnp
from jax import lax
from jax.experimental import pallas as pl
from jax.experimental.pallas import tpu as pltpu
from jax.sharding import PartitionSpec as P

ADAM_STEP = 4
EPS = 1e-05
BF = jnp.bfloat16
F32 = jnp.float32
LANES = 128
HALF = 64
BOTH = ("crop", "row")
NN = (((1,), (0,)), ((), ()))
NT = (((1,), (1,)), ((), ()))
TN = (((0,), (0,)), ((), ()))


def mm(left, right, dims=NN):
    return lax.dot_general(left, right, dims, preferred_element_type=F32)


def adam_step(master, first_old, second_old, grad_total, rate, decay):
    first_new = 0.9 * first_old + 0.1 * grad_total
    second_new = 0.999 * second_old + 0.001 * grad_total * grad_total
    first_hat = first_new / (1.0 - 0.9**ADAM_STEP)
    second_hat = second_new / (1.0 - 0.999**ADAM_STEP)
    master_new = master - rate * (first_hat / (jnp.sqrt(second_hat) + 1e-08) + decay * master)
    return (first_new, second_new, master_new)


def after(value, event):
    return lax.optimization_barrier((value, event))[0]


def gather_all(part, row_devices, during=()):
    every = 2 * row_devices
    groups = [[d for d in range(every) if d % 2 == k] for k in range(2)]
    spread = jnp.broadcast_to(part[None], (every // 2,) + part.shape)
    got = lax.all_to_all(
        spread, BOTH, split_axis=0, concat_axis=0, tiled=True, axis_index_groups=groups
    )
    got = after(got, during)
    other = lax.ppermute(got, "row", [(d, d ^ 1) for d in range(row_devices)])
    odd = lax.axis_index("row") % 2 == 1
    pair = [jnp.where(odd, other, got), jnp.where(odd, got, other)]
    return jnp.stack(pair, axis=1).reshape((every,) + part.shape)


def scatter_sum(sent):
    parts = lax.all_to_all(sent, BOTH, split_axis=0, concat_axis=0, tiled=True)
    return jnp.sum(parts.astype(F32), axis=0).astype(BF)


def norm_rows(values):
    centred = values - jnp.mean(values, axis=0, keepdims=True)
    inv = lax.rsqrt(jnp.mean(centred * centred, axis=0, keepdims=True) + EPS)
    return centred * inv, inv


def norm_rows_back(scaled, hat, inv):
    return inv * (
        scaled
        - jnp.mean(scaled, axis=0, keepdims=True)
        - hat * jnp.mean(scaled * hat, axis=0, keepdims=True)
    )


def turn(values):
    return pltpu.roll(values, HALF, values.ndim - 1)


def low_lanes(shape):
    return lax.broadcasted_iota(jnp.int32, shape, len(shape) - 1) < HALF


def fold_pair(first, second):
    low = low_lanes((first.shape[0], LANES))
    f_lo, f_hi = first[:, :LANES], first[:, LANES:]
    s_lo, s_hi = second[:, :LANES], second[:, LANES:]
    f_turn, s_turn = turn(f_hi), turn(s_hi)
    main_f = f_lo + jnp.where(low, f_turn, 0.0)
    main_s = s_lo + jnp.where(low, s_turn, 0.0)
    return main_f, main_s, jnp.where(low, f_hi, s_turn)


def unfold_pair(main_f, main_s, tail):
    low = low_lanes(tail.shape)
    first = jnp.concatenate([main_f, jnp.where(low, tail, turn(main_f))], axis=1)
    second = jnp.concatenate([main_s, jnp.where(low, turn(tail), turn(main_s))], axis=1)
    return first, second


def put_tile(stage_ref, tile, row, rows, values):
    high = values.shape[0]
    stage_ref[pl.ds(tile * high * rows + row, high, stride=rows), :] = values


def get_tile(stage_ref, tile, row, rows, high):
    return stage_ref[pl.ds(tile * high * rows + row, high, stride=rows), :]


def ship(stage_ref, send_ref, tiles, share, rows):
    devices = send_ref.shape[0]
    span = share * rows
    for t in range(tiles):
        block = stage_ref[t * devices * span : (t + 1) * devices * span]
        send_ref[:, t * span : (t + 1) * span] = block.reshape(devices, span, LANES).astype(BF)


def unship(got_ref, stage_ref, tiles, share, rows):
    devices = got_ref.shape[0]
    span = share * rows
    for t in range(tiles):
        block = got_ref[:, t * span : (t + 1) * span].astype(F32)
        stage_ref[t * devices * span : (t + 1) * devices * span] = block.reshape(-1, LANES)


def lane_sums(ref):
    count = ref.shape[0] // LANES
    cut = [ref[k * LANES : (k + 1) * LANES].T for k in range(count)]
    return jnp.concatenate([jnp.sum(part, axis=0, keepdims=True) for part in cut], axis=0)


def turn_blocks(ref):
    count = ref.shape[0] // LANES
    return jnp.concatenate([ref[k * LANES : (k + 1) * LANES].T for k in range(count)], axis=0)


def bias_kernel(x_ref, gain_ref, weight_ref, xt_ref, norm_ref, bias_ref):
    for r in range(x_ref.shape[0]):
        xt = x_ref[r].astype(F32).T
        xt_ref[r] = xt.astype(BF)
        hat, _ = norm_rows(xt)
        norm = (hat * gain_ref[...]).astype(BF)
        norm_ref[r] = norm
        bias_ref[r] = mm(weight_ref[...], norm)


def first_kernel(
    share, rows, xt_ref, mix_ref, right_ref, mask_ref, gain_ref, weight_ref, ride_ref,
    sum_ref, send_ref, *stage,
):
    hidden = weight_ref.shape[0] // 9
    for r in range(xt_ref.shape[0]):
        row = pl.program_id(0) * xt_ref.shape[0] + r
        total = xt_ref[r].astype(F32) + mm(mix_ref[r], right_ref[...], TN)
        sum_ref[r] = total
        hat, _ = norm_rows(total)
        norm = (hat * gain_ref[...]).astype(BF)
        mask = mask_ref[r]
        acts = []
        for block in range(4):
            value = mm(weight_ref[block * hidden : (block + 1) * hidden], norm)
            gate = mm(weight_ref[(block + 4) * hidden : (block + 5) * hidden], norm)
            acts.append(jax.nn.sigmoid(gate) * value * mask)
        for pair in range(2):
            tiles = fold_pair(acts[2 * pair], acts[2 * pair + 1])
            for t in range(3):
                if stage:
                    put_tile(stage[0], 3 * pair + t, row, rows, tiles[t])
                else:
                    send_ref[r, 3 * pair + t] = tiles[t].astype(BF)
    if stage:

        @pl.when(pl.program_id(0) == pl.num_programs(0) - 1)
        def _():
            ship(stage[0], send_ref, 6, share, rows)
            send_ref[:, 6 * share * rows :] = ride_ref[...]


def chain_mask(col_ref, row_ref):
    return col_ref[...] == row_ref[...]


def channel_rows(dims, tile):
    share, rows = dims
    return pl.ds(pl.multiple_of((tile * share + pl.program_id(0)) * rows, rows), rows)


def flat_rows(ref, tile, dims):
    block = ref[:, channel_rows(dims, tile)] if dims else ref[:, tile, 0]
    return block.reshape(-1, block.shape[-1])


def slot_operands(ref, pair, dims):
    main_f, main_s, tail = (flat_rows(ref, 3 * pair + t, dims).astype(F32) for t in range(3))
    low = low_lanes(tail.shape)
    zero = jnp.zeros_like(tail)
    first = jnp.concatenate([main_f, jnp.where(low, tail, zero)], axis=1).astype(BF)
    second = jnp.concatenate([main_s, jnp.where(low, turn(tail), zero)], axis=1).astype(BF)
    return first, second


def raw_columns(slots, same):
    values = slots.astype(F32)
    main, tail = values[:, :LANES], values[:, LANES:]
    wide = jnp.concatenate(
        [main, jnp.where(low_lanes(tail.shape), tail, turn(main))], axis=1
    )
    return jnp.where(same, wide, 0.0).astype(BF)


def store_tiles(out_ref, pair, dims, tiles):
    for t in range(3):
        block = tiles[t].astype(BF).reshape(out_ref.shape[0], -1, LANES)
        if dims:
            out_ref[:, channel_rows(dims, 3 * pair + t)] = block
        else:
            out_ref[:, 3 * pair + t, 0] = block


def tri_kernel(dims, col_ref, row_ref, acts_ref, out_ref):
    same = chain_mask(col_ref, row_ref)
    left_out, right_out = slot_operands(acts_ref, 0, dims)
    left_in, right_in = slot_operands(acts_ref, 1, dims)
    outgoing = jnp.where(same, mm(left_out, right_out, NT), 0.0)
    incoming = mm(raw_columns(left_in, same), right_in, TN)
    low = low_lanes((outgoing.shape[0], LANES))
    o_lo, o_hi = outgoing[:, :LANES], outgoing[:, LANES:]
    main_o = o_lo + jnp.where(low, turn(o_hi), 0.0)
    tail = jnp.where(low, o_hi, turn(incoming[:, LANES:]))
    store_tiles(out_ref, 0, dims, (main_o, incoming[:, :LANES], tail))


def tri_back_kernel(dims, col_ref, row_ref, acts_ref, grad_ref, out_ref):
    same = chain_mask(col_ref, row_ref)
    left_out, right_out = slot_operands(acts_ref, 0, dims)
    left_in, right_in = slot_operands(acts_ref, 1, dims)
    grad_out, grad_in = slot_operands(grad_ref, 0, dims)
    raw_out = raw_columns(grad_out, same)
    d_left = mm(raw_out, right_out)
    d_right = mm(raw_out, left_out, TN)
    low = low_lanes((d_left.shape[0], LANES))
    tail = jnp.where(low, d_left[:, LANES:], turn(d_right[:, LANES:]))
    store_tiles(out_ref, 0, dims, (d_left[:, :LANES], d_right[:, :LANES], tail))
    d_left = jnp.where(same, mm(right_in, grad_in, NT), 0.0)
    d_right = mm(raw_columns(left_in, same), grad_in)
    l_lo, l_hi = d_left[:, :LANES], d_left[:, LANES:]
    main_l = l_lo + jnp.where(low, turn(l_hi), 0.0)
    tail = jnp.where(low, l_hi, turn(d_right[:, LANES:]))
    store_tiles(out_ref, 1, dims, (main_l, d_right[:, :LANES], tail))


def second_kernel(
    share, rows, sum_ref, tri_ref, grad_ref, mask_ref, gx_ref, gt_ref, gh_ref,
    wgate_ref, wzt_ref, wz_ref, wut_ref, wu_ref, wdt_ref, wd_ref,
    out_ref, ds_ref, dlogit_ref, send_ref, gd_ref, gu_ref, gz_ref, gains_ref, gaint_ref, gainh_ref,
    *stage,
):
    @pl.when(pl.program_id(0) == 0)
    def _():
        for acc in (gd_ref, gu_ref, gz_ref, gaint_ref, gainh_ref):
            acc[...] = jnp.zeros_like(acc)
        if stage:
            unship(tri_ref, stage[0], 3, share, rows)

    for r in range(sum_ref.shape[0]):
        row = pl.program_id(0) * sum_ref.shape[0] + r
        total = sum_ref[r]
        mask = mask_ref[r]
        hat_x, _ = norm_rows(total)
        norm = (hat_x * gx_ref[...]).astype(BF)
        out_gate = jax.nn.sigmoid(mm(wgate_ref[...], norm))
        if stage:
            tiles = [get_tile(stage[0], t, row, rows, total.shape[0]) for t in range(3)]
        else:
            tiles = [tri_ref[r, t].astype(F32) for t in range(3)]
        tri_out, tri_in = unfold_pair(*tiles)
        hat_t, inv_t = norm_rows(jnp.concatenate([tri_out, tri_in], axis=0))
        tri_norm = (hat_t * gt_ref[...]).astype(BF)
        tri_proj = mm(wzt_ref[...], tri_norm)
        second = total + out_gate * tri_proj * mask
        hat_h, inv_h = norm_rows(second)
        trans_in = (hat_h * gh_ref[...]).astype(BF)
        act, slope = gelu_parts(mm(wut_ref[...], trans_in))
        act = act.astype(BF)
        out_ref[r] = (second + mm(wdt_ref[...], act)).T.astype(BF)
        grad_low = grad_ref[r].astype(F32).T.astype(BF)
        gd_ref[...] += mm(act, grad_low, NT)
        d_up = (mm(wd_ref[...], grad_low) * slope).astype(BF)
        gu_ref[...] += mm(d_up, trans_in, NT)
        back = mm(wu_ref[...], d_up)
        gainh_ref[...] += back * hat_h
        d_second = grad_low.astype(F32) + norm_rows_back(back * gh_ref[...], hat_h, inv_h)
        ds_ref[r] = d_second
        gated = d_second * mask * out_gate
        d_tri = gated.astype(BF)
        dlogit_ref[r] = (gated * tri_proj * (1.0 - out_gate)).astype(BF)
        gz_ref[...] += mm(tri_norm, d_tri, NT)
        back = mm(wz_ref[...], d_tri)
        gaint_ref[...] += back * hat_t
        comb = norm_rows_back(back * gt_ref[...], hat_t, inv_t)
        hidden = comb.shape[0] // 2
        tiles = fold_pair(comb[:hidden], comb[hidden:])
        for t in range(3):
            if stage:
                put_tile(stage[1], t, row, rows, tiles[t])
            else:
                send_ref[r, t] = tiles[t].astype(BF)

    @pl.when(pl.program_id(0) == pl.num_programs(0) - 1)
    def _():
        gains_ref[...] = jnp.concatenate([lane_sums(gaint_ref), lane_sums(gainh_ref)], axis=0)
        if stage:
            ship(stage[1], send_ref, 3, share, rows)
            devices = send_ref.shape[0]
            at = 3 * share * rows
            for acc, turned in ((gd_ref, False), (gu_ref, True), (gz_ref, False)):
                part = acc.shape[0] // devices
                block = turn_blocks(acc) if turned else acc[...]
                send_ref[:, at : at + part] = block.reshape(devices, part, LANES).astype(BF)
                at = at + part
            spare = send_ref.shape[1] - at
            send_ref[:, at:] = jnp.zeros((devices, spare, LANES), BF)


def third_kernel(
    share, rows, sum_ref, acts_ref, ds_ref, dlogit_ref, mask_ref, mix_ref, right_ref, gx_ref, wt_ref, w_ref,
    fg_ref, dmix_ref, dright_ref, gin_ref, gains_ref, gainx_ref, dproj_ref, acc_ref, *stage,
):
    @pl.when(pl.program_id(0) == 0)
    def _():
        for acc in (dright_ref, acc_ref, gainx_ref):
            acc[...] = jnp.zeros_like(acc)
        if stage:
            unship(acts_ref, stage[0], 6, share, rows)

    hidden = wt_ref.shape[0] // 9
    for r in range(sum_ref.shape[0]):
        row = pl.program_id(0) * sum_ref.shape[0] + r
        hat, inv = norm_rows(sum_ref[r])
        norm = (hat * gx_ref[...]).astype(BF)
        mask = mask_ref[r]
        for pair in range(2):
            tiles = range(3 * pair, 3 * pair + 3)
            if stage:
                tiles = [get_tile(stage[0], t, row, rows, hidden) for t in tiles]
            else:
                tiles = [acts_ref[r, t].astype(F32) for t in tiles]
            both = unfold_pair(*tiles)
            for side in range(2):
                block = 2 * pair + side
                value = mm(wt_ref[block * hidden : (block + 1) * hidden], norm)
                gate = mm(wt_ref[(block + 4) * hidden : (block + 5) * hidden], norm)
                sig = jax.nn.sigmoid(gate)
                d_value = both[side] * mask * sig
                d_gate = d_value * value * (1.0 - sig)
                dproj_ref[block * hidden : (block + 1) * hidden] = d_value.astype(BF)
                dproj_ref[(block + 4) * hidden : (block + 5) * hidden] = d_gate.astype(BF)
        dproj_ref[8 * hidden :] = dlogit_ref[r]
        d_proj = dproj_ref[...]
        acc_ref[...] += mm(d_proj, norm, NT)
        back = mm(w_ref[...], d_proj)
        gainx_ref[...] += back * hat
        first = ds_ref[r] + norm_rows_back(back * gx_ref[...], hat, inv)
        fg_ref[r] = first
        low = first.astype(BF)
        dmix_ref[r] = mm(right_ref[...], low, NT).astype(BF)
        right = mm(mix_ref[r], low)
        for half in range(dright_ref.shape[0]):
            dright_ref[half] += right[:, half * LANES : (half + 1) * LANES]

    @pl.when(pl.program_id(0) == pl.num_programs(0) - 1)
    def _():
        gin_ref[...] = turn_blocks(acc_ref).astype(BF)
        gains_ref[...] = lane_sums(gainx_ref)


def last_kernel(xt_ref, fg_ref, ds_ref, gain_ref, w_ref, out_ref):
    for r in range(xt_ref.shape[0]):
        hat, inv = norm_rows(xt_ref[r].astype(F32))
        back = mm(w_ref[...], ds_ref[r])
        out_ref[r] = (fg_ref[r] + norm_rows_back(back * gain_ref[...], hat, inv)).T


def norm_lanes(values):
    centred = values - jnp.mean(values, axis=1, keepdims=True)
    inv = lax.rsqrt(jnp.mean(centred * centred, axis=1, keepdims=True) + EPS)
    return centred * inv, inv


def norm_lanes_back(scaled, hat, inv):
    return inv * (
        scaled
        - jnp.mean(scaled, axis=1, keepdims=True)
        - hat * jnp.mean(scaled * hat, axis=1, keepdims=True)
    )


def head_lanes(heads, width):
    depth = width // heads
    lane = lax.broadcasted_iota(jnp.int32, (heads, width), 1)
    head = lax.broadcasted_iota(jnp.int32, (heads, width), 0)
    return ((lane >= head * depth) & (lane < (head + 1) * depth)).astype(F32)


def rows_by_head(values, lanes):
    spread = values[:, None, :] * lanes[None]
    return spread.reshape(-1, values.shape[1])


def heads_by_row(values, lanes):
    spread = values[None] * lanes[:, None, :]
    return spread.reshape(-1, values.shape[1])


def crop_rows(residues):
    return pl.ds(pl.multiple_of(lax.axis_index("crop") * residues, residues), residues)


def attend_kernel(
    both_ref, own_ref, gain_ref, w_ref, bias_ref, mask_ref,
    norm_ref, gate_ref, qkv_ref, weights_ref, low_ref, gated_ref,
):
    width = own_ref.shape[1]
    residues = mask_ref.shape[2]
    heads = bias_ref.shape[1]
    rows = own_ref.shape[0]
    scale = 1.0 / (width // heads) ** 0.5
    hat, _ = norm_lanes(both_ref[:, :width].astype(F32))
    norm_ref[...] = (hat * gain_ref[...]).astype(BF)
    gate_ref[...] = jax.nn.sigmoid(mm(norm_ref[...], w_ref[:, 3 * width :]))
    qkv_ref[...] = mm(norm_ref[crop_rows(residues), :], w_ref[:, : 3 * width]).astype(BF)
    keys, values = qkv_ref[:, width : 2 * width], qkv_ref[:, 2 * width :]
    hat, _ = norm_lanes(own_ref[...].astype(F32))
    own = (hat * gain_ref[...]).astype(BF)
    query = mm(own, w_ref[:, :width]).astype(BF).astype(F32)
    gate = jax.nn.sigmoid(mm(own, w_ref[:, 3 * width :]))
    lanes = head_lanes(heads, width)
    query = rows_by_head(query, lanes).astype(BF)
    scores = mm(query, keys, NT) * scale + bias_ref[...].reshape(rows * heads, residues)
    mask = jnp.broadcast_to(mask_ref[...], bias_ref.shape).reshape(rows * heads, residues)
    scores = jnp.where(mask > 0.5, scores, -1000000000.0)
    powers = jnp.exp(scores - jnp.max(scores, axis=1, keepdims=True))
    weights = powers / jnp.sum(powers, axis=1, keepdims=True)
    weights_ref[...] = weights
    low = weights.astype(BF)
    low_ref[...] = low
    attn = mm(low, values).reshape(rows, heads, width)
    attn = jnp.sum(attn * lanes[None], axis=1)
    gated_ref[...] = (gate * attn).astype(BF)


def node_chunks(rows):
    size = min(rows, LANES)
    return [slice(k * size, (k + 1) * size) for k in range(rows // size)]


def gelu_parts(up):
    square = up * up
    curve = jnp.tanh(0.7978845608 * up * (1.0 + 0.044715 * square))
    half = 0.5 * (1.0 + curve)
    slope = half + up * (1.0 - curve * curve) * (0.3989422804 + 0.05351611220 * square)
    return up * half, slope


def node_kernel(
    both_ref, gated_ref, gn_ref, gs_ref, wo_ref, wu_ref, wd_ref, wn_ref, wr_ref,
    mid_ref, next_ref, proj_ref, right_ref, norm_ref,
):
    width = gated_ref.shape[1]
    residues = right_ref.shape[1]
    for rows in node_chunks(gated_ref.shape[0]):
        mid = both_ref[rows, :width].astype(F32) + mm(gated_ref[rows], wo_ref[...])
        mid_ref[rows] = mid
        hat, _ = norm_lanes(mid)
        act, _ = gelu_parts(mm((hat * gn_ref[...]).astype(BF), wu_ref[...]))
        following = mid + mm(act.astype(BF), wd_ref[...])
        next_ref[rows] = following
        hat, _ = norm_lanes(following)
        norm = (hat * gs_ref[...]).astype(BF)
        norm_ref[rows] = norm
        proj_ref[rows] = mm(norm, wn_ref[...]).astype(BF)
    right_ref[...] = mm(wr_ref[...], norm_ref[crop_rows(residues), :], NT).astype(BF)


def sublane_sum(values):
    return jnp.sum(values, axis=0, keepdims=True)


def node_back_kernel(
    outer_dim, got_ref, left_ref, both_ref, mid_ref, next_ref, gated_ref, gate_ref,
    gn_ref, gs_ref, wo_ref, wu_ref, wd_ref, wn_ref,
    gnode_ref, gd_ref, gu_ref, gout_ref, gains_ref, gainn_ref,
    dmid_ref, dattn_ref, dgate_ref, inner_ref,
    proj_ref, norm_ref, act_ref, low_ref, trans_ref, up_ref, midlow_ref,
):
    width = gated_ref.shape[1]
    devices = got_ref.shape[0] // 2
    halves = gated_ref.shape[0] // 2 // LANES
    at = 0
    for crop in range(2):
        for half in range(halves):
            total = jnp.zeros((outer_dim, LANES), F32)
            for d in range(devices):
                part = got_ref[crop * devices + d, half * outer_dim : (half + 1) * outer_dim]
                total += part.astype(F32)
            above = jnp.zeros((outer_dim, LANES), F32)
            below = jnp.zeros((LANES - 2 * outer_dim, LANES), F32)
            turned = jnp.concatenate([above, total, below], axis=0).T
            if left_ref.shape[0] == gated_ref.shape[0]:
                left = left_ref[at : at + LANES].astype(F32)
            else:
                rows = gated_ref.shape[0] // got_ref.shape[0]
                own = slice(halves * outer_dim, halves * outer_dim + rows)
                left = got_ref[at // rows : (at + LANES) // rows, own].astype(F32)
                left = left.reshape(LANES, LANES)
            proj_ref[at : at + LANES] = (turned + left).astype(BF)
            at = at + LANES
    gains, gainn = jnp.zeros((1, width), F32), jnp.zeros((1, width), F32)
    for rows in node_chunks(gated_ref.shape[0]):
        hat, inv = norm_lanes(next_ref[rows])
        norm_ref[rows] = (hat * gs_ref[...]).astype(BF)
        back = mm(proj_ref[rows], wn_ref[...], NT)
        gains += sublane_sum(back * hat)
        d_next = both_ref[rows, width:].astype(F32)
        d_next += norm_lanes_back(back * gs_ref[...], hat, inv)
        low = d_next.astype(BF)
        low_ref[rows] = low
        hat, inv = norm_lanes(mid_ref[rows])
        trans = (hat * gn_ref[...]).astype(BF)
        trans_ref[rows] = trans
        act, slope = gelu_parts(mm(trans, wu_ref[...]))
        act_ref[rows] = act.astype(BF)
        d_up = (mm(low, wd_ref[...], NT) * slope).astype(BF)
        up_ref[rows] = d_up
        back = mm(d_up, wu_ref[...], NT)
        gainn += sublane_sum(back * hat)
        d_mid = d_next + norm_lanes_back(back * gn_ref[...], hat, inv)
        dmid_ref[rows] = d_mid
        low = d_mid.astype(BF)
        midlow_ref[rows] = low
        d_gated = mm(low, wo_ref[...], NT)
        gate = gate_ref[rows]
        product = d_gated * gated_ref[rows].astype(F32)
        inner_ref[rows] = product
        dattn_ref[rows] = (d_gated * gate).astype(BF)
        dgate_ref[rows] = (product * (1.0 - gate)).astype(BF)
    gains_ref[...] = gains
    gainn_ref[...] = gainn
    gnode_ref[...] = mm(proj_ref[...], norm_ref[...], TN)[: 2 * outer_dim]
    gd_ref[...] = mm(act_ref[...], low_ref[...], TN)
    gu_ref[...] = mm(trans_ref[...], up_ref[...], TN)
    gout_ref[...] = mm(gated_ref[...], midlow_ref[...], TN)


def attend_back_kernel(
    own_ref, dattn_ref, inner_ref, qkv_ref, values_ref, weights_ref, column_ref, norm_ref,
    ds_ref, grad_ref, bias_ref,
):
    width = own_ref.shape[1]
    residues = qkv_ref.shape[0]
    rows, _, _ = norm_ref.shape
    heads = ds_ref.shape[0] // rows
    scale = 1.0 / (width // heads) ** 0.5
    lanes = head_lanes(heads, width)
    query, keys = qkv_ref[:, :width], qkv_ref[:, width : 2 * width]
    own = rows_by_head(own_ref[...].astype(F32), lanes).astype(BF)
    d_weights = mm(own, qkv_ref[:, 2 * width :], NT)
    weights = weights_ref[...]
    inner = jnp.sum(d_weights * weights, axis=1, keepdims=True)
    d_scores = (weights * (d_weights - inner)).astype(BF)
    ds_ref[...] = d_scores
    d_query = mm(d_scores, keys).reshape(rows, heads, width)
    d_query = jnp.sum(d_query * lanes[None], axis=1) * scale
    total = jnp.zeros(bias_ref.shape, F32)
    for r in range(rows):
        total += mm(d_scores[r * heads : (r + 1) * heads], norm_ref[r], NT)
    bias_ref[...] = total
    crop = crop_rows(residues)
    d_attn = dattn_ref[crop, :]
    spread = heads_by_row(values_ref[...].astype(F32), lanes).astype(BF)
    ones = heads_by_row(jnp.ones(values_ref.shape, F32), lanes).astype(BF)
    product = inner_ref[crop, :]
    high = product.astype(BF)
    rest = (product - high.astype(F32)).astype(BF)
    inner = mm(high, ones, NT) + mm(rest, ones, NT)
    column = column_ref[...]
    d_column = (column.astype(F32) * (mm(d_attn, spread, NT) - inner)).astype(BF)
    d_key = mm(d_column, query, TN).reshape(heads, rows, width)
    d_key = jnp.sum(d_key * lanes[:, None, :], axis=0) * scale
    d_value = mm(column, d_attn, TN).reshape(heads, rows, width)
    d_value = jnp.sum(d_value * lanes[:, None, :], axis=0)
    at = 0
    for part in (d_query, d_key, d_value):
        for half in range(width // LANES):
            grad_ref[at] = part[:, half * LANES : (half + 1) * LANES].astype(BF)
            at = at + 1


def adam_refs(master_ref, first_ref, second_ref, grad, outs):
    for ref, value in zip(
        outs, adam_step(master_ref[...], first_ref[...], second_ref[...], grad, 0.1, 0.1)
    ):
        ref[...] = value


def adam_kernel(count, *refs):
    for k in range(count):
        master, first, second, grad = refs[4 * k : 4 * k + 4]
        outs = refs[4 * count + 3 * k : 4 * count + 3 * k + 3]
        adam_refs(master, first, second, grad[...], outs)


def unpack(take, every, layout):
    count, late_rows, half_rows, part_up, part_z, in_blocks, outer_rows, small_rows = layout
    blocks, at = [], 0
    for _ in range(6):
        blocks.append(take(at, at + count).reshape(-1, LANES))
        at = at + count
    late = take(at, at + late_rows).reshape(-1, LANES)
    at = at + late_rows
    pair = take(at, at + half_rows)
    small = jnp.sum(take(at + half_rows, at + half_rows + small_rows), axis=0)
    lower, upper = pair[: every // 2], pair[every // 2 :]
    over = 2 * part_up - half_rows
    g_up = jnp.concatenate([lower[:, part_up:], upper[:, :over]], axis=1).reshape(-1, LANES)
    across = lambda g: jnp.concatenate(
        [g[k * LANES : (k + 1) * LANES] for k in range(g.shape[0] // LANES)], axis=1
    )
    g_in = across(late[: in_blocks * LANES])
    g_outer = late[in_blocks * LANES : in_blocks * LANES + outer_rows]
    g_down = lower[:, :part_up].reshape(-1, LANES)
    g_z = upper[:, over : over + part_z].reshape(-1, LANES)
    return blocks, (g_outer, g_in, g_z, across(g_up), g_down), small


def final_kernel(
    layout, dgate_ref, norm_ref, both_ref, dmid_ref, gain_ref, w_ref, *refs
):
    n_got = 1 if layout else 12
    got, refs = refs[:n_got], refs[n_got:]
    olds, refs = refs[:18], refs[18:]
    news, (dnode_ref, gaina_ref, small_ref, grad_ref), sums = refs[:18], refs[18:22], refs[22:]
    width = dmid_ref.shape[1]

    @pl.when(pl.program_id(0) == 0)
    def _():
        if layout:
            take = lambda start, stop: got[0][:, start:stop].astype(F32)
            blocks, grads, small = unpack(take, got[0].shape[0], layout)
        else:
            values = [ref[...] for ref in got]
            blocks, grads, small = values[:6], values[6:11], values[11]
        small_ref[...] = small
        for ref, grad in zip(sums[1:], grads):
            ref[...] = grad
        for k, block in enumerate(blocks):
            grad_ref[:, k * LANES : (k + 1) * LANES] = block.astype(BF)
        grad_ref[:, 3 * width :] = dgate_ref[...]
        sums[0][...] = mm(norm_ref[...], grad_ref[...], TN)
        total = jnp.zeros((1, width), F32)
        for rows in node_chunks(dmid_ref.shape[0]):
            hat, inv = norm_lanes(both_ref[rows, :width].astype(F32))
            back = mm(grad_ref[rows], w_ref[...], NT)
            total += sublane_sum(back * hat)
            dnode_ref[rows] = dmid_ref[rows] + norm_lanes_back(back * gain_ref[...], hat, inv)
        gaina_ref[...] = total

    for k in range(6):
        height = olds[3 * k].shape[0]
        start = pl.multiple_of(pl.program_id(0) * height, height)
        adam_refs(*olds[3 * k : 3 * k + 3], sums[k][pl.ds(start, height), :], news[3 * k : 3 * k + 3])


def whole(shape):
    return pl.BlockSpec(shape, lambda i: (0,) * len(shape))


def by_row(step, shape):
    return pl.BlockSpec((step,) + shape, lambda i: (i,) + (0,) * len(shape))


def pair_call(kernel, steps, ins, outs, args, scratch=(), flops=0, moved=0):
    return pl.pallas_call(
        kernel,
        grid=(steps,),
        in_specs=ins,
        out_specs=[spec for spec, _ in outs],
        out_shape=[shape for _, shape in outs],
        scratch_shapes=list(scratch),
        compiler_params=pltpu.CompilerParams(vmem_limit_bytes=48 * 1024 * 1024),
        cost_estimate=pl.CostEstimate(flops=flops, bytes_accessed=moved, transcendentals=0),
    )(*args)


def shards(row_devices, *arrays):
    (pair_feats, node_feats, chain_ids, out_grad, node_out_grad) = arrays[:5]
    masters, firsts, seconds = arrays[5:17], arrays[17:29], arrays[29:41]
    w_attend, w_pairbias, w_attout, w_nodeup, w_nodedown = masters[:5]
    w_node, w_outer, w_in, w_z, w_up, w_down, ln_gains = masters[5:]
    count, _, residues, width_z = pair_feats.shape
    width_s = node_feats.shape[2]
    heads = w_pairbias.shape[1]
    outer_dim = w_node.shape[1] // 2
    hidden = (w_in.shape[1] - width_z) // 8
    expand = w_up.shape[1]
    every = 2 * row_devices
    shape_of = jax.ShapeDtypeStruct
    cuts = [width_s, width_z, width_s, width_s, width_z, 2 * hidden, width_z]
    gains, at = [], 0
    for cut in cuts:
        gains.append(ln_gains[at : at + cut])
        at = at + cut
    gain_a, gain_b, gain_n, gain_s, gain_x, gain_t, gain_h = gains
    column = lambda gain: gain.reshape(-1, 1)
    line = lambda gain: gain.reshape(1, -1)
    nodes = 2 * residues
    crop_index, row_index = lax.axis_index("crop"), lax.axis_index("row")
    first_row = row_index * count
    chains = chain_ids[0]
    own_chain = lax.dynamic_slice_in_dim(chains, first_row, count, 0)
    same_own = own_chain[:, None] == chains[None, :]
    mask = same_own.astype(F32)[:, None, :]
    chain_col, chain_row = chains.reshape(-1, 1), chains.reshape(1, -1)

    att_wb, attout_wb = w_attend.astype(BF), w_attout.astype(BF)
    nodeup_wb, nodedown_wb, node_wb = w_nodeup.astype(BF), w_nodedown.astype(BF), w_node.astype(BF)
    outer_wb = w_outer.astype(BF).reshape(outer_dim, outer_dim * width_z)
    bias_wb, in_wb, z_wb = w_pairbias.astype(BF), w_in.astype(BF), w_z.astype(BF)
    up_wb, down_wb = w_up.astype(BF), w_down.astype(BF)
    bias_wt, in_wt, z_wt, up_wt, down_wt = bias_wb.T, in_wb.T, z_wb.T, up_wb.T, down_wb.T

    direct = count % 16 == 0
    step = 2 if count % 2 == 0 else 1
    steps = count // step
    pairs = count * residues

    node_both = jnp.concatenate([node_feats[:, 0], node_out_grad[:, 0]], axis=1)
    pair_x = pair_feats[:, 0]
    xt, bias_norm, pair_bias = pair_call(
        bias_kernel, steps,
        [by_row(step, (residues, width_z)), whole((width_z, 1)), whole((heads, width_z))],
        [(by_row(step, (width_z, residues)), shape_of((count, width_z, residues), BF)),
         (by_row(step, (width_z, residues)), shape_of((count, width_z, residues), BF)),
         (by_row(step, (heads, residues)), shape_of((count, heads, residues), F32))],
        [pair_x, column(gain_b), bias_wt],
        flops=2 * pairs * width_z * heads, moved=4 * pairs * width_z,
    )

    def own_rows(values):
        return lax.dynamic_slice_in_dim(values, crop_index * residues + first_row, count, 0)

    def single(kernel, outs, args, scratch=(), flops=0):
        moved = sum(arg.size * 4 for arg in args)
        return pair_call(
            kernel, 1, [whole(arg.shape) for arg in args],
            [(whole(shape), shape_of(shape, kind)) for shape, kind in outs],
            args, scratch, flops, moved,
        )

    columns = [column(gain) for gain in (gain_x, gain_t, gain_h)]
    ready = [att_wb, attout_wb, nodeup_wb, nodedown_wb, mask]
    node_both = gather_all(node_both, row_devices, [xt, pair_bias] + ready)
    node_both = node_both.reshape(nodes, 2 * width_s)
    square = (nodes, width_s)
    att_norm, gate_all, qkv_crop, att_weights, weights_low, gated_own = single(
        attend_kernel,
        [(square, BF), (square, F32), ((residues, 3 * width_s), BF),
         ((count * heads, residues), F32), ((count * heads, residues), BF),
         ((count, width_s), BF)],
        [node_both, node_feats[:, 0], line(gain_a), att_wb, pair_bias, mask],
        flops=8 * nodes * width_s * width_s,
    )
    weights_cut = weights_low.reshape(count, heads, row_devices, count).transpose(2, 0, 1, 3)
    if direct:
        weights_cut = weights_cut.reshape(row_devices, -1, LANES)
    ready = [weights_cut, node_wb, outer_wb, in_wt, chain_col, columns[0]]
    gated = gather_all(gated_own, row_devices, ready).reshape(nodes, width_s)

    node_mid, node_next, node_proj, right_t = single(
        node_kernel,
        [(square, F32), (square, F32), ((nodes, 2 * outer_dim), BF), ((outer_dim, residues), BF)],
        [node_both, gated, line(gain_n), line(gain_s), attout_wb, nodeup_wb, nodedown_wb, node_wb,
         node_wb[:, outer_dim:].T],
        scratch=[pltpu.VMEM(square, BF)], flops=18 * nodes * width_s * width_s,
    )
    node_out = own_rows(node_next).astype(BF)[:, None]
    left_vec = own_rows(node_proj[:, :outer_dim])
    outer_mix = mm(left_vec, outer_wb).astype(BF).reshape(count, outer_dim, width_z)

    share = hidden // row_devices
    dims = (share, count) if direct else None

    def sent_block(tiles, extra=0):
        if direct:
            shape = (row_devices, tiles * share * count + extra, LANES)
            return whole(shape), shape_of(shape, BF)
        return by_row(step, (tiles, hidden, LANES)), shape_of((count, tiles, hidden, LANES), BF)

    def stage(tiles):
        return [pltpu.VMEM((tiles * hidden * count, LANES), F32)] if direct else []

    def swap(block):
        return lax.all_to_all(block, "row", split_axis=0, concat_axis=0, tiled=True)

    def to_channels(block):
        if direct:
            return swap(block)
        tiles = block.shape[1]
        cut = block.reshape(count, tiles, row_devices, share, LANES)
        sent = swap(cut.transpose(2, 1, 3, 0, 4))
        return sent.transpose(1, 2, 0, 3, 4).reshape(1, tiles, share, residues, LANES)

    def to_rows(block):
        if direct:
            return swap(block)
        tiles = block.shape[1]
        cut = block.reshape(tiles, share, row_devices, count, LANES)
        got = swap(cut.transpose(2, 0, 1, 3, 4))
        return got.transpose(3, 1, 0, 2, 4).reshape(count, tiles, hidden, LANES)

    def tri_block(tiles, extra=0):
        if direct:
            return sent_block(tiles, extra)
        shape = (1, tiles, share, residues, LANES)
        spec = pl.BlockSpec((1, tiles, 1, residues, LANES), lambda i: (0, 0, i, 0, 0))
        return spec, shape_of(shape, BF)

    ride = weights_cut if direct else jnp.zeros((1, 1, LANES), BF)
    extra = ride.shape[1]
    first_sum, acts_own = pair_call(
        functools.partial(first_kernel, share, count), steps,
        [by_row(step, (width_z, residues)), by_row(step, (outer_dim, width_z)),
         whole((outer_dim, residues)), by_row(step, (1, residues)), whole((width_z, 1)),
         whole(in_wt.shape), whole(ride.shape)],
        [(by_row(step, (width_z, residues)), shape_of((count, width_z, residues), F32)),
         sent_block(6, extra)],
        [xt, outer_mix, right_t, mask, column(gain_x), in_wt, ride],
        scratch=stage(6),
        flops=16 * pairs * width_z * hidden, moved=12 * pairs * width_z,
    )

    chain_specs = [whole((residues, 1)), whole((1, residues))]
    product = 2 * share * residues**3
    ready = [in_wb, z_wb, up_wb, down_wb, z_wt, up_wt, down_wt] + columns
    acts = after(to_channels(acts_own), ready)
    weights_col = acts[:, 6 * share * count :] if direct else swap(weights_cut)
    weights_col = weights_col.reshape(residues, heads * count)
    (tri,) = pair_call(
        functools.partial(tri_kernel, dims), share, chain_specs + [tri_block(6, extra)[0]],
        [tri_block(3)], [chain_col, chain_row, acts],
        flops=2 * product, moved=share * residues * 9 * 256,
    )
    tri_rows = to_rows(tri)

    slab = by_row(step, (width_z, residues))
    second_args = [
        (by_row(step, (width_z, residues)), first_sum),
        (sent_block(3)[0], tri_rows),
        (by_row(step, (residues, width_z)), out_grad[:, 0]),
        (by_row(step, (1, residues)), mask),
    ]
    second_args += [
        (whole(v.shape), v)
        for v in (
            column(gain_x), column(gain_t), column(gain_h),
            in_wt[8 * hidden :], z_wt, z_wb, up_wt, up_wb, down_wt, down_wb,
        )
    ]
    part_up, part_z = expand // row_devices, 2 * hidden // row_devices
    half_rows = part_up + part_up // 2
    carried = 2 * half_rows if direct else 0
    acc_shapes = [
        (expand, width_z), (expand, width_z), (2 * hidden, width_z),
        ((2 * hidden + width_z) // LANES, LANES),
    ]
    pair_out, d_second, d_logit, dtri_own, g_down, g_up_t, g_z, gains_th = pair_call(
        functools.partial(second_kernel, share, count), steps,
        [spec for spec, _ in second_args],
        [(by_row(step, (residues, width_z)), shape_of((count, residues, width_z), BF)),
         (slab, shape_of((count, width_z, residues), F32)),
         (slab, shape_of((count, width_z, residues), BF)),
         sent_block(3, carried)]
        + [(whole(s), shape_of(s, F32)) for s in acc_shapes],
        [arg for _, arg in second_args],
        scratch=[pltpu.VMEM((2 * hidden, residues), F32), pltpu.VMEM((width_z, residues), F32)]
        + stage(3) + stage(3),
        flops=12 * pairs * width_z * expand, moved=20 * pairs * width_z,
    )

    dtri = to_channels(dtri_own)
    if direct:
        grad_parts = dtri[:, 3 * share * count :]
    else:
        turned = g_up_t.reshape(-1, LANES, LANES).transpose(0, 2, 1)
        parts = [g.reshape(row_devices, -1, LANES) for g in (g_down, turned, g_z)]
        spare = jnp.zeros((row_devices, part_up - part_z, LANES), F32)
        grad_parts = swap(jnp.concatenate(parts + [spare], axis=1).astype(BF))
    row_sum = jnp.sum(grad_parts.astype(F32), axis=0)
    lower, upper = row_sum[:half_rows], row_sum[half_rows:]
    low_crop = crop_index == 0
    theirs = lax.ppermute(jnp.where(low_crop, upper, lower), "crop", [(0, 1), (1, 0)])
    pair_own = (jnp.where(low_crop, lower, upper) + theirs).astype(BF)
    (dacts,) = pair_call(
        functools.partial(tri_back_kernel, dims), share,
        chain_specs + [tri_block(6, extra)[0], tri_block(3, carried)[0]],
        [tri_block(6)], [chain_col, chain_row, acts, dtri],
        flops=4 * product, moved=share * residues * 15 * 256,
    )
    dacts_rows = after(to_rows(dacts), pair_own)

    first_grad, d_mix, d_right, g_in_blocks, gains_x = pair_call(
        functools.partial(third_kernel, share, count), steps,
        [slab, sent_block(6)[0], slab, slab, by_row(step, (1, residues)),
         by_row(step, (outer_dim, width_z)), whole((outer_dim, residues)), whole((width_z, 1)),
         whole(in_wt.shape), whole(in_wb.shape)],
        [(slab, shape_of((count, width_z, residues), F32)),
         (by_row(step, (outer_dim, width_z)), shape_of((count, outer_dim, width_z), BF)),
         (whole((residues // LANES, outer_dim, LANES)),
          shape_of((residues // LANES, outer_dim, LANES), F32)),
         (whole(in_wt.shape), shape_of(in_wt.shape, BF)),
         (whole((width_z // LANES, LANES)), shape_of((width_z // LANES, LANES), F32))],
        [first_sum, dacts_rows, d_second, d_logit, mask, outer_mix, right_t, column(gain_x),
         in_wt, in_wb],
        scratch=[pltpu.VMEM((width_z, residues), F32), pltpu.VMEM((9 * hidden, residues), BF),
                 pltpu.VMEM(in_wt.shape, F32)] + stage(6),
        flops=54 * pairs * width_z * hidden, moved=20 * pairs * width_z,
    )

    mix_flat = d_mix.reshape(count, outer_dim * width_z)
    d_left = mm(mix_flat, outer_wb, NT)
    right_rows = d_right.shape[0] * outer_dim
    left_rows = jnp.pad(d_left, ((0, 0), (0, LANES - outer_dim)))
    packed = jnp.concatenate([d_right.reshape(right_rows, LANES), left_rows]).astype(BF)

    g_outer = mm(left_vec, mix_flat, TN).reshape(outer_dim * outer_dim, width_z).astype(BF)
    late_rows = g_in_blocks.shape[0] + g_outer.shape[0]
    spare = jnp.zeros((-late_rows % (every * 16), LANES), BF)
    late = jnp.concatenate([g_in_blocks, g_outer, spare]).reshape(every, -1, LANES)
    got = gather_all(packed, row_devices, late)
    late_own = scatter_sum(after(late, got))
    left_all = left_rows
    if not direct:
        left_all = got[:, right_rows : right_rows + count].reshape(nodes, LANES)

    wide_node = jnp.pad(node_wb, ((0, 0), (0, LANES - 2 * outer_dim)))
    tall, low_square = (nodes, w_nodeup.shape[1]), pltpu.VMEM(square, BF)
    (g_node, g_nodedown, g_nodeup, g_attout, gain_s_grad, gain_n_grad,
     grad_mid, d_attn, d_gate, inner) = single(
        functools.partial(node_back_kernel, outer_dim),
        [((2 * outer_dim, width_s), F32), (w_nodedown.shape, F32), (w_nodeup.shape, F32),
         (w_attout.shape, F32), ((1, width_s), F32), ((1, width_s), F32),
         (square, F32), (square, BF), (square, BF), (square, F32)],
        [got, left_all, node_both, node_mid, node_next, gated, gate_all,
         line(gain_n), line(gain_s), attout_wb, nodeup_wb, nodedown_wb, wide_node],
        scratch=[pltpu.VMEM((nodes, LANES), BF), low_square, pltpu.VMEM(tall, BF), low_square,
                 low_square, pltpu.VMEM(tall, BF), low_square],
        flops=50 * nodes * width_s * width_s,
    )

    values_own = lax.dynamic_slice(qkv_crop, (first_row, 2 * width_s), (count, width_s))
    score_grad, qkv_grad, g_bias_t = single(
        attend_back_kernel,
        [((count * heads, residues), BF), ((3 * width_s // LANES, count, LANES), BF),
         ((heads, width_z), F32)],
        [own_rows(d_attn), d_attn, inner, qkv_crop, values_own, att_weights, weights_col,
         bias_norm],
        flops=12 * count * heads * residues * width_s,
    )

    small = jnp.concatenate([g_bias_t, gains_x, gains_th]).astype(BF)
    small = jnp.pad(small, ((0, -small.shape[0] % 16), (0, 0)))
    pieces = [qkv_grad.reshape(-1, LANES), late_own, pair_own, small]
    layout = (
        count, late_own.shape[0], half_rows, part_up, part_z,
        in_wb.shape[1] // LANES, g_outer.shape[0], small.shape[0],
    )

    (pair_grad,) = pair_call(
        last_kernel, steps,
        [slab, slab, by_row(step, (heads, residues)), whole((width_z, 1)), whole((width_z, heads))],
        [(by_row(step, (residues, width_z)), shape_of((count, residues, width_z), F32))],
        [xt, first_grad, score_grad.reshape(count, heads, residues), column(gain_b), bias_wb],
        flops=4 * pairs * width_z * heads, moved=10 * pairs * width_z,
    )

    parts = 8
    split = lambda k: pl.BlockSpec((olds[k].shape[0] // parts, olds[k].shape[1]), lambda i: (i, 0))
    updated = {}

    early = {2: g_attout, 3: g_nodeup, 4: g_nodedown, 5: g_node}
    turned = lambda k, value: value.T if k == 5 else value
    specs, args, outs = [], [], []
    for k, grad in early.items():
        spec = pl.BlockSpec((grad.shape[0] // parts, grad.shape[1]), lambda i: (i, 0))
        specs += [spec] * 4
        args += [turned(k, old[k]) for old in (masters, firsts, seconds)] + [grad]
        outs += [(spec, shape_of(grad.shape, F32))] * 3
    found = pair_call(
        functools.partial(adam_kernel, len(early)), parts, specs, outs, args,
        moved=sum(7 * arg.size for arg in args),
    )
    last = gather_all(jnp.concatenate(pieces), row_devices, (pair_grad, found[0]))
    for at, k in enumerate(early):
        updated[k] = [turned(k, value) for value in found[3 * at : 3 * at + 3]]

    late_keys = (0, 6, 7, 8, 9, 10)
    got_last = [last]
    if not direct:
        blocks, sums, small = unpack(lambda a, b: last[:, a:b].astype(F32), every, layout)
        got_last = blocks + list(sums) + [small]
    fixed = [d_gate, att_norm, node_both, grad_mid, line(gain_a), att_wb] + got_last
    olds, specs = [], [whole(arg.shape) for arg in fixed]
    for k in late_keys:
        olds += [masters[k], firsts[k], seconds[k]]
    blocked = [split(k) for k in range(len(olds))]
    found = pair_call(
        functools.partial(final_kernel, layout if direct else None), parts, specs + blocked,
        [(spec, shape_of(old.shape, F32)) for spec, old in zip(blocked, olds)]
        + [(whole(shape), shape_of(shape, F32)) for shape in (square, (1, width_s), small.shape)],
        fixed + olds,
        scratch=[pltpu.VMEM((nodes, 4 * width_s), BF)]
        + [pltpu.VMEM(masters[k].shape, F32) for k in late_keys],
        flops=16 * nodes * width_s * width_s, moved=sum(7 * old.size for old in olds),
    )
    for at, k in enumerate(late_keys):
        updated[k] = found[3 * at : 3 * at + 3]
    d_nodes, gain_a_grad, small = found[18:]
    node_grad = own_rows(d_nodes)[:, None]

    g_bias = small[:heads].T
    gain_b_grad = jnp.sum(bias_wb.astype(F32) * g_bias, axis=1) / gain_b
    pair_gains = small[heads : heads + gains_x.shape[0] + gains_th.shape[0]].reshape(-1)
    gain_grad = jnp.concatenate(
        [gain_a_grad[0], gain_b_grad, gain_n_grad[0], gain_s_grad[0], pair_gains]
    )
    updated[1] = adam_step(masters[1], firsts[1], seconds[1], g_bias, 0.1, 0.1)
    updated[11] = adam_step(masters[11], firsts[11], seconds[11], gain_grad, 1.0, 0.0)
    results = [pair_out[:, None], node_out, pair_grad[:, None], node_grad]
    for k in range(12):
        results.extend(updated[k])
    return tuple(results)


def solution(mesh):
    rows4, rows3 = P("row", "crop", None, None), P("row", "crop", None)
    return jax.shard_map(
        functools.partial(shards, mesh.shape["row"]),
        mesh=mesh,
        in_specs=(rows4, rows3, P("crop", None), rows4, rows3) + (P(),) * 36,
        out_specs=(rows4, rows3, rows4, rows3) + (P(),) * 36,
        check_vma=False,
    )
```

```python
import functools
import jax
import jax.numpy as jnp
from jax import lax
from jax.experimental import pallas as pl
from jax.experimental.pallas import tpu as pltpu
from jax.sharding import PartitionSpec as P

ADAM_STEP = 4
EPS = 1e-05
BF = jnp.bfloat16
F32 = jnp.float32
LANES = 128
HALF = 64
BOTH = ("crop", "row")
NN = (((1,), (0,)), ((), ()))
NT = (((1,), (1,)), ((), ()))
TN = (((0,), (0,)), ((), ()))


def mm(left, right, dims=NN):
    return lax.dot_general(left, right, dims, preferred_element_type=F32)


def adam_step(master, first_old, second_old, grad_total, rate, decay):
    first_new = 0.9 * first_old + 0.1 * grad_total
    second_new = 0.999 * second_old + 0.001 * grad_total * grad_total
    first_hat = first_new / (1.0 - 0.9**ADAM_STEP)
    second_hat = second_new / (1.0 - 0.999**ADAM_STEP)
    master_new = master - rate * (first_hat / (jnp.sqrt(second_hat) + 1e-08) + decay * master)
    return (first_new, second_new, master_new)


def after(value, event):
    return lax.optimization_barrier((value, event))[0]


def gather_all(part, row_devices, during=()):
    every = 2 * row_devices
    groups = [[d for d in range(every) if d % 2 == k] for k in range(2)]
    spread = jnp.broadcast_to(part[None], (every // 2,) + part.shape)
    got = lax.all_to_all(
        spread, BOTH, split_axis=0, concat_axis=0, tiled=True, axis_index_groups=groups
    )
    got = after(got, during)
    other = lax.ppermute(got, "row", [(d, d ^ 1) for d in range(row_devices)])
    odd = lax.axis_index("row") % 2 == 1
    pair = [jnp.where(odd, other, got), jnp.where(odd, got, other)]
    return jnp.stack(pair, axis=1).reshape((every,) + part.shape)


def scatter_sum(sent):
    parts = lax.all_to_all(sent, BOTH, split_axis=0, concat_axis=0, tiled=True)
    return jnp.sum(parts.astype(F32), axis=0).astype(BF)


def norm_rows(values):
    centred = values - jnp.mean(values, axis=0, keepdims=True)
    inv = lax.rsqrt(jnp.mean(centred * centred, axis=0, keepdims=True) + EPS)
    return centred * inv, inv


def norm_rows_back(scaled, hat, inv):
    return inv * (
        scaled
        - jnp.mean(scaled, axis=0, keepdims=True)
        - hat * jnp.mean(scaled * hat, axis=0, keepdims=True)
    )


def turn(values):
    return pltpu.roll(values, HALF, values.ndim - 1)


def low_lanes(shape):
    return lax.broadcasted_iota(jnp.int32, shape, len(shape) - 1) < HALF


def fold_pair(first, second):
    low = low_lanes((first.shape[0], LANES))
    f_lo, f_hi = first[:, :LANES], first[:, LANES:]
    s_lo, s_hi = second[:, :LANES], second[:, LANES:]
    f_turn, s_turn = turn(f_hi), turn(s_hi)
    main_f = f_lo + jnp.where(low, f_turn, 0.0)
    main_s = s_lo + jnp.where(low, s_turn, 0.0)
    return main_f, main_s, jnp.where(low, f_hi, s_turn)


def unfold_pair(main_f, main_s, tail):
    low = low_lanes(tail.shape)
    first = jnp.concatenate([main_f, jnp.where(low, tail, turn(main_f))], axis=1)
    second = jnp.concatenate([main_s, jnp.where(low, turn(tail), turn(main_s))], axis=1)
    return first, second


def put_tile(stage_ref, tile, row, rows, values):
    high = values.shape[0]
    stage_ref[pl.ds(tile * high * rows + row, high, stride=rows), :] = values


def get_tile(stage_ref, tile, row, rows, high):
    return stage_ref[pl.ds(tile * high * rows + row, high, stride=rows), :]


def ship(stage_ref, send_ref, tiles, share, rows):
    devices = send_ref.shape[0]
    span = share * rows
    for t in range(tiles):
        block = stage_ref[t * devices * span : (t + 1) * devices * span]
        send_ref[:, t * span : (t + 1) * span] = block.reshape(devices, span, LANES).astype(BF)


def unship(got_ref, stage_ref, tiles, share, rows):
    devices = got_ref.shape[0]
    span = share * rows
    for t in range(tiles):
        block = got_ref[:, t * span : (t + 1) * span].astype(F32)
        stage_ref[t * devices * span : (t + 1) * devices * span] = block.reshape(-1, LANES)


def lane_sums(ref):
    count = ref.shape[0] // LANES
    cut = [ref[k * LANES : (k + 1) * LANES].T for k in range(count)]
    return jnp.concatenate([jnp.sum(part, axis=0, keepdims=True) for part in cut], axis=0)


def turn_blocks(ref):
    count = ref.shape[0] // LANES
    return jnp.concatenate([ref[k * LANES : (k + 1) * LANES].T for k in range(count)], axis=0)


def bias_kernel(x_ref, gain_ref, weight_ref, xt_ref, norm_ref, bias_ref):
    for r in range(x_ref.shape[0]):
        xt = x_ref[r].astype(F32).T
        xt_ref[r] = xt.astype(BF)
        hat, _ = norm_rows(xt)
        norm = (hat * gain_ref[...]).astype(BF)
        norm_ref[r] = norm
        bias_ref[r] = mm(weight_ref[...], norm)


def first_kernel(
    share, rows, xt_ref, mix_ref, right_ref, mask_ref, gain_ref, weight_ref, ride_ref,
    sum_ref, send_ref, *stage,
):
    hidden = weight_ref.shape[0] // 9
    step, _, residues = xt_ref.shape
    columns = [slice(r * residues, (r + 1) * residues) for r in range(step)]
    mixes = [mm(mix_ref[r], right_ref[...], TN) for r in range(step)]
    total = jnp.concatenate([xt_ref[r].astype(F32) + mixes[r] for r in range(step)], axis=1)
    for r in range(step):
        sum_ref[r] = total[:, columns[r]]
    hat, _ = norm_rows(total)
    norm = (hat * gain_ref[...]).astype(BF)
    mask = jnp.concatenate([mask_ref[r] for r in range(step)], axis=1)
    for pair in range(2):
        acts = []
        for block in (2 * pair, 2 * pair + 1):
            value = mm(weight_ref[block * hidden : (block + 1) * hidden], norm)
            gate = mm(weight_ref[(block + 4) * hidden : (block + 5) * hidden], norm)
            acts.append(jax.nn.sigmoid(gate) * value * mask)
        for r in range(step):
            row = pl.program_id(0) * step + r
            tiles = fold_pair(*(act[:, columns[r]] for act in acts))
            for t in range(3):
                if stage:
                    put_tile(stage[0], 3 * pair + t, row, rows, tiles[t])
                else:
                    send_ref[r, 3 * pair + t] = tiles[t].astype(BF)
    if stage:

        @pl.when(pl.program_id(0) == pl.num_programs(0) - 1)
        def _():
            ship(stage[0], send_ref, 6, share, rows)
            send_ref[:, 6 * share * rows :] = ride_ref[...]


def chain_mask(col_ref, row_ref):
    return col_ref[...] == row_ref[...]


def flat_rows(ref, tile, spot):
    block = ref[:, spot(tile)] if spot else ref[:, tile, 0]
    return block.reshape(-1, block.shape[-1])


def slot_operands(ref, pair, spot):
    main_f, main_s, tail = (flat_rows(ref, 3 * pair + t, spot).astype(F32) for t in range(3))
    low = low_lanes(tail.shape)
    zero = jnp.zeros_like(tail)
    first = jnp.concatenate([main_f, jnp.where(low, tail, zero)], axis=1).astype(BF)
    second = jnp.concatenate([main_s, jnp.where(low, turn(tail), zero)], axis=1).astype(BF)
    return first, second


def channel_spots(dims):
    if not dims:
        return [None]
    share, rows = dims
    each = share // pl.num_programs(0)
    first = pl.program_id(0) * each

    def spot_of(channel):
        return lambda tile: pl.ds(pl.multiple_of((tile * share + channel) * rows, rows), rows)

    return [spot_of(first + k) for k in range(each)]


def raw_columns(slots, same):
    values = slots.astype(F32)
    main, tail = values[:, :LANES], values[:, LANES:]
    wide = jnp.concatenate(
        [main, jnp.where(low_lanes(tail.shape), tail, turn(main))], axis=1
    )
    return jnp.where(same, wide, 0.0).astype(BF)


def store_tiles(out_ref, pair, spot, tiles):
    for t in range(3):
        block = tiles[t].astype(BF).reshape(out_ref.shape[0], -1, LANES)
        if spot:
            out_ref[:, spot(3 * pair + t)] = block
        else:
            out_ref[:, 3 * pair + t, 0] = block


def tri_kernel(dims, col_ref, row_ref, acts_ref, out_ref):
    same = chain_mask(col_ref, row_ref)
    for spot in channel_spots(dims):
        left_out, right_out = slot_operands(acts_ref, 0, spot)
        left_in, right_in = slot_operands(acts_ref, 1, spot)
        outgoing = jnp.where(same, mm(left_out, right_out, NT), 0.0)
        incoming = mm(raw_columns(left_in, same), right_in, TN)
        low = low_lanes((outgoing.shape[0], LANES))
        o_lo, o_hi = outgoing[:, :LANES], outgoing[:, LANES:]
        main_o = o_lo + jnp.where(low, turn(o_hi), 0.0)
        tail = jnp.where(low, o_hi, turn(incoming[:, LANES:]))
        store_tiles(out_ref, 0, spot, (main_o, incoming[:, :LANES], tail))


def tri_back_kernel(dims, col_ref, row_ref, acts_ref, grad_ref, out_ref):
    same = chain_mask(col_ref, row_ref)
    for spot in channel_spots(dims):
        left_out, right_out = slot_operands(acts_ref, 0, spot)
        left_in, right_in = slot_operands(acts_ref, 1, spot)
        grad_out, grad_in = slot_operands(grad_ref, 0, spot)
        raw_out = raw_columns(grad_out, same)
        d_left = mm(raw_out, right_out)
        d_right = mm(raw_out, left_out, TN)
        low = low_lanes((d_left.shape[0], LANES))
        tail = jnp.where(low, d_left[:, LANES:], turn(d_right[:, LANES:]))
        store_tiles(out_ref, 0, spot, (d_left[:, :LANES], d_right[:, :LANES], tail))
        d_left = jnp.where(same, mm(right_in, grad_in, NT), 0.0)
        d_right = mm(raw_columns(left_in, same), grad_in)
        l_lo, l_hi = d_left[:, :LANES], d_left[:, LANES:]
        main_l = l_lo + jnp.where(low, turn(l_hi), 0.0)
        tail = jnp.where(low, l_hi, turn(d_right[:, LANES:]))
        store_tiles(out_ref, 1, spot, (main_l, d_right[:, :LANES], tail))


def second_kernel(
    share, rows, sum_ref, tri_ref, grad_ref, mask_ref, gx_ref, gt_ref, gh_ref,
    wgate_ref, wzt_ref, wz_ref, wut_ref, wu_ref, wdt_ref, wd_ref,
    out_ref, ds_ref, dlogit_ref, send_ref, gd_ref, gu_ref, gz_ref, gains_ref, gaint_ref, gainh_ref,
    *stage,
):
    @pl.when(pl.program_id(0) == 0)
    def _():
        for acc in (gd_ref, gu_ref, gz_ref, gaint_ref, gainh_ref):
            acc[...] = jnp.zeros_like(acc)
        if stage:
            unship(tri_ref, stage[0], 3, share, rows)

    step, _, residues = sum_ref.shape
    joined = lambda values: jnp.concatenate(list(values), axis=1)
    total = joined(sum_ref[r] for r in range(step))
    mask = joined(mask_ref[r] for r in range(step))
    hat_x, _ = norm_rows(total)
    norm = (hat_x * gx_ref[...]).astype(BF)
    out_gate = jax.nn.sigmoid(mm(wgate_ref[...], norm))
    combined = []
    for r in range(step):
        row = pl.program_id(0) * step + r
        if stage:
            tiles = [get_tile(stage[0], t, row, rows, total.shape[0]) for t in range(3)]
        else:
            tiles = [tri_ref[r, t].astype(F32) for t in range(3)]
        combined.append(jnp.concatenate(unfold_pair(*tiles), axis=0))
    hat_t, inv_t = norm_rows(joined(combined))
    tri_norm = (hat_t * gt_ref[...]).astype(BF)
    tri_proj = mm(wzt_ref[...], tri_norm)
    second = total + out_gate * tri_proj * mask
    hat_h, inv_h = norm_rows(second)
    trans_in = (hat_h * gh_ref[...]).astype(BF)
    act, slope = gelu_parts(mm(wut_ref[...], trans_in))
    act = act.astype(BF)
    result = second + mm(wdt_ref[...], act)
    for r in range(step):
        out_ref[r] = result[:, r * residues : (r + 1) * residues].T.astype(BF)
    grad_low = joined(grad_ref[r].astype(F32).T.astype(BF) for r in range(step))
    gd_ref[...] += mm(act, grad_low, NT)
    d_up = (mm(wd_ref[...], grad_low) * slope).astype(BF)
    gu_ref[...] += mm(d_up, trans_in, NT)
    back = mm(wu_ref[...], d_up)
    prod = back * hat_h
    gainh_ref[...] += sum(prod[:, r * residues : (r + 1) * residues] for r in range(step))
    d_second = grad_low.astype(F32) + norm_rows_back(back * gh_ref[...], hat_h, inv_h)
    gated = d_second * mask * out_gate
    d_tri = gated.astype(BF)
    d_logit = (gated * tri_proj * (1.0 - out_gate)).astype(BF)
    for r in range(step):
        ds_ref[r] = d_second[:, r * residues : (r + 1) * residues]
        dlogit_ref[r] = d_logit[:, r * residues : (r + 1) * residues]
    gz_ref[...] += mm(tri_norm, d_tri, NT)
    back = mm(wz_ref[...], d_tri)
    prod = back * hat_t
    gaint_ref[...] += sum(prod[:, r * residues : (r + 1) * residues] for r in range(step))
    comb = norm_rows_back(back * gt_ref[...], hat_t, inv_t)
    hidden = comb.shape[0] // 2
    for r in range(step):
        row = pl.program_id(0) * step + r
        own = comb[:, r * residues : (r + 1) * residues]
        tiles = fold_pair(own[:hidden], own[hidden:])
        for t in range(3):
            if stage:
                put_tile(stage[1], t, row, rows, tiles[t])
            else:
                send_ref[r, t] = tiles[t].astype(BF)

    @pl.when(pl.program_id(0) == pl.num_programs(0) - 1)
    def _():
        gains_ref[...] = jnp.concatenate([lane_sums(gaint_ref), lane_sums(gainh_ref)], axis=0)
        if stage:
            ship(stage[1], send_ref, 3, share, rows)
            devices = send_ref.shape[0]
            at = 3 * share * rows
            for acc, turned in ((gd_ref, False), (gu_ref, True), (gz_ref, False)):
                part = acc.shape[0] // devices
                block = turn_blocks(acc) if turned else acc[...]
                send_ref[:, at : at + part] = block.reshape(devices, part, LANES).astype(BF)
                at = at + part
            spare = send_ref.shape[1] - at
            send_ref[:, at:] = jnp.zeros((devices, spare, LANES), BF)


def third_kernel(
    share, rows, sum_ref, acts_ref, ds_ref, dlogit_ref, mask_ref, mix_ref, right_ref, gx_ref,
    wt_ref, w_ref, left_ref, outer_ref, carry_ref,
    fg_ref, packed_ref, late_ref, gains_ref,
    gainx_ref, dproj_ref, acc_ref, dmix_ref, dright_ref, gout_ref, *stage,
):
    @pl.when(pl.program_id(0) == 0)
    def _():
        for acc in (dright_ref, acc_ref, gainx_ref):
            acc[...] = jnp.zeros_like(acc)
        if stage:
            unship(acts_ref, stage[0], 6, share, rows)

    hidden = wt_ref.shape[0] // 9
    step, _, residues = sum_ref.shape
    joined = lambda ref: jnp.concatenate([ref[r] for r in range(step)], axis=1)
    hat, inv = norm_rows(joined(sum_ref))
    norm = (hat * gx_ref[...]).astype(BF)
    mask = joined(mask_ref)
    for pair in range(2):
        unfolded = []
        for r in range(step):
            row = pl.program_id(0) * step + r
            tiles = range(3 * pair, 3 * pair + 3)
            if stage:
                tiles = [get_tile(stage[0], t, row, rows, hidden) for t in tiles]
            else:
                tiles = [acts_ref[r, t].astype(F32) for t in tiles]
            unfolded.append(unfold_pair(*tiles))
        for side in range(2):
            block = 2 * pair + side
            value = mm(wt_ref[block * hidden : (block + 1) * hidden], norm)
            gate = mm(wt_ref[(block + 4) * hidden : (block + 5) * hidden], norm)
            sig = jax.nn.sigmoid(gate)
            d_value = jnp.concatenate([both[side] for both in unfolded], axis=1) * mask * sig
            d_gate = d_value * value * (1.0 - sig)
            dproj_ref[block * hidden : (block + 1) * hidden] = d_value.astype(BF)
            dproj_ref[(block + 4) * hidden : (block + 5) * hidden] = d_gate.astype(BF)
    dproj_ref[8 * hidden :] = joined(dlogit_ref)
    d_proj = dproj_ref[...]
    acc_ref[...] += mm(d_proj, norm, NT)
    back = mm(w_ref[...], d_proj)
    prod = back * hat
    gainx_ref[...] += sum(prod[:, r * residues : (r + 1) * residues] for r in range(step))
    first = joined(ds_ref) + norm_rows_back(back * gx_ref[...], hat, inv)
    low = first.astype(BF)
    for r in range(step):
        own = slice(r * residues, (r + 1) * residues)
        fg_ref[r] = first[:, own]
        outer_dim = right_ref.shape[0]
        row = pl.program_id(0) * step + r
        mixed = pl.ds(pl.multiple_of(row * outer_dim, outer_dim), outer_dim)
        dmix_ref[mixed, :] = mm(right_ref[...], low[:, own], NT).astype(BF).astype(F32)
        right = mm(mix_ref[r], low[:, own])
        for half in range(dright_ref.shape[0]):
            dright_ref[half] += right[:, half * LANES : (half + 1) * LANES]

    @pl.when(pl.program_id(0) == pl.num_programs(0) - 1)
    def _():
        gains_ref[...] = lane_sums(gainx_ref)
        outer_dim, count = right_ref.shape[0], left_ref.shape[0]
        d_left = jnp.zeros((count, LANES), F32)
        below = jnp.zeros((LANES - outer_dim, LANES), BF)
        for b in range(outer_dim):
            mixed = dmix_ref[pl.ds(b, count, stride=outer_dim), :].astype(BF)
            weight = outer_ref[pl.ds(b, outer_dim, stride=outer_dim), :].astype(BF)
            d_left += mm(mixed, jnp.concatenate([weight, below], axis=0), NT)
            gout_ref[pl.ds(b, outer_dim, stride=outer_dim), :] = mm(left_ref[...], mixed, TN)
        at = 0
        for half in range(dright_ref.shape[0]):
            packed_ref[at : at + outer_dim] = dright_ref[half].astype(BF)
            at = at + outer_dim
        packed_ref[at : at + count] = d_left.astype(BF)
        if carry_ref.shape[0] > 1:
            start = packed_ref.shape[0] - carry_ref.shape[0]
            packed_ref[start:] = carry_ref[...]
        in_rows, outer_rows = acc_ref.shape[0], gout_ref.shape[0]
        late_ref[:in_rows] = turn_blocks(acc_ref).astype(BF)
        late_ref[in_rows : in_rows + outer_rows] = gout_ref[...].astype(BF)
        spare = late_ref.shape[0] - in_rows - outer_rows
        late_ref[in_rows + outer_rows :] = jnp.zeros((spare, LANES), BF)


def last_kernel(xt_ref, fg_ref, ds_ref, gain_ref, w_ref, out_ref):
    for r in range(xt_ref.shape[0]):
        hat, inv = norm_rows(xt_ref[r].astype(F32))
        back = mm(w_ref[...], ds_ref[r])
        out_ref[r] = (fg_ref[r] + norm_rows_back(back * gain_ref[...], hat, inv)).T


def norm_lanes(values):
    centred = values - jnp.mean(values, axis=1, keepdims=True)
    inv = lax.rsqrt(jnp.mean(centred * centred, axis=1, keepdims=True) + EPS)
    return centred * inv, inv


def norm_lanes_back(scaled, hat, inv):
    return inv * (
        scaled
        - jnp.mean(scaled, axis=1, keepdims=True)
        - hat * jnp.mean(scaled * hat, axis=1, keepdims=True)
    )


def head_lanes(heads, width):
    depth = width // heads
    lane = lax.broadcasted_iota(jnp.int32, (heads, width), 1)
    head = lax.broadcasted_iota(jnp.int32, (heads, width), 0)
    return ((lane >= head * depth) & (lane < (head + 1) * depth)).astype(F32)


def rows_by_head(values, lanes):
    spread = values[:, None, :] * lanes[None]
    return spread.reshape(-1, values.shape[1])


def heads_by_row(values, lanes):
    spread = values[None] * lanes[:, None, :]
    return spread.reshape(-1, values.shape[1])


def crop_rows(residues):
    return pl.ds(pl.multiple_of(lax.axis_index("crop") * residues, residues), residues)


def attend_kernel(
    both_ref, own_ref, gain_ref, w_ref, bias_ref, mask_ref,
    norm_ref, gate_ref, qkv_ref, weights_ref, low_ref, gated_ref,
):
    width = own_ref.shape[1]
    residues = mask_ref.shape[2]
    heads = bias_ref.shape[1]
    rows = own_ref.shape[0]
    scale = 1.0 / (width // heads) ** 0.5
    hat, _ = norm_lanes(both_ref[:, :width].astype(F32))
    norm_ref[...] = (hat * gain_ref[...]).astype(BF)
    gate_ref[...] = jax.nn.sigmoid(mm(norm_ref[...], w_ref[:, 3 * width :]))
    qkv_ref[...] = mm(norm_ref[crop_rows(residues), :], w_ref[:, : 3 * width]).astype(BF)
    keys, values = qkv_ref[:, width : 2 * width], qkv_ref[:, 2 * width :]
    hat, _ = norm_lanes(own_ref[...].astype(F32))
    own = (hat * gain_ref[...]).astype(BF)
    query = mm(own, w_ref[:, :width]).astype(BF).astype(F32)
    gate = jax.nn.sigmoid(mm(own, w_ref[:, 3 * width :]))
    lanes = head_lanes(heads, width)
    query = rows_by_head(query, lanes).astype(BF)
    scores = mm(query, keys, NT) * scale + bias_ref[...].reshape(rows * heads, residues)
    mask = jnp.broadcast_to(mask_ref[...], bias_ref.shape).reshape(rows * heads, residues)
    scores = jnp.where(mask > 0.5, scores, -1000000000.0)
    powers = jnp.exp(scores - jnp.max(scores, axis=1, keepdims=True))
    weights = powers / jnp.sum(powers, axis=1, keepdims=True)
    weights_ref[...] = weights
    low = weights.astype(BF)
    low_ref[...] = low
    attn = mm(low, values).reshape(rows, heads, width)
    attn = jnp.sum(attn * lanes[None], axis=1)
    gated_ref[...] = (gate * attn).astype(BF)


def node_chunks(rows):
    size = min(rows, LANES)
    return [slice(k * size, (k + 1) * size) for k in range(rows // size)]


def gelu_parts(up):
    square = up * up
    curve = jnp.tanh(0.7978845608 * up * (1.0 + 0.044715 * square))
    half = 0.5 * (1.0 + curve)
    slope = half + up * (1.0 - curve * curve) * (0.3989422804 + 0.05351611220 * square)
    return up * half, slope


def node_kernel(
    both_ref, gated_ref, gn_ref, gs_ref, wo_ref, wu_ref, wd_ref, wn_ref, wr_ref,
    mid_ref, next_ref, proj_ref, right_ref, norm_ref,
):
    width = gated_ref.shape[1]
    residues = right_ref.shape[1]
    for rows in node_chunks(gated_ref.shape[0]):
        mid = both_ref[rows, :width].astype(F32) + mm(gated_ref[rows], wo_ref[...])
        mid_ref[rows] = mid
        hat, _ = norm_lanes(mid)
        act, _ = gelu_parts(mm((hat * gn_ref[...]).astype(BF), wu_ref[...]))
        following = mid + mm(act.astype(BF), wd_ref[...])
        next_ref[rows] = following
        hat, _ = norm_lanes(following)
        norm = (hat * gs_ref[...]).astype(BF)
        norm_ref[rows] = norm
        proj_ref[rows] = mm(norm, wn_ref[...]).astype(BF)
    right_ref[...] = mm(wr_ref[...], norm_ref[crop_rows(residues), :], NT).astype(BF)


def sublane_sum(values):
    return jnp.sum(values, axis=0, keepdims=True)


def node_back_kernel(
    outer_dim, got_ref, left_ref, both_ref, mid_ref, next_ref, gated_ref, gate_ref,
    gn_ref, gs_ref, wo_ref, wu_ref, wd_ref, wn_ref,
    gnode_ref, gd_ref, gu_ref, gout_ref, gains_ref, gainn_ref,
    dmid_ref, dattn_ref, dgate_ref, inner_ref,
    proj_ref, norm_ref, act_ref, low_ref, trans_ref, up_ref, midlow_ref,
):
    width = gated_ref.shape[1]
    devices = got_ref.shape[0] // 2
    halves = gated_ref.shape[0] // 2 // LANES
    at = 0
    for crop in range(2):
        for half in range(halves):
            total = jnp.zeros((outer_dim, LANES), F32)
            for d in range(devices):
                part = got_ref[crop * devices + d, half * outer_dim : (half + 1) * outer_dim]
                total += part.astype(F32)
            above = jnp.zeros((outer_dim, LANES), F32)
            below = jnp.zeros((LANES - 2 * outer_dim, LANES), F32)
            turned = jnp.concatenate([above, total, below], axis=0).T
            if left_ref.shape[0] == gated_ref.shape[0]:
                left = left_ref[at : at + LANES].astype(F32)
            else:
                rows = gated_ref.shape[0] // got_ref.shape[0]
                own = slice(halves * outer_dim, halves * outer_dim + rows)
                left = got_ref[at // rows : (at + LANES) // rows, own].astype(F32)
                left = left.reshape(LANES, LANES)
            proj_ref[at : at + LANES] = (turned + left).astype(BF)
            at = at + LANES
    gains, gainn = jnp.zeros((1, width), F32), jnp.zeros((1, width), F32)
    for rows in node_chunks(gated_ref.shape[0]):
        hat, inv = norm_lanes(next_ref[rows])
        norm_ref[rows] = (hat * gs_ref[...]).astype(BF)
        back = mm(proj_ref[rows], wn_ref[...], NT)
        gains += sublane_sum(back * hat)
        d_next = both_ref[rows, width:].astype(F32)
        d_next += norm_lanes_back(back * gs_ref[...], hat, inv)
        low = d_next.astype(BF)
        low_ref[rows] = low
        hat, inv = norm_lanes(mid_ref[rows])
        trans = (hat * gn_ref[...]).astype(BF)
        trans_ref[rows] = trans
        act, slope = gelu_parts(mm(trans, wu_ref[...]))
        act_ref[rows] = act.astype(BF)
        d_up = (mm(low, wd_ref[...], NT) * slope).astype(BF)
        up_ref[rows] = d_up
        back = mm(d_up, wu_ref[...], NT)
        gainn += sublane_sum(back * hat)
        d_mid = d_next + norm_lanes_back(back * gn_ref[...], hat, inv)
        dmid_ref[rows] = d_mid
        low = d_mid.astype(BF)
        midlow_ref[rows] = low
        d_gated = mm(low, wo_ref[...], NT)
        gate = gate_ref[rows]
        product = d_gated * gated_ref[rows].astype(F32)
        inner_ref[rows] = product
        dattn_ref[rows] = (d_gated * gate).astype(BF)
        dgate_ref[rows] = (product * (1.0 - gate)).astype(BF)
    gains_ref[...] = gains
    gainn_ref[...] = gainn
    gnode_ref[...] = mm(proj_ref[...], norm_ref[...], TN)[: 2 * outer_dim]
    gd_ref[...] = mm(act_ref[...], low_ref[...], TN)
    gu_ref[...] = mm(trans_ref[...], up_ref[...], TN)
    gout_ref[...] = mm(gated_ref[...], midlow_ref[...], TN)


def attend_back_kernel(
    own_ref, dattn_ref, inner_ref, qkv_ref, values_ref, weights_ref, column_ref, norm_ref,
    ds_ref, grad_ref, bias_ref,
):
    width = own_ref.shape[1]
    residues = qkv_ref.shape[0]
    rows, _, _ = norm_ref.shape
    heads = ds_ref.shape[0] // rows
    scale = 1.0 / (width // heads) ** 0.5
    lanes = head_lanes(heads, width)
    query, keys = qkv_ref[:, :width], qkv_ref[:, width : 2 * width]
    own = rows_by_head(own_ref[...].astype(F32), lanes).astype(BF)
    d_weights = mm(own, qkv_ref[:, 2 * width :], NT)
    weights = weights_ref[...]
    inner = jnp.sum(d_weights * weights, axis=1, keepdims=True)
    d_scores = (weights * (d_weights - inner)).astype(BF)
    ds_ref[...] = d_scores
    d_query = mm(d_scores, keys).reshape(rows, heads, width)
    d_query = jnp.sum(d_query * lanes[None], axis=1) * scale
    total = jnp.zeros(bias_ref.shape, F32)
    for r in range(rows):
        total += mm(d_scores[r * heads : (r + 1) * heads], norm_ref[r], NT)
    bias_ref[...] = total
    crop = crop_rows(residues)
    d_attn = dattn_ref[crop, :]
    spread = heads_by_row(values_ref[...].astype(F32), lanes).astype(BF)
    ones = heads_by_row(jnp.ones(values_ref.shape, F32), lanes).astype(BF)
    product = inner_ref[crop, :]
    high = product.astype(BF)
    rest = (product - high.astype(F32)).astype(BF)
    inner = mm(high, ones, NT) + mm(rest, ones, NT)
    column = column_ref[...]
    d_column = (column.astype(F32) * (mm(d_attn, spread, NT) - inner)).astype(BF)
    d_key = mm(d_column, query, TN).reshape(heads, rows, width)
    d_key = jnp.sum(d_key * lanes[:, None, :], axis=0) * scale
    d_value = mm(column, d_attn, TN).reshape(heads, rows, width)
    d_value = jnp.sum(d_value * lanes[:, None, :], axis=0)
    at = 0
    for part in (d_query, d_key, d_value):
        for half in range(width // LANES):
            grad_ref[at] = part[:, half * LANES : (half + 1) * LANES].astype(BF)
            at = at + 1


def adam_refs(master_ref, first_ref, second_ref, grad, outs):
    for ref, value in zip(
        outs, adam_step(master_ref[...], first_ref[...], second_ref[...], grad, 0.1, 0.1)
    ):
        ref[...] = value


def adam_kernel(count, layout, *refs):
    n_pair = 1 if layout else 3
    ins = 4 * count + 9 + n_pair
    outs, sums = refs[ins : ins + 3 * count + 9], refs[ins + 3 * count + 9 :]
    for k in range(count):
        master, first, second, grad = refs[4 * k : 4 * k + 4]
        adam_refs(master, first, second, grad[...], outs[3 * k : 3 * k + 3])
    olds, pair = refs[4 * count : 4 * count + 9], refs[4 * count + 9 : ins]

    @pl.when(pl.program_id(0) == 0)
    def _():
        if layout:
            start, part_up, part_z = layout
            values = unpack_pair(pair[0][:, start:].astype(F32), part_up, part_z)
        else:
            values = [ref[...] for ref in pair]
        for ref, value in zip(sums, values):
            ref[...] = value

    for k in range(3):
        height = olds[3 * k].shape[0]
        start = pl.multiple_of(pl.program_id(0) * height, height)
        at = 3 * (count + k)
        adam_refs(*olds[3 * k : 3 * k + 3], sums[k][pl.ds(start, height), :], outs[at : at + 3])


def across(rows):
    count = rows.shape[0] // LANES
    return jnp.concatenate([rows[k * LANES : (k + 1) * LANES] for k in range(count)], axis=1)


def unpack(take, layout):
    count, late_rows, in_rows, outer_rows, small_rows = layout
    blocks, at = [], 0
    for _ in range(6):
        blocks.append(take(at, at + count).reshape(-1, LANES))
        at = at + count
    late = take(at, at + late_rows).reshape(-1, LANES)
    at = at + late_rows
    small = jnp.sum(take(at, at + small_rows), axis=0)
    return blocks, (late[in_rows : in_rows + outer_rows], across(late[:in_rows])), small


def unpack_pair(pair, part_up, part_z):
    devices, half_rows, _ = pair.shape
    lower, upper = pair[: devices // 2], pair[devices // 2 :]
    over = 2 * part_up - half_rows
    g_up = jnp.concatenate([lower[:, part_up:], upper[:, :over]], axis=1).reshape(-1, LANES)
    g_down = lower[:, :part_up].reshape(-1, LANES)
    return upper[:, over : over + part_z].reshape(-1, LANES), across(g_up), g_down


def final_kernel(
    layout, dgate_ref, norm_ref, both_ref, dmid_ref, gain_ref, w_ref, *refs
):
    n_got = 1 if layout else 9
    got, refs = refs[:n_got], refs[n_got:]
    olds, refs = refs[:9], refs[9:]
    news, (dnode_ref, gaina_ref, small_ref, grad_ref), sums = refs[:9], refs[9:13], refs[13:]
    width = dmid_ref.shape[1]

    @pl.when(pl.program_id(0) == 0)
    def _():
        if layout:
            take = lambda start, stop: got[0][:, start:stop].astype(F32)
            blocks, grads, small = unpack(take, layout)
        else:
            values = [ref[...] for ref in got]
            blocks, grads, small = values[:6], values[6:8], values[8]
        small_ref[...] = small
        for ref, grad in zip(sums[1:], grads):
            ref[...] = grad
        for k, block in enumerate(blocks):
            grad_ref[:, k * LANES : (k + 1) * LANES] = block.astype(BF)
        grad_ref[:, 3 * width :] = dgate_ref[...]
        sums[0][...] = mm(norm_ref[...], grad_ref[...], TN)
        total = jnp.zeros((1, width), F32)
        for rows in node_chunks(dmid_ref.shape[0]):
            hat, inv = norm_lanes(both_ref[rows, :width].astype(F32))
            back = mm(grad_ref[rows], w_ref[...], NT)
            total += sublane_sum(back * hat)
            dnode_ref[rows] = dmid_ref[rows] + norm_lanes_back(back * gain_ref[...], hat, inv)
        gaina_ref[...] = total

    for k in range(3):
        height = olds[3 * k].shape[0]
        start = pl.multiple_of(pl.program_id(0) * height, height)
        adam_refs(*olds[3 * k : 3 * k + 3], sums[k][pl.ds(start, height), :], news[3 * k : 3 * k + 3])


def whole(shape):
    return pl.BlockSpec(shape, lambda i: (0,) * len(shape))


def by_row(step, shape):
    return pl.BlockSpec((step,) + shape, lambda i: (i,) + (0,) * len(shape))


def pair_call(kernel, steps, ins, outs, args, scratch=(), flops=0, moved=0, free=(), near=()):
    args = [
        arg if at in free else pltpu.with_memory_space_constraint(arg, pltpu.HBM)
        for at, arg in enumerate(args)
    ]
    shapes = [
        shape if at in near else pltpu.HBM(shape.shape, shape.dtype)
        for at, (_, shape) in enumerate(outs)
    ]
    return pl.pallas_call(
        kernel,
        grid=(steps,),
        in_specs=ins,
        out_specs=[spec for spec, _ in outs],
        out_shape=shapes,
        scratch_shapes=list(scratch),
        compiler_params=pltpu.CompilerParams(vmem_limit_bytes=48 * 1024 * 1024),
        cost_estimate=pl.CostEstimate(flops=flops, bytes_accessed=moved, transcendentals=0),
    )(*args)


def shards(row_devices, *arrays):
    (pair_feats, node_feats, chain_ids, out_grad, node_out_grad) = arrays[:5]
    masters, firsts, seconds = arrays[5:17], arrays[17:29], arrays[29:41]
    w_attend, w_pairbias, w_attout, w_nodeup, w_nodedown = masters[:5]
    w_node, w_outer, w_in, w_z, w_up, w_down, ln_gains = masters[5:]
    count, _, residues, width_z = pair_feats.shape
    width_s = node_feats.shape[2]
    heads = w_pairbias.shape[1]
    outer_dim = w_node.shape[1] // 2
    hidden = (w_in.shape[1] - width_z) // 8
    expand = w_up.shape[1]
    every = 2 * row_devices
    shape_of = jax.ShapeDtypeStruct
    cuts = [width_s, width_z, width_s, width_s, width_z, 2 * hidden, width_z]
    gains, at = [], 0
    for cut in cuts:
        gains.append(ln_gains[at : at + cut])
        at = at + cut
    gain_a, gain_b, gain_n, gain_s, gain_x, gain_t, gain_h = gains
    column = lambda gain: gain.reshape(-1, 1)
    line = lambda gain: gain.reshape(1, -1)
    nodes = 2 * residues
    crop_index, row_index = lax.axis_index("crop"), lax.axis_index("row")
    first_row = row_index * count
    chains = chain_ids[0]
    own_chain = lax.dynamic_slice_in_dim(chains, first_row, count, 0)
    same_own = own_chain[:, None] == chains[None, :]
    mask = same_own.astype(F32)[:, None, :]
    chain_col, chain_row = chains.reshape(-1, 1), chains.reshape(1, -1)

    att_wb, attout_wb = w_attend.astype(BF), w_attout.astype(BF)
    nodeup_wb, nodedown_wb, node_wb = w_nodeup.astype(BF), w_nodedown.astype(BF), w_node.astype(BF)
    outer_wb = w_outer.astype(BF).reshape(outer_dim, outer_dim * width_z)
    bias_wb, in_wb, z_wb = w_pairbias.astype(BF), w_in.astype(BF), w_z.astype(BF)
    up_wb, down_wb = w_up.astype(BF), w_down.astype(BF)
    bias_wt, in_wt, z_wt, up_wt, down_wt = bias_wb.T, in_wb.T, z_wb.T, up_wb.T, down_wb.T

    direct = count % 16 == 0
    step = next(size for size in (4, 2, 1) if count % size == 0)
    steps = count // step
    pairs = count * residues

    node_both = jnp.concatenate([node_feats[:, 0], node_out_grad[:, 0]], axis=1)
    pair_x = pair_feats[:, 0]
    xt, bias_norm, pair_bias = pair_call(
        bias_kernel, steps,
        [by_row(step, (residues, width_z)), whole((width_z, 1)), whole((heads, width_z))],
        [(by_row(step, (width_z, residues)), shape_of((count, width_z, residues), BF)),
         (by_row(step, (width_z, residues)), shape_of((count, width_z, residues), BF)),
         (by_row(step, (heads, residues)), shape_of((count, heads, residues), F32))],
        [pair_x, column(gain_b), bias_wt], free=(0, 1, 2), near=(2,),
        flops=2 * pairs * width_z * heads, moved=4 * pairs * width_z,
    )

    def own_rows(values):
        return lax.dynamic_slice_in_dim(values, crop_index * residues + first_row, count, 0)

    def single(kernel, outs, args, scratch=(), flops=0, far=(), apart=False):
        moved = sum(arg.size * 4 for arg in args)
        return pair_call(
            kernel, 1, [whole(arg.shape) for arg in args],
            [(whole(shape), shape_of(shape, kind)) for shape, kind in outs],
            args, scratch, flops, moved, (0,) if apart else range(len(args)),
            [at for at in range(len(outs)) if at not in far],
        )

    columns = [column(gain) for gain in (gain_x, gain_t, gain_h)]
    ready = [att_wb, attout_wb, nodeup_wb, nodedown_wb, mask]
    node_both = gather_all(node_both, row_devices, [xt, pair_bias] + ready)
    node_both = node_both.reshape(nodes, 2 * width_s)
    square = (nodes, width_s)
    att_norm, gate_all, qkv_crop, att_weights, weights_low, gated_own = single(
        attend_kernel,
        [(square, BF), (square, F32), ((residues, 3 * width_s), BF),
         ((count * heads, residues), F32), ((count * heads, residues), BF),
         ((count, width_s), BF)],
        [node_both, node_feats[:, 0], line(gain_a), att_wb, pair_bias, mask],
        flops=8 * nodes * width_s * width_s, far=(0, 1, 2, 3),
    )
    weights_cut = weights_low.reshape(count, heads, row_devices, count).transpose(2, 0, 1, 3)
    if direct:
        weights_cut = weights_cut.reshape(row_devices, -1, LANES)
    ready = [weights_cut, node_wb, outer_wb, in_wt, chain_col, columns[0]]
    gated = gather_all(gated_own, row_devices, ready).reshape(nodes, width_s)

    node_mid, node_next, node_proj, right_t = single(
        node_kernel,
        [(square, F32), (square, F32), ((nodes, 2 * outer_dim), BF), ((outer_dim, residues), BF)],
        [node_both, gated, line(gain_n), line(gain_s), attout_wb, nodeup_wb, nodedown_wb, node_wb,
         node_wb[:, outer_dim:].T],
        scratch=[pltpu.VMEM(square, BF)], flops=18 * nodes * width_s * width_s, far=(0, 1),
    )
    node_out = own_rows(node_next).astype(BF)[:, None]
    left_vec = own_rows(node_proj[:, :outer_dim])
    outer_mix = mm(left_vec, outer_wb).astype(BF).reshape(count, outer_dim, width_z)

    share = hidden // row_devices
    dims = (share, count) if direct else None

    def sent_block(tiles, extra=0):
        if direct:
            shape = (row_devices, tiles * share * count + extra, LANES)
            return whole(shape), shape_of(shape, BF)
        return by_row(step, (tiles, hidden, LANES)), shape_of((count, tiles, hidden, LANES), BF)

    def stage(tiles):
        return [pltpu.VMEM((tiles * hidden * count, LANES), F32)] if direct else []

    def swap(block):
        return lax.all_to_all(block, "row", split_axis=0, concat_axis=0, tiled=True)

    def to_channels(block):
        if direct:
            return swap(block)
        tiles = block.shape[1]
        cut = block.reshape(count, tiles, row_devices, share, LANES)
        sent = swap(cut.transpose(2, 1, 3, 0, 4))
        return sent.transpose(1, 2, 0, 3, 4).reshape(1, tiles, share, residues, LANES)

    def to_rows(block):
        if direct:
            return swap(block)
        tiles = block.shape[1]
        cut = block.reshape(tiles, share, row_devices, count, LANES)
        got = swap(cut.transpose(2, 0, 1, 3, 4))
        return got.transpose(3, 1, 0, 2, 4).reshape(count, tiles, hidden, LANES)

    def tri_block(tiles, extra=0):
        if direct:
            return sent_block(tiles, extra)
        shape = (1, tiles, share, residues, LANES)
        spec = pl.BlockSpec((1, tiles, 1, residues, LANES), lambda i: (0, 0, i, 0, 0))
        return spec, shape_of(shape, BF)

    ride = weights_cut if direct else jnp.zeros((1, 1, LANES), BF)
    extra = ride.shape[1]
    first_sum, acts_own = pair_call(
        functools.partial(first_kernel, share, count), steps,
        [by_row(step, (width_z, residues)), by_row(step, (outer_dim, width_z)),
         whole((outer_dim, residues)), by_row(step, (1, residues)), whole((width_z, 1)),
         whole(in_wt.shape), whole(ride.shape)],
        [(by_row(step, (width_z, residues)), shape_of((count, width_z, residues), F32)),
         sent_block(6, extra)],
        [xt, outer_mix, right_t, mask, column(gain_x), in_wt, ride],
        scratch=stage(6),
        flops=16 * pairs * width_z * hidden, moved=12 * pairs * width_z,
    )

    tri_steps = lambda channels: channels // 2 if direct and channels % 2 == 0 else channels
    chain_specs = [whole((residues, 1)), whole((1, residues))]
    product = 2 * share * residues**3
    ready = [in_wb, z_wb, up_wb, down_wb, z_wt, up_wt, down_wt] + columns
    acts = after(to_channels(acts_own), ready)
    weights_col = acts[:, 6 * share * count :] if direct else swap(weights_cut)
    weights_col = weights_col.reshape(residues, heads * count)
    (tri,) = pair_call(
        functools.partial(tri_kernel, dims), tri_steps(share), chain_specs + [tri_block(6, extra)[0]],
        [tri_block(3)], [chain_col, chain_row, acts], free=(2,),
        flops=2 * product, moved=share * residues * 9 * 256,
    )
    tri_rows = to_rows(tri)

    slab = by_row(step, (width_z, residues))
    second_args = [
        (by_row(step, (width_z, residues)), first_sum),
        (sent_block(3)[0], tri_rows),
        (by_row(step, (residues, width_z)), out_grad[:, 0]),
        (by_row(step, (1, residues)), mask),
    ]
    second_args += [
        (whole(v.shape), v)
        for v in (
            column(gain_x), column(gain_t), column(gain_h),
            in_wt[8 * hidden :], z_wt, z_wb, up_wt, up_wb, down_wt, down_wb,
        )
    ]
    part_up, part_z = expand // row_devices, 2 * hidden // row_devices
    half_rows = part_up + part_up // 2
    carried = 2 * half_rows if direct else 0
    acc_shapes = [
        (expand, width_z), (expand, width_z), (2 * hidden, width_z),
        ((2 * hidden + width_z) // LANES, LANES),
    ]
    pair_out, d_second, d_logit, dtri_own, g_down, g_up_t, g_z, gains_th = pair_call(
        functools.partial(second_kernel, share, count), steps,
        [spec for spec, _ in second_args],
        [(by_row(step, (residues, width_z)), shape_of((count, residues, width_z), BF)),
         (slab, shape_of((count, width_z, residues), F32)),
         (slab, shape_of((count, width_z, residues), BF)),
         sent_block(3, carried)]
        + [(whole(s), shape_of(s, F32)) for s in acc_shapes],
        [arg for _, arg in second_args], free=(1,),
        scratch=[pltpu.VMEM((2 * hidden, residues), F32), pltpu.VMEM((width_z, residues), F32)]
        + stage(3) + stage(3),
        flops=12 * pairs * width_z * expand, moved=20 * pairs * width_z,
    )

    dtri = to_channels(dtri_own)
    if direct:
        grad_parts = dtri[:, 3 * share * count :]
    else:
        turned = g_up_t.reshape(-1, LANES, LANES).transpose(0, 2, 1)
        parts = [g.reshape(row_devices, -1, LANES) for g in (g_down, turned, g_z)]
        spare = jnp.zeros((row_devices, part_up - part_z, LANES), F32)
        grad_parts = swap(jnp.concatenate(parts + [spare], axis=1).astype(BF))
    row_sum = jnp.sum(grad_parts.astype(F32), axis=0)
    lower, upper = row_sum[:half_rows], row_sum[half_rows:]
    low_crop = crop_index == 0
    theirs = lax.ppermute(jnp.where(low_crop, upper, lower), "crop", [(0, 1), (1, 0)])
    pair_own = (jnp.where(low_crop, lower, upper) + theirs).astype(BF)
    (dacts,) = pair_call(
        functools.partial(tri_back_kernel, dims), tri_steps(share),
        chain_specs + [tri_block(6, extra)[0], tri_block(3, carried)[0]],
        [tri_block(6)], [chain_col, chain_row, acts, dtri], free=(2,),
        flops=4 * product, moved=share * residues * 15 * 256,
    )
    dacts_rows = after(to_rows(dacts), pair_own)

    right_rows = residues // LANES * outer_dim
    left_rows = -(-count // 16) * 16
    carry = pair_own if direct else jnp.zeros((1, LANES), BF)
    packed_rows = right_rows + left_rows + (half_rows if direct else 0)
    in_rows, outer_rows = in_wt.shape[0], w_outer.shape[0]
    late_rows = -(-(in_rows + outer_rows) // (every * 16)) * every * 16
    first_grad, packed, late, gains_x = pair_call(
        functools.partial(third_kernel, share, count), steps,
        [slab, sent_block(6)[0], slab, slab, by_row(step, (1, residues)),
         by_row(step, (outer_dim, width_z)), whole((outer_dim, residues)), whole((width_z, 1)),
         whole(in_wt.shape), whole(in_wb.shape), whole(left_vec.shape), whole(w_outer.shape),
         whole(carry.shape)],
        [(slab, shape_of((count, width_z, residues), F32)),
         (whole((packed_rows, LANES)), shape_of((packed_rows, LANES), BF)),
         (whole((late_rows, LANES)), shape_of((late_rows, LANES), BF)),
         (whole((width_z // LANES, LANES)), shape_of((width_z // LANES, LANES), F32))],
        [first_sum, dacts_rows, d_second, d_logit, mask, outer_mix, right_t, columns[0],
         in_wt, in_wb, left_vec, w_outer, carry],
        free=(1,), near=(1, 2),
        scratch=[pltpu.VMEM((width_z, residues), F32), pltpu.VMEM((9 * hidden, step * residues), BF),
                 pltpu.VMEM(in_wt.shape, F32), pltpu.VMEM((count * outer_dim, LANES), F32),
                 pltpu.VMEM((residues // LANES, outer_dim, LANES), F32),
                 pltpu.VMEM(w_outer.shape, F32)] + stage(6),
        flops=54 * pairs * width_z * hidden, moved=20 * pairs * width_z,
    )
    got = gather_all(packed, row_devices, late)
    late_own = scatter_sum(after(late, got).reshape(every, -1, LANES))
    left_all = left_vec
    if not direct:
        left_all = got[:, right_rows : right_rows + count].reshape(nodes, LANES)

    wide_node = jnp.pad(node_wb, ((0, 0), (0, LANES - 2 * outer_dim)))
    tall, low_square = (nodes, w_nodeup.shape[1]), pltpu.VMEM(square, BF)
    (g_node, g_nodedown, g_nodeup, g_attout, gain_s_grad, gain_n_grad,
     grad_mid, d_attn, d_gate, inner) = single(
        functools.partial(node_back_kernel, outer_dim),
        [((2 * outer_dim, width_s), F32), (w_nodedown.shape, F32), (w_nodeup.shape, F32),
         (w_attout.shape, F32), ((1, width_s), F32), ((1, width_s), F32),
         (square, F32), (square, BF), (square, BF), (square, F32)],
        [got, left_all, node_both, node_mid, node_next, gated, gate_all,
         line(gain_n), line(gain_s), attout_wb, nodeup_wb, nodedown_wb, wide_node],
        scratch=[pltpu.VMEM((nodes, LANES), BF), low_square, pltpu.VMEM(tall, BF), low_square,
                 low_square, pltpu.VMEM(tall, BF), low_square],
        flops=50 * nodes * width_s * width_s, apart=True,
    )

    values_own = lax.dynamic_slice(qkv_crop, (first_row, 2 * width_s), (count, width_s))
    score_grad, qkv_grad, g_bias_t = single(
        attend_back_kernel,
        [((count * heads, residues), BF), ((3 * width_s // LANES, count, LANES), BF),
         ((heads, width_z), F32)],
        [own_rows(d_attn), d_attn, inner, qkv_crop, values_own, att_weights, weights_col,
         bias_norm],
        flops=12 * count * heads * residues * width_s,
    )

    small = jnp.concatenate([g_bias_t, gains_x, gains_th]).astype(BF)
    small = jnp.pad(small, ((0, -small.shape[0] % 16), (0, 0)))
    pieces = [qkv_grad.reshape(-1, LANES), late_own, small]
    layout = (count, late_own.shape[0], in_rows, outer_rows, small.shape[0])

    (pair_grad,) = pair_call(
        last_kernel, steps,
        [slab, slab, by_row(step, (heads, residues)), whole((width_z, 1)), whole((width_z, heads))],
        [(by_row(step, (residues, width_z)), shape_of((count, residues, width_z), F32))],
        [xt, first_grad, score_grad.reshape(count, heads, residues), column(gain_b), bias_wb],
        flops=4 * pairs * width_z * heads, moved=10 * pairs * width_z,
    )

    parts = 2
    split = lambda k: pl.BlockSpec((olds[k].shape[0] // parts, olds[k].shape[1]), lambda i: (i, 0))
    updated = {}

    early = {2: g_attout, 3: g_nodeup, 4: g_nodedown, 5: g_node}
    turned = lambda k, value: value.T if k == 5 else value
    specs, args, outs = [], [], []
    for k, grad in early.items():
        spec = pl.BlockSpec((grad.shape[0] // parts, grad.shape[1]), lambda i: (i, 0))
        specs += [spec] * 4
        args += [turned(k, old[k]) for old in (masters, firsts, seconds)] + [grad]
        outs += [(spec, shape_of(grad.shape, F32))] * 3
    pair_keys = (8, 9, 10)
    for k in pair_keys:
        height, width = masters[k].shape
        spec = pl.BlockSpec((height // parts, width), lambda i: (i, 0))
        specs += [spec] * 3
        args += [masters[k], firsts[k], seconds[k]]
        outs += [(spec, shape_of((height, width), F32))] * 3
    if direct:
        pair_got, pair_layout = [got], (right_rows + left_rows, part_up, part_z)
    else:
        pair_all = gather_all(pair_own, row_devices)
        pair_got, pair_layout = list(unpack_pair(pair_all.astype(F32), part_up, part_z)), None
    specs += [whole(arg.shape) for arg in pair_got]
    args += pair_got
    found = pair_call(
        functools.partial(adam_kernel, len(early), pair_layout), parts, specs, outs, args,
        scratch=[pltpu.VMEM(masters[k].shape, F32) for k in pair_keys],
        moved=sum(7 * arg.size for arg in args),
    )
    beside = (pair_grad, found[0], node_out)
    last = gather_all(jnp.concatenate(pieces), row_devices, beside)
    for at, k in enumerate(early):
        updated[k] = [turned(k, value) for value in found[3 * at : 3 * at + 3]]
    for at, k in enumerate(pair_keys, len(early)):
        updated[k] = found[3 * at : 3 * at + 3]

    late_keys = (0, 6, 7)
    got_last = [last]
    if not direct:
        blocks, sums, small = unpack(lambda a, b: last[:, a:b].astype(F32), layout)
        got_last = blocks + list(sums) + [small]
    fixed = [d_gate, att_norm, node_both, grad_mid, line(gain_a), att_wb] + got_last
    olds, specs = [], [whole(arg.shape) for arg in fixed]
    for k in late_keys:
        olds += [masters[k], firsts[k], seconds[k]]
    blocked = [split(k) for k in range(len(olds))]
    found = pair_call(
        functools.partial(final_kernel, layout if direct else None), parts, specs + blocked,
        [(spec, shape_of(old.shape, F32)) for spec, old in zip(blocked, olds)]
        + [(whole(shape), shape_of(shape, F32)) for shape in (square, (1, width_s), small.shape)],
        fixed + olds,
        scratch=[pltpu.VMEM((nodes, 4 * width_s), BF)]
        + [pltpu.VMEM(masters[k].shape, F32) for k in late_keys],
        flops=16 * nodes * width_s * width_s, moved=sum(7 * old.size for old in olds),
    )
    for at, k in enumerate(late_keys):
        updated[k] = found[3 * at : 3 * at + 3]
    d_nodes, gain_a_grad, small = found[9:]
    node_grad = own_rows(d_nodes)[:, None]

    g_bias = small[:heads].T
    gain_b_grad = jnp.sum(bias_wb.astype(F32) * g_bias, axis=1) / gain_b
    pair_gains = small[heads : heads + gains_x.shape[0] + gains_th.shape[0]].reshape(-1)
    gain_grad = jnp.concatenate(
        [gain_a_grad[0], gain_b_grad, gain_n_grad[0], gain_s_grad[0], pair_gains]
    )
    updated[1] = adam_step(masters[1], firsts[1], seconds[1], g_bias, 0.1, 0.1)
    updated[11] = adam_step(masters[11], firsts[11], seconds[11], gain_grad, 1.0, 0.0)
    results = [pair_out[:, None], node_out, pair_grad[:, None], node_grad]
    for k in range(12):
        results.extend(updated[k])
    return tuple(results)


def solution(mesh):
    rows4, rows3 = P("row", "crop", None, None), P("row", "crop", None)
    return jax.shard_map(
        functools.partial(shards, mesh.shape["row"]),
        mesh=mesh,
        in_specs=(rows4, rows3, P("crop", None), rows4, rows3) + (P(),) * 36,
        out_specs=(rows4, rows3, rows4, rows3) + (P(),) * 36,
        check_vma=False,
    )
```

```python
import functools
import jax
import jax.numpy as jnp
from jax import lax
from jax.experimental import pallas as pl
from jax.experimental.pallas import tpu as pltpu
from jax.sharding import PartitionSpec as P

ADAM_STEP = 4
EPS = 1e-05
BF = jnp.bfloat16
F32 = jnp.float32
LANES = 128
HALF = 64
BOTH = ("crop", "row")
NN = (((1,), (0,)), ((), ()))
NT = (((1,), (1,)), ((), ()))
TN = (((0,), (0,)), ((), ()))


def mm(left, right, dims=NN):
    return lax.dot_general(left, right, dims, preferred_element_type=F32)


def adam_step(master, first_old, second_old, grad_total, rate, decay):
    first_new = 0.9 * first_old + 0.1 * grad_total
    second_new = 0.999 * second_old + 0.001 * grad_total * grad_total
    first_hat = first_new / (1.0 - 0.9**ADAM_STEP)
    second_hat = second_new / (1.0 - 0.999**ADAM_STEP)
    master_new = master - rate * (first_hat / (jnp.sqrt(second_hat) + 1e-08) + decay * master)
    return (first_new, second_new, master_new)


def after(value, event):
    return lax.optimization_barrier((value, event))[0]


def spread_over(part, row_devices):
    return jnp.broadcast_to(part[None], (row_devices,) + part.shape)


def same_core_exchange(block, row_devices):
    groups = [[d for d in range(2 * row_devices) if d % 2 == k] for k in range(2)]
    return lax.all_to_all(
        block, BOTH, split_axis=0, concat_axis=0, tiled=True, axis_index_groups=groups
    )


def core_exchange(block, row_devices):
    return lax.ppermute(block, "row", [(d, d ^ 1) for d in range(row_devices)])


def gather_all(spread, row_devices, during=()):
    every = 2 * row_devices
    first = same_core_exchange(spread, row_devices)
    got = after(first, during)
    other = core_exchange(got, row_devices)
    odd = lax.axis_index("row") % 2 == 1
    pair = [jnp.where(odd, other, got), jnp.where(odd, got, other)]
    return jnp.stack(pair, axis=1).reshape((every,) + spread.shape[1:]), first


def norm_rows(values):
    centred = values - jnp.mean(values, axis=0, keepdims=True)
    inv = lax.rsqrt(jnp.mean(centred * centred, axis=0, keepdims=True) + EPS)
    return centred * inv, inv


def norm_rows_back(scaled, hat, inv):
    return inv * (
        scaled
        - jnp.mean(scaled, axis=0, keepdims=True)
        - hat * jnp.mean(scaled * hat, axis=0, keepdims=True)
    )


def turn(values):
    return pltpu.roll(values, HALF, values.ndim - 1)


def low_lanes(shape):
    return lax.broadcasted_iota(jnp.int32, shape, len(shape) - 1) < HALF


def fold_pair(first, second):
    low = low_lanes((first.shape[0], LANES))
    f_lo, f_hi = first[:, :LANES], first[:, LANES:]
    s_lo, s_hi = second[:, :LANES], second[:, LANES:]
    f_turn, s_turn = turn(f_hi), turn(s_hi)
    main_f = f_lo + jnp.where(low, f_turn, 0.0)
    main_s = s_lo + jnp.where(low, s_turn, 0.0)
    return main_f, main_s, jnp.where(low, f_hi, s_turn)


def unfold_pair(main_f, main_s, tail):
    low = low_lanes(tail.shape)
    first = jnp.concatenate([main_f, jnp.where(low, tail, turn(main_f))], axis=1)
    second = jnp.concatenate([main_s, jnp.where(low, turn(tail), turn(main_s))], axis=1)
    return first, second


def put_tile(stage_ref, tile, row, rows, values):
    high = values.shape[0]
    stage_ref[pl.ds(tile * high * rows + row, high, stride=rows), :] = values


def get_tile(stage_ref, tile, row, rows, high):
    return stage_ref[pl.ds(tile * high * rows + row, high, stride=rows), :]


def ship(stage_ref, send_ref, tiles, share, rows):
    devices = send_ref.shape[0]
    span = share * rows
    for t in range(tiles):
        block = stage_ref[t * devices * span : (t + 1) * devices * span]
        send_ref[:, t * span : (t + 1) * span] = block.reshape(devices, span, LANES).astype(BF)


def unship(got_ref, stage_ref, tiles, share, rows):
    devices = got_ref.shape[0]
    span = share * rows
    for t in range(tiles):
        block = got_ref[:, t * span : (t + 1) * span].astype(F32)
        stage_ref[t * devices * span : (t + 1) * devices * span] = block.reshape(-1, LANES)


def lane_sums(ref):
    count = ref.shape[0] // LANES
    cut = [ref[k * LANES : (k + 1) * LANES].T for k in range(count)]
    return jnp.concatenate([jnp.sum(part, axis=0, keepdims=True) for part in cut], axis=0)


def spread_rows(ref, at, rows):
    shape = (ref.shape[0],) + rows.shape
    ref[:, at : at + rows.shape[0]] = jnp.broadcast_to(rows[None], shape)


def turn_blocks(ref):
    count = ref.shape[0] // LANES
    return jnp.concatenate([ref[k * LANES : (k + 1) * LANES].T for k in range(count)], axis=0)


def bias_kernel(x_ref, gain_ref, weight_ref, xt_ref, norm_ref, bias_ref):
    for r in range(x_ref.shape[0]):
        xt = x_ref[r].astype(F32).T
        xt_ref[r] = xt.astype(BF)
        hat, _ = norm_rows(xt)
        norm = (hat * gain_ref[...]).astype(BF)
        norm_ref[r] = norm
        bias_ref[r] = mm(weight_ref[...], norm)


def first_kernel(
    share, rows, xt_ref, mix_ref, right_ref, mask_ref, gain_ref, weight_ref, ride_ref,
    sum_ref, send_ref, *stage,
):
    hidden = weight_ref.shape[0] // 9
    step, _, residues = xt_ref.shape
    columns = [slice(r * residues, (r + 1) * residues) for r in range(step)]
    mixes = [mm(mix_ref[r], right_ref[...], TN) for r in range(step)]
    total = jnp.concatenate([xt_ref[r].astype(F32) + mixes[r] for r in range(step)], axis=1)
    for r in range(step):
        sum_ref[r] = total[:, columns[r]]
    hat, _ = norm_rows(total)
    norm = (hat * gain_ref[...]).astype(BF)
    mask = jnp.concatenate([mask_ref[r] for r in range(step)], axis=1)
    for pair in range(2):
        acts = []
        for block in (2 * pair, 2 * pair + 1):
            value = mm(weight_ref[block * hidden : (block + 1) * hidden], norm)
            gate = mm(weight_ref[(block + 4) * hidden : (block + 5) * hidden], norm)
            acts.append(jax.nn.sigmoid(gate) * value * mask)
        for r in range(step):
            row = pl.program_id(0) * step + r
            tiles = fold_pair(*(act[:, columns[r]] for act in acts))
            for t in range(3):
                if stage:
                    put_tile(stage[0], 3 * pair + t, row, rows, tiles[t])
                else:
                    send_ref[r, 3 * pair + t] = tiles[t].astype(BF)
    if stage:

        @pl.when(pl.program_id(0) == pl.num_programs(0) - 1)
        def _():
            ship(stage[0], send_ref, 6, share, rows)
            send_ref[:, 6 * share * rows :] = ride_ref[...]


def chain_mask(col_ref, row_ref):
    return col_ref[...] == row_ref[...]


def flat_rows(ref, tile, spot):
    block = ref[:, spot(tile)] if spot else ref[:, tile, 0]
    return block.reshape(-1, block.shape[-1])


def slot_operands(ref, pair, spot):
    main_f, main_s, tail = (flat_rows(ref, 3 * pair + t, spot).astype(F32) for t in range(3))
    low = low_lanes(tail.shape)
    zero = jnp.zeros_like(tail)
    first = jnp.concatenate([main_f, jnp.where(low, tail, zero)], axis=1).astype(BF)
    second = jnp.concatenate([main_s, jnp.where(low, turn(tail), zero)], axis=1).astype(BF)
    return first, second


def channel_spots(dims):
    if not dims:
        return [None]
    share, rows = dims
    each = share // pl.num_programs(0)
    first = pl.program_id(0) * each

    def spot_of(channel):
        return lambda tile: pl.ds(pl.multiple_of((tile * share + channel) * rows, rows), rows)

    return [spot_of(first + k) for k in range(each)]


def raw_columns(slots, same):
    values = slots.astype(F32)
    main, tail = values[:, :LANES], values[:, LANES:]
    wide = jnp.concatenate(
        [main, jnp.where(low_lanes(tail.shape), tail, turn(main))], axis=1
    )
    return jnp.where(same, wide, 0.0).astype(BF)


def store_tiles(out_ref, pair, spot, tiles):
    for t in range(3):
        block = tiles[t].astype(BF).reshape(out_ref.shape[0], -1, LANES)
        if spot:
            out_ref[:, spot(3 * pair + t)] = block
        else:
            out_ref[:, 3 * pair + t, 0] = block


def tri_kernel(dims, col_ref, row_ref, acts_ref, out_ref):
    same = chain_mask(col_ref, row_ref)
    for spot in channel_spots(dims):
        left_out, right_out = slot_operands(acts_ref, 0, spot)
        left_in, right_in = slot_operands(acts_ref, 1, spot)
        outgoing = jnp.where(same, mm(left_out, right_out, NT), 0.0)
        incoming = mm(raw_columns(left_in, same), right_in, TN)
        low = low_lanes((outgoing.shape[0], LANES))
        o_lo, o_hi = outgoing[:, :LANES], outgoing[:, LANES:]
        main_o = o_lo + jnp.where(low, turn(o_hi), 0.0)
        tail = jnp.where(low, o_hi, turn(incoming[:, LANES:]))
        store_tiles(out_ref, 0, spot, (main_o, incoming[:, :LANES], tail))


def tri_back_kernel(dims, col_ref, row_ref, acts_ref, grad_ref, out_ref):
    same = chain_mask(col_ref, row_ref)
    for spot in channel_spots(dims):
        left_out, right_out = slot_operands(acts_ref, 0, spot)
        left_in, right_in = slot_operands(acts_ref, 1, spot)
        grad_out, grad_in = slot_operands(grad_ref, 0, spot)
        raw_out = raw_columns(grad_out, same)
        d_left = mm(raw_out, right_out)
        d_right = mm(raw_out, left_out, TN)
        low = low_lanes((d_left.shape[0], LANES))
        tail = jnp.where(low, d_left[:, LANES:], turn(d_right[:, LANES:]))
        store_tiles(out_ref, 0, spot, (d_left[:, :LANES], d_right[:, :LANES], tail))
        d_left = jnp.where(same, mm(right_in, grad_in, NT), 0.0)
        d_right = mm(raw_columns(left_in, same), grad_in)
        l_lo, l_hi = d_left[:, :LANES], d_left[:, LANES:]
        main_l = l_lo + jnp.where(low, turn(l_hi), 0.0)
        tail = jnp.where(low, l_hi, turn(d_right[:, LANES:]))
        store_tiles(out_ref, 1, spot, (main_l, d_right[:, :LANES], tail))


def second_kernel(
    share, rows, sum_ref, tri_ref, grad_ref, mask_ref, gx_ref, gt_ref, gh_ref,
    wgate_ref, wzt_ref, wz_ref, wut_ref, wu_ref, wdt_ref, wd_ref,
    out_ref, ds_ref, dlogit_ref, send_ref, gd_ref, gu_ref, gz_ref, gains_ref, gaint_ref, gainh_ref,
    *stage,
):
    @pl.when(pl.program_id(0) == 0)
    def _():
        for acc in (gd_ref, gu_ref, gz_ref, gaint_ref, gainh_ref):
            acc[...] = jnp.zeros_like(acc)
        if stage:
            unship(tri_ref, stage[0], 3, share, rows)

    step, _, residues = sum_ref.shape
    joined = lambda values: jnp.concatenate(list(values), axis=1)
    total = joined(sum_ref[r] for r in range(step))
    mask = joined(mask_ref[r] for r in range(step))
    hat_x, _ = norm_rows(total)
    norm = (hat_x * gx_ref[...]).astype(BF)
    out_gate = jax.nn.sigmoid(mm(wgate_ref[...], norm))
    combined = []
    for r in range(step):
        row = pl.program_id(0) * step + r
        if stage:
            tiles = [get_tile(stage[0], t, row, rows, total.shape[0]) for t in range(3)]
        else:
            tiles = [tri_ref[r, t].astype(F32) for t in range(3)]
        combined.append(jnp.concatenate(unfold_pair(*tiles), axis=0))
    hat_t, inv_t = norm_rows(joined(combined))
    tri_norm = (hat_t * gt_ref[...]).astype(BF)
    tri_proj = mm(wzt_ref[...], tri_norm)
    second = total + out_gate * tri_proj * mask
    hat_h, inv_h = norm_rows(second)
    trans_in = (hat_h * gh_ref[...]).astype(BF)
    act, slope = gelu_parts(mm(wut_ref[...], trans_in))
    act = act.astype(BF)
    result = second + mm(wdt_ref[...], act)
    for r in range(step):
        out_ref[r] = result[:, r * residues : (r + 1) * residues].T.astype(BF)
    grad_low = joined(grad_ref[r].astype(F32).T.astype(BF) for r in range(step))
    gd_ref[...] += mm(act, grad_low, NT)
    d_up = (mm(wd_ref[...], grad_low) * slope).astype(BF)
    gu_ref[...] += mm(d_up, trans_in, NT)
    back = mm(wu_ref[...], d_up)
    prod = back * hat_h
    gainh_ref[...] += sum(prod[:, r * residues : (r + 1) * residues] for r in range(step))
    d_second = grad_low.astype(F32) + norm_rows_back(back * gh_ref[...], hat_h, inv_h)
    gated = d_second * mask * out_gate
    d_tri = gated.astype(BF)
    d_logit = (gated * tri_proj * (1.0 - out_gate)).astype(BF)
    for r in range(step):
        ds_ref[r] = d_second[:, r * residues : (r + 1) * residues]
        dlogit_ref[r] = d_logit[:, r * residues : (r + 1) * residues]
    gz_ref[...] += mm(tri_norm, d_tri, NT)
    back = mm(wz_ref[...], d_tri)
    prod = back * hat_t
    gaint_ref[...] += sum(prod[:, r * residues : (r + 1) * residues] for r in range(step))
    comb = norm_rows_back(back * gt_ref[...], hat_t, inv_t)
    hidden = comb.shape[0] // 2
    for r in range(step):
        row = pl.program_id(0) * step + r
        own = comb[:, r * residues : (r + 1) * residues]
        tiles = fold_pair(own[:hidden], own[hidden:])
        for t in range(3):
            if stage:
                put_tile(stage[1], t, row, rows, tiles[t])
            else:
                send_ref[r, t] = tiles[t].astype(BF)

    @pl.when(pl.program_id(0) == pl.num_programs(0) - 1)
    def _():
        gains_ref[...] = jnp.concatenate([lane_sums(gaint_ref), lane_sums(gainh_ref)], axis=0)
        if stage:
            ship(stage[1], send_ref, 3, share, rows)
            devices = send_ref.shape[0]
            at = 3 * share * rows
            for acc, turned in ((gd_ref, False), (gu_ref, True), (gz_ref, False)):
                part = acc.shape[0] // devices
                block = turn_blocks(acc) if turned else acc[...]
                send_ref[:, at : at + part] = block.reshape(devices, part, LANES).astype(BF)
                at = at + part
            spare = send_ref.shape[1] - at
            send_ref[:, at:] = jnp.zeros((devices, spare, LANES), BF)


def third_kernel(
    share, rows, sum_ref, acts_ref, ds_ref, dlogit_ref, mask_ref, mix_ref, right_ref, gx_ref,
    wt_ref, w_ref, left_ref, outer_ref, carry_ref,
    fg_ref, packed_ref, late_ref, gains_ref,
    gainx_ref, dproj_ref, acc_ref, dmix_ref, dright_ref, gout_ref, *stage,
):
    @pl.when(pl.program_id(0) == 0)
    def _():
        for acc in (dright_ref, acc_ref, gainx_ref):
            acc[...] = jnp.zeros_like(acc)
        if stage:
            unship(acts_ref, stage[0], 6, share, rows)

    hidden = wt_ref.shape[0] // 9
    step, _, residues = sum_ref.shape
    joined = lambda ref: jnp.concatenate([ref[r] for r in range(step)], axis=1)
    hat, inv = norm_rows(joined(sum_ref))
    norm = (hat * gx_ref[...]).astype(BF)
    mask = joined(mask_ref)
    for pair in range(2):
        unfolded = []
        for r in range(step):
            row = pl.program_id(0) * step + r
            tiles = range(3 * pair, 3 * pair + 3)
            if stage:
                tiles = [get_tile(stage[0], t, row, rows, hidden) for t in tiles]
            else:
                tiles = [acts_ref[r, t].astype(F32) for t in tiles]
            unfolded.append(unfold_pair(*tiles))
        for side in range(2):
            block = 2 * pair + side
            value = mm(wt_ref[block * hidden : (block + 1) * hidden], norm)
            gate = mm(wt_ref[(block + 4) * hidden : (block + 5) * hidden], norm)
            sig = jax.nn.sigmoid(gate)
            d_value = jnp.concatenate([both[side] for both in unfolded], axis=1) * mask * sig
            d_gate = d_value * value * (1.0 - sig)
            dproj_ref[block * hidden : (block + 1) * hidden] = d_value.astype(BF)
            dproj_ref[(block + 4) * hidden : (block + 5) * hidden] = d_gate.astype(BF)
    dproj_ref[8 * hidden :] = joined(dlogit_ref)
    d_proj = dproj_ref[...]
    acc_ref[...] += mm(d_proj, norm, NT)
    back = mm(w_ref[...], d_proj)
    prod = back * hat
    gainx_ref[...] += sum(prod[:, r * residues : (r + 1) * residues] for r in range(step))
    first = joined(ds_ref) + norm_rows_back(back * gx_ref[...], hat, inv)
    low = first.astype(BF)
    for r in range(step):
        own = slice(r * residues, (r + 1) * residues)
        fg_ref[r] = first[:, own]
        outer_dim = right_ref.shape[0]
        row = pl.program_id(0) * step + r
        mixed = pl.ds(pl.multiple_of(row * outer_dim, outer_dim), outer_dim)
        dmix_ref[mixed, :] = mm(right_ref[...], low[:, own], NT).astype(BF).astype(F32)
        right = mm(mix_ref[r], low[:, own])
        for half in range(dright_ref.shape[0]):
            dright_ref[half] += right[:, half * LANES : (half + 1) * LANES]

    @pl.when(pl.program_id(0) == pl.num_programs(0) - 1)
    def _():
        gains_ref[...] = lane_sums(gainx_ref)
        outer_dim, count = right_ref.shape[0], left_ref.shape[0]
        d_left = jnp.zeros((count, LANES), F32)
        below = jnp.zeros((LANES - outer_dim, LANES), BF)
        for b in range(outer_dim):
            mixed = dmix_ref[pl.ds(b, count, stride=outer_dim), :].astype(BF)
            weight = outer_ref[pl.ds(b, outer_dim, stride=outer_dim), :].astype(BF)
            d_left += mm(mixed, jnp.concatenate([weight, below], axis=0), NT)
            gout_ref[pl.ds(b, outer_dim, stride=outer_dim), :] = mm(left_ref[...], mixed, TN)
        at = 0
        for half in range(dright_ref.shape[0]):
            spread_rows(packed_ref, at, dright_ref[half].astype(BF))
            at = at + outer_dim
        spread_rows(packed_ref, at, d_left.astype(BF))
        if carry_ref.shape[0] > 1:
            spread_rows(packed_ref, packed_ref.shape[1] - carry_ref.shape[0], carry_ref[...])
        in_rows, outer_rows = acc_ref.shape[0], gout_ref.shape[0]
        late_ref[:in_rows] = turn_blocks(acc_ref).astype(BF)
        late_ref[in_rows : in_rows + outer_rows] = gout_ref[...].astype(BF)
        spare = late_ref.shape[0] - in_rows - outer_rows
        late_ref[in_rows + outer_rows :] = jnp.zeros((spare, LANES), BF)


def last_kernel(xt_ref, fg_ref, ds_ref, gain_ref, w_ref, out_ref):
    for r in range(xt_ref.shape[0]):
        hat, inv = norm_rows(xt_ref[r].astype(F32))
        back = mm(w_ref[...], ds_ref[r])
        out_ref[r] = (fg_ref[r] + norm_rows_back(back * gain_ref[...], hat, inv)).T


def norm_lanes(values):
    centred = values - jnp.mean(values, axis=1, keepdims=True)
    inv = lax.rsqrt(jnp.mean(centred * centred, axis=1, keepdims=True) + EPS)
    return centred * inv, inv


def norm_lanes_back(scaled, hat, inv):
    return inv * (
        scaled
        - jnp.mean(scaled, axis=1, keepdims=True)
        - hat * jnp.mean(scaled * hat, axis=1, keepdims=True)
    )


def head_lanes(heads, width):
    depth = width // heads
    lane = lax.broadcasted_iota(jnp.int32, (heads, width), 1)
    head = lax.broadcasted_iota(jnp.int32, (heads, width), 0)
    return ((lane >= head * depth) & (lane < (head + 1) * depth)).astype(F32)


def rows_by_head(values, lanes):
    spread = values[:, None, :] * lanes[None]
    return spread.reshape(-1, values.shape[1])


def heads_by_row(values, lanes):
    spread = values[None] * lanes[:, None, :]
    return spread.reshape(-1, values.shape[1])


def crop_rows(residues):
    return pl.ds(pl.multiple_of(lax.axis_index("crop") * residues, residues), residues)


def attend_kernel(
    both_ref, own_ref, gain_ref, w_ref, bias_ref, mask_ref,
    norm_ref, gate_ref, qkv_ref, weights_ref, low_ref, gated_ref,
):
    width = own_ref.shape[1]
    residues = mask_ref.shape[2]
    heads = bias_ref.shape[1]
    rows = own_ref.shape[0]
    scale = 1.0 / (width // heads) ** 0.5
    hat, _ = norm_lanes(both_ref[:, :width].astype(F32))
    norm_ref[...] = (hat * gain_ref[...]).astype(BF)
    gate_ref[...] = jax.nn.sigmoid(mm(norm_ref[...], w_ref[:, 3 * width :]))
    qkv_ref[...] = mm(norm_ref[crop_rows(residues), :], w_ref[:, : 3 * width]).astype(BF)
    keys, values = qkv_ref[:, width : 2 * width], qkv_ref[:, 2 * width :]
    hat, _ = norm_lanes(own_ref[...].astype(F32))
    own = (hat * gain_ref[...]).astype(BF)
    query = mm(own, w_ref[:, :width]).astype(BF).astype(F32)
    gate = jax.nn.sigmoid(mm(own, w_ref[:, 3 * width :]))
    lanes = head_lanes(heads, width)
    query = rows_by_head(query, lanes).astype(BF)
    scores = mm(query, keys, NT) * scale + bias_ref[...].reshape(rows * heads, residues)
    mask = jnp.broadcast_to(mask_ref[...], bias_ref.shape).reshape(rows * heads, residues)
    scores = jnp.where(mask > 0.5, scores, -1000000000.0)
    powers = jnp.exp(scores - jnp.max(scores, axis=1, keepdims=True))
    weights = powers / jnp.sum(powers, axis=1, keepdims=True)
    weights_ref[...] = weights
    low = weights.astype(BF)
    low_ref[...] = low
    attn = mm(low, values).reshape(rows, heads, width)
    attn = jnp.sum(attn * lanes[None], axis=1)
    gated_ref[...] = jnp.broadcast_to((gate * attn).astype(BF)[None], gated_ref.shape)


def node_chunks(rows):
    size = min(rows, LANES)
    return [slice(k * size, (k + 1) * size) for k in range(rows // size)]


def gelu_parts(up):
    square = up * up
    curve = jnp.tanh(0.7978845608 * up * (1.0 + 0.044715 * square))
    half = 0.5 * (1.0 + curve)
    slope = half + up * (1.0 - curve * curve) * (0.3989422804 + 0.05351611220 * square)
    return up * half, slope


def node_kernel(
    both_ref, gated_ref, gn_ref, gs_ref, wo_ref, wu_ref, wd_ref, wn_ref, wr_ref,
    mid_ref, next_ref, proj_ref, right_ref, norm_ref,
):
    width = gated_ref.shape[1]
    residues = right_ref.shape[1]
    for rows in node_chunks(gated_ref.shape[0]):
        mid = both_ref[rows, :width].astype(F32) + mm(gated_ref[rows], wo_ref[...])
        mid_ref[rows] = mid
        hat, _ = norm_lanes(mid)
        act, _ = gelu_parts(mm((hat * gn_ref[...]).astype(BF), wu_ref[...]))
        following = mid + mm(act.astype(BF), wd_ref[...])
        next_ref[rows] = following
        hat, _ = norm_lanes(following)
        norm = (hat * gs_ref[...]).astype(BF)
        norm_ref[rows] = norm
        proj_ref[rows] = mm(norm, wn_ref[...]).astype(BF)
    right_ref[...] = mm(wr_ref[...], norm_ref[crop_rows(residues), :], NT).astype(BF)


def sublane_sum(values):
    return jnp.sum(values, axis=0, keepdims=True)


def node_back_kernel(
    outer_dim, got_ref, left_ref, both_ref, mid_ref, next_ref, gated_ref, gate_ref,
    gn_ref, gs_ref, wo_ref, wu_ref, wd_ref, wn_ref,
    gnode_ref, gd_ref, gu_ref, gout_ref, gains_ref, gainn_ref,
    dmid_ref, dattn_ref, dgate_ref, inner_ref,
    proj_ref, norm_ref, act_ref, low_ref, trans_ref, up_ref, midlow_ref,
):
    width = gated_ref.shape[1]
    devices = got_ref.shape[0] // 2
    halves = gated_ref.shape[0] // 2 // LANES
    at = 0
    for crop in range(2):
        for half in range(halves):
            total = jnp.zeros((outer_dim, LANES), F32)
            for d in range(devices):
                part = got_ref[crop * devices + d, half * outer_dim : (half + 1) * outer_dim]
                total += part.astype(F32)
            above = jnp.zeros((outer_dim, LANES), F32)
            below = jnp.zeros((LANES - 2 * outer_dim, LANES), F32)
            turned = jnp.concatenate([above, total, below], axis=0).T
            if left_ref.shape[0] == gated_ref.shape[0]:
                left = left_ref[at : at + LANES].astype(F32)
            else:
                rows = gated_ref.shape[0] // got_ref.shape[0]
                own = slice(halves * outer_dim, halves * outer_dim + rows)
                left = got_ref[at // rows : (at + LANES) // rows, own].astype(F32)
                left = left.reshape(LANES, LANES)
            proj_ref[at : at + LANES] = (turned + left).astype(BF)
            at = at + LANES
    gains, gainn = jnp.zeros((1, width), F32), jnp.zeros((1, width), F32)
    for rows in node_chunks(gated_ref.shape[0]):
        hat, inv = norm_lanes(next_ref[rows])
        norm_ref[rows] = (hat * gs_ref[...]).astype(BF)
        back = mm(proj_ref[rows], wn_ref[...], NT)
        gains += sublane_sum(back * hat)
        d_next = both_ref[rows, width:].astype(F32)
        d_next += norm_lanes_back(back * gs_ref[...], hat, inv)
        low = d_next.astype(BF)
        low_ref[rows] = low
        hat, inv = norm_lanes(mid_ref[rows])
        trans = (hat * gn_ref[...]).astype(BF)
        trans_ref[rows] = trans
        act, slope = gelu_parts(mm(trans, wu_ref[...]))
        act_ref[rows] = act.astype(BF)
        d_up = (mm(low, wd_ref[...], NT) * slope).astype(BF)
        up_ref[rows] = d_up
        back = mm(d_up, wu_ref[...], NT)
        gainn += sublane_sum(back * hat)
        d_mid = d_next + norm_lanes_back(back * gn_ref[...], hat, inv)
        dmid_ref[rows] = d_mid
        low = d_mid.astype(BF)
        midlow_ref[rows] = low
        d_gated = mm(low, wo_ref[...], NT)
        gate = gate_ref[rows]
        product = d_gated * gated_ref[rows].astype(F32)
        inner_ref[rows] = product
        dattn_ref[rows] = (d_gated * gate).astype(BF)
        dgate_ref[rows] = (product * (1.0 - gate)).astype(BF)
    gains_ref[...] = gains
    gainn_ref[...] = gainn
    gnode_ref[...] = mm(proj_ref[...], norm_ref[...], TN)[: 2 * outer_dim]
    gd_ref[...] = mm(act_ref[...], low_ref[...], TN)
    gu_ref[...] = mm(trans_ref[...], up_ref[...], TN)
    gout_ref[...] = mm(gated_ref[...], midlow_ref[...], TN)


def attend_back_kernel(
    own_ref, dattn_ref, inner_ref, qkv_ref, values_ref, weights_ref, column_ref, norm_ref,
    ds_ref, grad_ref, bias_ref,
):
    width = own_ref.shape[1]
    residues = qkv_ref.shape[0]
    rows, _, _ = norm_ref.shape
    heads = ds_ref.shape[0] // rows
    scale = 1.0 / (width // heads) ** 0.5
    lanes = head_lanes(heads, width)
    query, keys = qkv_ref[:, :width], qkv_ref[:, width : 2 * width]
    own = rows_by_head(own_ref[...].astype(F32), lanes).astype(BF)
    d_weights = mm(own, qkv_ref[:, 2 * width :], NT)
    weights = weights_ref[...]
    inner = jnp.sum(d_weights * weights, axis=1, keepdims=True)
    d_scores = (weights * (d_weights - inner)).astype(BF)
    ds_ref[...] = d_scores
    d_query = mm(d_scores, keys).reshape(rows, heads, width)
    d_query = jnp.sum(d_query * lanes[None], axis=1) * scale
    total = jnp.zeros(bias_ref.shape, F32)
    for r in range(rows):
        total += mm(d_scores[r * heads : (r + 1) * heads], norm_ref[r], NT)
    bias_ref[...] = total
    crop = crop_rows(residues)
    d_attn = dattn_ref[crop, :]
    spread = heads_by_row(values_ref[...].astype(F32), lanes).astype(BF)
    ones = heads_by_row(jnp.ones(values_ref.shape, F32), lanes).astype(BF)
    product = inner_ref[crop, :]
    high = product.astype(BF)
    rest = (product - high.astype(F32)).astype(BF)
    inner = mm(high, ones, NT) + mm(rest, ones, NT)
    column = column_ref[...]
    d_column = (column.astype(F32) * (mm(d_attn, spread, NT) - inner)).astype(BF)
    d_key = mm(d_column, query, TN).reshape(heads, rows, width)
    d_key = jnp.sum(d_key * lanes[:, None, :], axis=0) * scale
    d_value = mm(column, d_attn, TN).reshape(heads, rows, width)
    d_value = jnp.sum(d_value * lanes[:, None, :], axis=0)
    at = 0
    for part in (d_query, d_key, d_value):
        for half in range(width // LANES):
            grad_ref[at] = part[:, half * LANES : (half + 1) * LANES].astype(BF)
            at = at + 1


def layout_kernel(parts_ref, qkv_ref, bias_ref, gainx_ref, gains_ref, out_ref):
    total = jnp.zeros(parts_ref.shape[1:], F32)
    for d in range(parts_ref.shape[0]):
        total += parts_ref[d].astype(F32)
    at = 0
    for k in range(qkv_ref.shape[0]):
        spread_rows(out_ref, at, qkv_ref[k])
        at = at + qkv_ref.shape[1]
    spread_rows(out_ref, at, total.astype(BF))
    at = at + total.shape[0]
    small = [bias_ref[...], gainx_ref[...], gains_ref[...]]
    filled = sum(part.shape[0] for part in small)
    spare = out_ref.shape[1] - at - filled
    small = jnp.concatenate(small + [jnp.zeros((spare, LANES), F32)], axis=0)
    spread_rows(out_ref, at, small.astype(BF))


def adam_refs(master_ref, first_ref, second_ref, grad, outs, rate=0.1, decay=0.1):
    found = adam_step(master_ref[...], first_ref[...], second_ref[...], grad, rate, decay)
    for ref, value in zip(outs, found):
        ref[...] = value


def adam_kernel(count, layout, *refs):
    n_pair = 1 if layout else 3
    ins = 4 * count + 9 + n_pair
    outs, sums = refs[ins : ins + 3 * count + 9], refs[ins + 3 * count + 9 :]
    for k in range(count):
        master, first, second, grad = refs[4 * k : 4 * k + 4]
        adam_refs(master, first, second, grad[...], outs[3 * k : 3 * k + 3])
    olds, pair = refs[4 * count : 4 * count + 9], refs[4 * count + 9 : ins]

    @pl.when(pl.program_id(0) == 0)
    def _():
        if layout:
            start, part_up, part_z = layout
            values = unpack_pair(pair[0][:, start:].astype(F32), part_up, part_z)
        else:
            values = [ref[...] for ref in pair]
        for ref, value in zip(sums, values):
            ref[...] = value

    for k in range(3):
        height = olds[3 * k].shape[0]
        start = pl.multiple_of(pl.program_id(0) * height, height)
        at = 3 * (count + k)
        adam_refs(*olds[3 * k : 3 * k + 3], sums[k][pl.ds(start, height), :], outs[at : at + 3])


def across(rows):
    count = rows.shape[0] // LANES
    return jnp.concatenate([rows[k * LANES : (k + 1) * LANES] for k in range(count)], axis=1)


def unpack(take, layout):
    count, late_rows, in_rows, outer_rows, small_rows = layout
    blocks, at = [], 0
    for _ in range(6):
        blocks.append(take(at, at + count).reshape(-1, LANES))
        at = at + count
    late = take(at, at + late_rows)
    late = late.reshape((-1, 2) + late.shape[1:])
    late = jnp.concatenate([late[:, 0], late[:, 1]], axis=0).reshape(-1, LANES)
    at = at + late_rows
    small = jnp.sum(take(at, at + small_rows), axis=0)
    return blocks, (late[in_rows : in_rows + outer_rows], across(late[:in_rows])), small


def unpack_pair(pair, part_up, part_z):
    devices, half_rows, _ = pair.shape
    lower, upper = pair[: devices // 2], pair[devices // 2 :]
    over = 2 * part_up - half_rows
    g_up = jnp.concatenate([lower[:, part_up:], upper[:, :over]], axis=1).reshape(-1, LANES)
    g_down = lower[:, :part_up].reshape(-1, LANES)
    return upper[:, over : over + part_z].reshape(-1, LANES), across(g_up), g_down


def final_kernel(
    layout, dgate_ref, norm_ref, both_ref, dmid_ref, gain_ref, w_ref, gainn_ref, gains_ref, *refs
):
    n_got = 1 if layout else 9
    minor, refs = refs[:6], refs[6:]
    got, refs = refs[:n_got], refs[n_got:]
    olds, refs = refs[:9], refs[9:]
    news, minor_new, (dnode_ref, grad_ref, full_ref), sums = refs[:9], refs[9:15], refs[15:18], refs[18:]
    width = dmid_ref.shape[1]

    @pl.when(pl.program_id(0) == 0)
    def _():
        if layout:
            take = lambda start, stop: got[0][:, start:stop].astype(F32)
            blocks, grads, small = unpack(take, layout)
        else:
            values = [ref[...] for ref in got]
            blocks, grads, small = values[:6], values[6:8], values[8]
        for ref, grad in zip(sums[1:], grads):
            ref[...] = grad
        for k, block in enumerate(blocks):
            grad_ref[:, k * LANES : (k + 1) * LANES] = block.astype(BF)
        grad_ref[:, 3 * width :] = dgate_ref[...]
        sums[0][...] = mm(norm_ref[...], grad_ref[...], TN)
        total = jnp.zeros((1, width), F32)
        for rows in node_chunks(dmid_ref.shape[0]):
            hat, inv = norm_lanes(both_ref[rows, :width].astype(F32))
            back = mm(grad_ref[rows], w_ref[...], NT)
            total += sublane_sum(back * hat)
            full_ref[rows] = dmid_ref[rows] + norm_lanes_back(back * gain_ref[...], hat, inv)
        if dnode_ref.shape[0] == full_ref.shape[0]:
            dnode_ref[...] = full_ref[...]
        else:
            count = dnode_ref.shape[0]
            first = lax.axis_index("crop") * (full_ref.shape[0] // 2)
            first = pl.multiple_of(first + lax.axis_index("row") * count, count)
            dnode_ref[:, 0] = full_ref[pl.ds(first, count), :]
        heads = minor[0].shape[0]
        bias = small[:heads]
        adam_refs(*minor[:3], bias, minor_new[:3])
        spots = width // LANES
        rows_of = lambda line: [line[:, k * LANES : (k + 1) * LANES] for k in range(spots)]
        gain_b = minor[3][spots : spots + 1]
        weight = minor[0][...].astype(BF).astype(F32)
        grad_b = jnp.sum(weight * bias, axis=0, keepdims=True) / gain_b
        lines = rows_of(total) + [grad_b] + rows_of(gainn_ref[...]) + rows_of(gains_ref[...])
        rest = minor[3].shape[0] - len(lines)
        lines.append(small[heads : heads + rest])
        adam_refs(*minor[3:], jnp.concatenate(lines, axis=0), minor_new[3:], 1.0, 0.0)

    for k in range(3):
        height = olds[3 * k].shape[0]
        start = pl.multiple_of(pl.program_id(0) * height, height)
        adam_refs(*olds[3 * k : 3 * k + 3], sums[k][pl.ds(start, height), :], news[3 * k : 3 * k + 3])


def whole(shape):
    return pl.BlockSpec(shape, lambda i: (0,) * len(shape))


def by_row(step, shape):
    return pl.BlockSpec((step,) + shape, lambda i: (i,) + (0,) * len(shape))


def pair_call(kernel, steps, ins, outs, args, scratch=(), flops=0, moved=0, free=(), near=()):
    args = [
        arg if at in free else pltpu.with_memory_space_constraint(arg, pltpu.HBM)
        for at, arg in enumerate(args)
    ]
    shapes = [
        shape if at in near else pltpu.HBM(shape.shape, shape.dtype)
        for at, (_, shape) in enumerate(outs)
    ]
    return pl.pallas_call(
        kernel,
        grid=(steps,),
        in_specs=ins,
        out_specs=[spec for spec, _ in outs],
        out_shape=shapes,
        scratch_shapes=list(scratch),
        compiler_params=pltpu.CompilerParams(vmem_limit_bytes=48 * 1024 * 1024),
        cost_estimate=pl.CostEstimate(flops=flops, bytes_accessed=moved, transcendentals=0),
    )(*args)


def shards(row_devices, *arrays):
    (pair_feats, node_feats, chain_ids, out_grad, node_out_grad) = arrays[:5]
    masters, firsts, seconds = arrays[5:17], arrays[17:29], arrays[29:41]
    w_attend, w_pairbias, w_attout, w_nodeup, w_nodedown = masters[:5]
    w_node, w_outer, w_in, w_z, w_up, w_down, ln_gains = masters[5:]
    count, _, residues, width_z = pair_feats.shape
    width_s = node_feats.shape[2]
    heads = w_pairbias.shape[1]
    outer_dim = w_node.shape[1] // 2
    hidden = (w_in.shape[1] - width_z) // 8
    expand = w_up.shape[1]
    every = 2 * row_devices
    shape_of = jax.ShapeDtypeStruct
    cuts = [width_s, width_z, width_s, width_s, width_z, 2 * hidden, width_z]
    gains, at = [], 0
    for cut in cuts:
        gains.append(ln_gains[at : at + cut])
        at = at + cut
    gain_a, gain_b, gain_n, gain_s, gain_x, gain_t, gain_h = gains
    column = lambda gain: gain.reshape(-1, 1)
    line = lambda gain: gain.reshape(1, -1)
    nodes = 2 * residues
    crop_index, row_index = lax.axis_index("crop"), lax.axis_index("row")
    first_row = row_index * count
    chains = chain_ids[0]
    own_chain = lax.dynamic_slice_in_dim(chains, first_row, count, 0)
    same_own = own_chain[:, None] == chains[None, :]
    mask = same_own.astype(F32)[:, None, :]
    chain_col, chain_row = chains.reshape(-1, 1), chains.reshape(1, -1)

    att_wb, attout_wb = w_attend.astype(BF), w_attout.astype(BF)
    nodeup_wb, nodedown_wb, node_wb = w_nodeup.astype(BF), w_nodedown.astype(BF), w_node.astype(BF)
    outer_wb = w_outer.astype(BF).reshape(outer_dim, outer_dim * width_z)
    bias_wb, in_wb, z_wb = w_pairbias.astype(BF), w_in.astype(BF), w_z.astype(BF)
    up_wb, down_wb = w_up.astype(BF), w_down.astype(BF)
    bias_wt, in_wt, z_wt, up_wt, down_wt = bias_wb.T, in_wb.T, z_wb.T, up_wb.T, down_wb.T

    direct = count % 16 == 0
    step = next(size for size in (4, 2, 1) if count % size == 0)
    steps = count // step
    pairs = count * residues

    node_both = jnp.concatenate([node_feats[:, 0], node_out_grad[:, 0]], axis=1)
    pair_x = pair_feats[:, 0]
    xt, bias_norm, pair_bias = pair_call(
        bias_kernel, steps,
        [by_row(step, (residues, width_z)), whole((width_z, 1)), whole((heads, width_z))],
        [(by_row(step, (width_z, residues)), shape_of((count, width_z, residues), BF)),
         (by_row(step, (width_z, residues)), shape_of((count, width_z, residues), BF)),
         (by_row(step, (heads, residues)), shape_of((count, heads, residues), F32))],
        [pair_x, column(gain_b), bias_wt], free=(0, 1, 2), near=(2,),
        flops=2 * pairs * width_z * heads, moved=4 * pairs * width_z,
    )

    def own_rows(values):
        return lax.dynamic_slice_in_dim(values, crop_index * residues + first_row, count, 0)

    def single(kernel, outs, args, scratch=(), flops=0, far=(), apart=False):
        moved = sum(arg.size * 4 for arg in args)
        return pair_call(
            kernel, 1, [whole(arg.shape) for arg in args],
            [(whole(shape), shape_of(shape, kind)) for shape, kind in outs],
            args, scratch, flops, moved, (0,) if apart else range(len(args)),
            [at for at in range(len(outs)) if at not in far],
        )

    columns = [column(gain) for gain in (gain_x, gain_t, gain_h)]
    ready = [att_wb, attout_wb, nodeup_wb, nodedown_wb, mask]
    node_both, _ = gather_all(
        spread_over(node_both, row_devices), row_devices, [xt, pair_bias] + ready
    )
    node_both = node_both.reshape(nodes, 2 * width_s)
    square = (nodes, width_s)
    att_norm, gate_all, qkv_crop, att_weights, weights_low, gated_own = single(
        attend_kernel,
        [(square, BF), (square, F32), ((residues, 3 * width_s), BF),
         ((count * heads, residues), F32), ((count * heads, residues), BF),
         ((row_devices, count, width_s), BF)],
        [node_both, node_feats[:, 0], line(gain_a), att_wb, pair_bias, mask],
        flops=8 * nodes * width_s * width_s, far=(0, 1, 2, 3),
    )
    weights_cut = weights_low.reshape(count, heads, row_devices, count).transpose(2, 0, 1, 3)
    if direct:
        weights_cut = weights_cut.reshape(row_devices, -1, LANES)
    ready = [weights_cut, node_wb, outer_wb, in_wt, chain_col, columns[0]]
    gated, _ = gather_all(gated_own, row_devices, ready)
    gated = gated.reshape(nodes, width_s)

    node_mid, node_next, node_proj, right_t = single(
        node_kernel,
        [(square, F32), (square, F32), ((nodes, 2 * outer_dim), BF), ((outer_dim, residues), BF)],
        [node_both, gated, line(gain_n), line(gain_s), attout_wb, nodeup_wb, nodedown_wb, node_wb,
         node_wb[:, outer_dim:].T],
        scratch=[pltpu.VMEM(square, BF)], flops=18 * nodes * width_s * width_s, far=(0, 1),
    )
    node_out = own_rows(node_next).astype(BF)[:, None]
    left_vec = own_rows(node_proj[:, :outer_dim])
    outer_mix = mm(left_vec, outer_wb).astype(BF).reshape(count, outer_dim, width_z)

    share = hidden // row_devices
    dims = (share, count) if direct else None

    def sent_block(tiles, extra=0):
        if direct:
            shape = (row_devices, tiles * share * count + extra, LANES)
            return whole(shape), shape_of(shape, BF)
        return by_row(step, (tiles, hidden, LANES)), shape_of((count, tiles, hidden, LANES), BF)

    def stage(tiles):
        return [pltpu.VMEM((tiles * hidden * count, LANES), F32)] if direct else []

    def swap(block):
        return lax.all_to_all(block, "row", split_axis=0, concat_axis=0, tiled=True)

    def to_channels(block):
        if direct:
            return swap(block)
        tiles = block.shape[1]
        cut = block.reshape(count, tiles, row_devices, share, LANES)
        sent = swap(cut.transpose(2, 1, 3, 0, 4))
        return sent.transpose(1, 2, 0, 3, 4).reshape(1, tiles, share, residues, LANES)

    def to_rows(block):
        if direct:
            return swap(block)
        tiles = block.shape[1]
        cut = block.reshape(tiles, share, row_devices, count, LANES)
        got = swap(cut.transpose(2, 0, 1, 3, 4))
        return got.transpose(3, 1, 0, 2, 4).reshape(count, tiles, hidden, LANES)

    def tri_block(tiles, extra=0):
        if direct:
            return sent_block(tiles, extra)
        shape = (1, tiles, share, residues, LANES)
        spec = pl.BlockSpec((1, tiles, 1, residues, LANES), lambda i: (0, 0, i, 0, 0))
        return spec, shape_of(shape, BF)

    ride = weights_cut if direct else jnp.zeros((1, 1, LANES), BF)
    extra = ride.shape[1]
    first_sum, acts_own = pair_call(
        functools.partial(first_kernel, share, count), steps,
        [by_row(step, (width_z, residues)), by_row(step, (outer_dim, width_z)),
         whole((outer_dim, residues)), by_row(step, (1, residues)), whole((width_z, 1)),
         whole(in_wt.shape), whole(ride.shape)],
        [(by_row(step, (width_z, residues)), shape_of((count, width_z, residues), F32)),
         sent_block(6, extra)],
        [xt, outer_mix, right_t, mask, column(gain_x), in_wt, ride],
        scratch=stage(6),
        flops=16 * pairs * width_z * hidden, moved=12 * pairs * width_z,
    )

    tri_steps = lambda channels: channels // 2 if direct and channels % 2 == 0 else channels
    chain_specs = [whole((residues, 1)), whole((1, residues))]
    product = 2 * share * residues**3
    ready = [in_wb, z_wb, up_wb, down_wb, z_wt, up_wt, down_wt] + columns
    acts = after(to_channels(acts_own), ready)
    weights_col = acts[:, 6 * share * count :] if direct else swap(weights_cut)
    weights_col = weights_col.reshape(residues, heads * count)
    (tri,) = pair_call(
        functools.partial(tri_kernel, dims), tri_steps(share), chain_specs + [tri_block(6, extra)[0]],
        [tri_block(3)], [chain_col, chain_row, acts], free=(2,),
        flops=2 * product, moved=share * residues * 9 * 256,
    )
    tri_rows = to_rows(tri)

    slab = by_row(step, (width_z, residues))
    second_args = [
        (by_row(step, (width_z, residues)), first_sum),
        (sent_block(3)[0], tri_rows),
        (by_row(step, (residues, width_z)), out_grad[:, 0]),
        (by_row(step, (1, residues)), mask),
    ]
    second_args += [
        (whole(v.shape), v)
        for v in (
            column(gain_x), column(gain_t), column(gain_h),
            in_wt[8 * hidden :], z_wt, z_wb, up_wt, up_wb, down_wt, down_wb,
        )
    ]
    part_up, part_z = expand // row_devices, 2 * hidden // row_devices
    half_rows = part_up + part_up // 2
    carried = 2 * half_rows if direct else 0
    acc_shapes = [
        (expand, width_z), (expand, width_z), (2 * hidden, width_z),
        ((2 * hidden + width_z) // LANES, LANES),
    ]
    pair_out, d_second, d_logit, dtri_own, g_down, g_up_t, g_z, gains_th = pair_call(
        functools.partial(second_kernel, share, count), steps,
        [spec for spec, _ in second_args],
        [(by_row(step, (residues, width_z)), shape_of((count, residues, width_z), BF)),
         (slab, shape_of((count, width_z, residues), F32)),
         (slab, shape_of((count, width_z, residues), BF)),
         sent_block(3, carried)]
        + [(whole(s), shape_of(s, F32)) for s in acc_shapes],
        [arg for _, arg in second_args], free=(1,),
        scratch=[pltpu.VMEM((2 * hidden, residues), F32), pltpu.VMEM((width_z, residues), F32)]
        + stage(3) + stage(3),
        flops=12 * pairs * width_z * expand, moved=20 * pairs * width_z,
    )

    dtri = to_channels(dtri_own)
    if direct:
        grad_parts = dtri[:, 3 * share * count :]
    else:
        turned = g_up_t.reshape(-1, LANES, LANES).transpose(0, 2, 1)
        parts = [g.reshape(row_devices, -1, LANES) for g in (g_down, turned, g_z)]
        spare = jnp.zeros((row_devices, part_up - part_z, LANES), F32)
        grad_parts = swap(jnp.concatenate(parts + [spare], axis=1).astype(BF))
    row_sum = jnp.sum(grad_parts.astype(F32), axis=0)
    lower, upper = row_sum[:half_rows], row_sum[half_rows:]
    low_crop = crop_index == 0
    theirs = lax.ppermute(jnp.where(low_crop, upper, lower), "crop", [(0, 1), (1, 0)])
    pair_own = (jnp.where(low_crop, lower, upper) + theirs).astype(BF)
    (dacts,) = pair_call(
        functools.partial(tri_back_kernel, dims), tri_steps(share),
        chain_specs + [tri_block(6, extra)[0], tri_block(3, carried)[0]],
        [tri_block(6)], [chain_col, chain_row, acts, dtri], free=(2,),
        flops=4 * product, moved=share * residues * 15 * 256,
    )
    dacts_rows = after(to_rows(dacts), pair_own)

    right_rows = residues // LANES * outer_dim
    left_rows = -(-count // 16) * 16
    carry = pair_own if direct else jnp.zeros((1, LANES), BF)
    packed_rows = right_rows + left_rows + (half_rows if direct else 0)
    in_rows, outer_rows = in_wt.shape[0], w_outer.shape[0]
    late_rows = -(-(in_rows + outer_rows) // (every * 16)) * every * 16
    first_grad, packed, late, gains_x = pair_call(
        functools.partial(third_kernel, share, count), steps,
        [slab, sent_block(6)[0], slab, slab, by_row(step, (1, residues)),
         by_row(step, (outer_dim, width_z)), whole((outer_dim, residues)), whole((width_z, 1)),
         whole(in_wt.shape), whole(in_wb.shape), whole(left_vec.shape), whole(w_outer.shape),
         whole(carry.shape)],
        [(slab, shape_of((count, width_z, residues), F32)),
         (whole((row_devices, packed_rows, LANES)),
          shape_of((row_devices, packed_rows, LANES), BF)),
         (whole((late_rows, LANES)), shape_of((late_rows, LANES), BF)),
         (whole((width_z // LANES, LANES)), shape_of((width_z // LANES, LANES), F32))],
        [first_sum, dacts_rows, d_second, d_logit, mask, outer_mix, right_t, columns[0],
         in_wt, in_wb, left_vec, w_outer, carry],
        free=(1,),
        scratch=[pltpu.VMEM((width_z, residues), F32), pltpu.VMEM((9 * hidden, step * residues), BF),
                 pltpu.VMEM(in_wt.shape, F32), pltpu.VMEM((count * outer_dim, LANES), F32),
                 pltpu.VMEM((residues // LANES, outer_dim, LANES), F32),
                 pltpu.VMEM(w_outer.shape, F32)] + stage(6),
        flops=54 * pairs * width_z * hidden, moved=20 * pairs * width_z,
    )
    late = late.reshape(2, late_rows // 2, LANES)
    odd = row_index % 2 == 1
    theirs = core_exchange(jnp.where(odd, late[0], late[1]), row_devices)
    late = jnp.where(odd, late[1], late[0]).astype(F32) + theirs.astype(F32)
    late = late.astype(BF).reshape(row_devices, -1, LANES)
    got, first_got = gather_all(packed, row_devices, late)
    late_parts = same_core_exchange(after(late, first_got), row_devices)
    left_all = left_vec
    if not direct:
        left_all = got[:, right_rows : right_rows + count].reshape(nodes, LANES)

    wide_node = jnp.pad(node_wb, ((0, 0), (0, LANES - 2 * outer_dim)))
    tall, low_square = (nodes, w_nodeup.shape[1]), pltpu.VMEM(square, BF)
    (g_node, g_nodedown, g_nodeup, g_attout, gain_s_grad, gain_n_grad,
     grad_mid, d_attn, d_gate, inner) = single(
        functools.partial(node_back_kernel, outer_dim),
        [((2 * outer_dim, width_s), F32), (w_nodedown.shape, F32), (w_nodeup.shape, F32),
         (w_attout.shape, F32), ((1, width_s), F32), ((1, width_s), F32),
         (square, F32), (square, BF), (square, BF), (square, F32)],
        [got, left_all, node_both, node_mid, node_next, gated, gate_all,
         line(gain_n), line(gain_s), attout_wb, nodeup_wb, nodedown_wb, wide_node],
        scratch=[pltpu.VMEM((nodes, LANES), BF), low_square, pltpu.VMEM(tall, BF), low_square,
                 low_square, pltpu.VMEM(tall, BF), low_square],
        flops=50 * nodes * width_s * width_s, far=(0, 1, 2, 3, 4, 5, 6, 8), apart=True,
    )

    values_own = lax.dynamic_slice(qkv_crop, (first_row, 2 * width_s), (count, width_s))
    score_grad, qkv_grad, g_bias_t = single(
        attend_back_kernel,
        [((count * heads, residues), BF), ((3 * width_s // LANES, count, LANES), BF),
         ((heads, width_z), F32)],
        [own_rows(d_attn), d_attn, inner, qkv_crop, values_own, att_weights, weights_col,
         bias_norm],
        flops=12 * count * heads * residues * width_s,
    )

    qkv_rows, share_rows = qkv_grad.size // LANES, late_parts.shape[1]
    small_rows = heads + gains_x.shape[0] + gains_th.shape[0]
    small_rows = small_rows + -small_rows % 16
    layout = (count, share_rows, in_rows, outer_rows, small_rows)
    last_shape = (row_devices, qkv_rows + share_rows + small_rows, LANES)
    pieces = [late_parts, qkv_grad, g_bias_t, gains_x, gains_th]
    if direct:
        (last_own,) = single(layout_kernel, [(last_shape, BF)], pieces)
    else:
        small = jnp.concatenate(pieces[2:])
        small = jnp.pad(small, ((0, small_rows - small.shape[0]), (0, 0)))
        late_own = jnp.sum(late_parts.astype(F32), axis=0)
        last_own = [qkv_grad.reshape(-1, LANES).astype(F32), late_own, small]
        last_own = spread_over(jnp.concatenate(last_own).astype(BF), row_devices)

    (pair_grad,) = pair_call(
        last_kernel, steps,
        [slab, slab, by_row(step, (heads, residues)), whole((width_z, 1)), whole((width_z, heads))],
        [(by_row(step, (residues, width_z)), shape_of((count, residues, width_z), F32))],
        [xt, first_grad, score_grad.reshape(count, heads, residues), column(gain_b), bias_wb],
        flops=4 * pairs * width_z * heads, moved=10 * pairs * width_z,
    )

    parts = 2
    split = lambda k: pl.BlockSpec((olds[k].shape[0] // parts, olds[k].shape[1]), lambda i: (i, 0))
    updated = {}

    early = {2: g_attout, 3: g_nodeup, 4: g_nodedown, 5: g_node}
    turned = lambda k, value: value.T if k == 5 else value
    specs, args, outs = [], [], []
    for k, grad in early.items():
        spec = pl.BlockSpec((grad.shape[0] // parts, grad.shape[1]), lambda i: (i, 0))
        specs += [spec] * 4
        args += [turned(k, old[k]) for old in (masters, firsts, seconds)] + [grad]
        outs += [(spec, shape_of(grad.shape, F32))] * 3
    pair_keys = (8, 9, 10)
    for k in pair_keys:
        height, width = masters[k].shape
        spec = pl.BlockSpec((height // parts, width), lambda i: (i, 0))
        specs += [spec] * 3
        args += [masters[k], firsts[k], seconds[k]]
        outs += [(spec, shape_of((height, width), F32))] * 3
    if direct:
        pair_got, pair_layout = [got], (right_rows + left_rows, part_up, part_z)
    else:
        pair_all, _ = gather_all(spread_over(pair_own, row_devices), row_devices)
        pair_got, pair_layout = list(unpack_pair(pair_all.astype(F32), part_up, part_z)), None
    specs += [whole(arg.shape) for arg in pair_got]
    args += pair_got
    found = pair_call(
        functools.partial(adam_kernel, len(early), pair_layout), parts, specs, outs, args,
        scratch=[pltpu.VMEM(masters[k].shape, F32) for k in pair_keys],
        moved=sum(7 * arg.size for arg in args),
    )
    beside = (pair_grad, found[0], node_out)
    last, _ = gather_all(last_own, row_devices, beside)
    for at, k in enumerate(early):
        updated[k] = [turned(k, value) for value in found[3 * at : 3 * at + 3]]
    for at, k in enumerate(pair_keys, len(early)):
        updated[k] = found[3 * at : 3 * at + 3]

    late_keys = (0, 6, 7)
    got_last = [last]
    if not direct:
        blocks, sums, small = unpack(lambda a, b: last[:, a:b].astype(F32), layout)
        got_last = blocks + list(sums) + [small]
    node_shape = (count, 1, width_s) if direct else square
    minor = [old[1].T for old in (masters, firsts, seconds)]
    minor += [old[11].reshape(-1, LANES) for old in (masters, firsts, seconds)]
    fixed = [d_gate, att_norm, node_both, grad_mid, line(gain_a), att_wb, gain_n_grad, gain_s_grad]
    fixed = fixed + minor + got_last
    olds, specs = [], [whole(arg.shape) for arg in fixed]
    for k in late_keys:
        olds += [masters[k], firsts[k], seconds[k]]
    blocked = [split(k) for k in range(len(olds))]
    found = pair_call(
        functools.partial(final_kernel, layout if direct else None), parts, specs + blocked,
        [(spec, shape_of(old.shape, F32)) for spec, old in zip(blocked, olds)]
        + [(whole(value.shape), shape_of(value.shape, F32)) for value in minor]
        + [(whole(node_shape), shape_of(node_shape, F32))],
        fixed + olds,
        scratch=[pltpu.VMEM((nodes, 4 * width_s), BF), pltpu.VMEM(square, F32)]
        + [pltpu.VMEM(masters[k].shape, F32) for k in late_keys],
        flops=16 * nodes * width_s * width_s, moved=sum(7 * old.size for old in olds),
    )
    for at, k in enumerate(late_keys):
        updated[k] = found[3 * at : 3 * at + 3]
    updated[1] = [value.T for value in found[9:12]]
    updated[11] = [value.reshape(-1) for value in found[12:15]]
    node_grad = found[15] if direct else own_rows(found[15])[:, None]
    results = [pair_out[:, None], node_out, pair_grad[:, None], node_grad]
    for k in range(12):
        results.extend(updated[k])
    return tuple(results)


def solution(mesh):
    rows4, rows3 = P("row", "crop", None, None), P("row", "crop", None)
    return jax.shard_map(
        functools.partial(shards, mesh.shape["row"]),
        mesh=mesh,
        in_specs=(rows4, rows3, P("crop", None), rows4, rows3) + (P(),) * 36,
        out_specs=(rows4, rows3, rows4, rows3) + (P(),) * 36,
        check_vma=False,
    )
```

```python
import functools
import jax
import jax.numpy as jnp
from jax import lax
from jax.experimental import pallas as pl
from jax.experimental.pallas import tpu as pltpu
from jax.sharding import PartitionSpec as P

ADAM_STEP = 4
EPS = 1e-05
BF = jnp.bfloat16
F32 = jnp.float32
LANES = 128
HALF = 64
BOTH = ("crop", "row")
NN = (((1,), (0,)), ((), ()))
NT = (((1,), (1,)), ((), ()))
TN = (((0,), (0,)), ((), ()))


def mm(left, right, dims=NN):
    return lax.dot_general(left, right, dims, preferred_element_type=F32)


def adam_step(master, first_old, second_old, grad_total, rate, decay):
    first_new = 0.9 * first_old + 0.1 * grad_total
    second_new = 0.999 * second_old + 0.001 * grad_total * grad_total
    first_hat = first_new / (1.0 - 0.9**ADAM_STEP)
    second_hat = second_new / (1.0 - 0.999**ADAM_STEP)
    master_new = master - rate * (first_hat / (jnp.sqrt(second_hat) + 1e-08) + decay * master)
    return (first_new, second_new, master_new)


def after(value, event):
    return lax.optimization_barrier((value, event))[0]


def spread_over(part, row_devices):
    return jnp.broadcast_to(part[None], (row_devices,) + part.shape)


def same_core_exchange(block, row_devices):
    groups = [[d for d in range(2 * row_devices) if d % 2 == k] for k in range(2)]
    return lax.all_to_all(
        block, BOTH, split_axis=0, concat_axis=0, tiled=True, axis_index_groups=groups
    )


def core_exchange(block, row_devices):
    return lax.ppermute(block, "row", [(d, d ^ 1) for d in range(row_devices)])


def gather_all(spread, row_devices, during=()):
    every = 2 * row_devices
    first = same_core_exchange(spread, row_devices)
    got = after(first, during)
    other = core_exchange(got, row_devices)
    odd = lax.axis_index("row") % 2 == 1
    pair = [jnp.where(odd, other, got), jnp.where(odd, got, other)]
    return jnp.stack(pair, axis=1).reshape((every,) + spread.shape[1:]), first


def norm_rows(values):
    centred = values - jnp.mean(values, axis=0, keepdims=True)
    inv = lax.rsqrt(jnp.mean(centred * centred, axis=0, keepdims=True) + EPS)
    return centred * inv, inv


def norm_rows_back(scaled, hat, inv):
    return inv * (
        scaled
        - jnp.mean(scaled, axis=0, keepdims=True)
        - hat * jnp.mean(scaled * hat, axis=0, keepdims=True)
    )


def turn(values):
    return pltpu.roll(values, HALF, values.ndim - 1)


def low_lanes(shape):
    return lax.broadcasted_iota(jnp.int32, shape, len(shape) - 1) < HALF


def fold_pair(first, second):
    low = low_lanes((first.shape[0], LANES))
    f_lo, f_hi = first[:, :LANES], first[:, LANES:]
    s_lo, s_hi = second[:, :LANES], second[:, LANES:]
    f_turn, s_turn = turn(f_hi), turn(s_hi)
    main_f = f_lo + jnp.where(low, f_turn, 0.0)
    main_s = s_lo + jnp.where(low, s_turn, 0.0)
    return main_f, main_s, jnp.where(low, f_hi, s_turn)


def unfold_pair(main_f, main_s, tail):
    low = low_lanes(tail.shape)
    first = jnp.concatenate([main_f, jnp.where(low, tail, turn(main_f))], axis=1)
    second = jnp.concatenate([main_s, jnp.where(low, turn(tail), turn(main_s))], axis=1)
    return first, second


def put_tile(stage_ref, tile, row, rows, values):
    high = values.shape[0]
    stage_ref[pl.ds(tile * high * rows + row, high, stride=rows), :] = values


def get_tile(stage_ref, tile, row, rows, high):
    return stage_ref[pl.ds(tile * high * rows + row, high, stride=rows), :]


def ship(stage_ref, send_ref, tiles, share, rows):
    devices = send_ref.shape[0]
    span = share * rows
    for t in range(tiles):
        block = stage_ref[t * devices * span : (t + 1) * devices * span]
        send_ref[:, t * span : (t + 1) * span] = block.reshape(devices, span, LANES).astype(BF)


def unship(got_ref, stage_ref, tiles, share, rows):
    devices = got_ref.shape[0]
    span = share * rows
    for t in range(tiles):
        block = got_ref[:, t * span : (t + 1) * span].astype(F32)
        stage_ref[t * devices * span : (t + 1) * devices * span] = block.reshape(-1, LANES)


def lane_sums(ref):
    count = ref.shape[0] // LANES
    cut = [ref[k * LANES : (k + 1) * LANES].T for k in range(count)]
    return jnp.concatenate([jnp.sum(part, axis=0, keepdims=True) for part in cut], axis=0)


def spread_rows(ref, at, rows):
    shape = (ref.shape[0],) + rows.shape
    ref[:, at : at + rows.shape[0]] = jnp.broadcast_to(rows[None], shape)


def turn_blocks(ref):
    count = ref.shape[0] // LANES
    return jnp.concatenate([ref[k * LANES : (k + 1) * LANES].T for k in range(count)], axis=0)


def bias_kernel(x_ref, gain_ref, weight_ref, xt_ref, norm_ref, bias_ref):
    for r in range(x_ref.shape[0]):
        xt = x_ref[r].astype(F32).T
        xt_ref[r] = xt.astype(BF)
        hat, _ = norm_rows(xt)
        norm = (hat * gain_ref[...]).astype(BF)
        norm_ref[r] = norm
        bias_ref[r] = mm(weight_ref[...], norm)


def first_kernel(
    share, rows, xt_ref, mix_ref, right_ref, mask_ref, gain_ref, weight_ref, ride_ref,
    sum_ref, send_ref, *stage,
):
    hidden = weight_ref.shape[0] // 9
    step, _, residues = xt_ref.shape
    columns = [slice(r * residues, (r + 1) * residues) for r in range(step)]
    mixes = [mm(mix_ref[r], right_ref[...], TN) for r in range(step)]
    total = jnp.concatenate([xt_ref[r].astype(F32) + mixes[r] for r in range(step)], axis=1)
    for r in range(step):
        sum_ref[r] = total[:, columns[r]]
    hat, _ = norm_rows(total)
    norm = (hat * gain_ref[...]).astype(BF)
    mask = jnp.concatenate([mask_ref[r] for r in range(step)], axis=1)
    for pair in range(2):
        acts = []
        for block in (2 * pair, 2 * pair + 1):
            value = mm(weight_ref[block * hidden : (block + 1) * hidden], norm)
            gate = mm(weight_ref[(block + 4) * hidden : (block + 5) * hidden], norm)
            acts.append(jax.nn.sigmoid(gate) * value * mask)
        for r in range(step):
            row = pl.program_id(0) * step + r
            tiles = fold_pair(*(act[:, columns[r]] for act in acts))
            for t in range(3):
                if stage:
                    put_tile(stage[0], 3 * pair + t, row, rows, tiles[t])
                else:
                    send_ref[r, 3 * pair + t] = tiles[t].astype(BF)
    if stage:

        @pl.when(pl.program_id(0) == pl.num_programs(0) - 1)
        def _():
            ship(stage[0], send_ref, 6, share, rows)
            send_ref[:, 6 * share * rows :] = ride_ref[...]


def chain_mask(col_ref, row_ref):
    return col_ref[...] == row_ref[...]


def flat_rows(ref, tile, spot):
    block = ref[:, spot(tile)] if spot else ref[:, tile, 0]
    return block.reshape(-1, block.shape[-1])


def slot_operands(ref, pair, spot):
    main_f, main_s, tail = (flat_rows(ref, 3 * pair + t, spot).astype(F32) for t in range(3))
    low = low_lanes(tail.shape)
    zero = jnp.zeros_like(tail)
    first = jnp.concatenate([main_f, jnp.where(low, tail, zero)], axis=1).astype(BF)
    second = jnp.concatenate([main_s, jnp.where(low, turn(tail), zero)], axis=1).astype(BF)
    return first, second


def channel_spots(dims):
    if not dims:
        return [None]
    share, rows = dims
    each = share // pl.num_programs(0)
    first = pl.program_id(0) * each

    def spot_of(channel):
        return lambda tile: pl.ds(pl.multiple_of((tile * share + channel) * rows, rows), rows)

    return [spot_of(first + k) for k in range(each)]


def raw_columns(slots, same):
    values = slots.astype(F32)
    main, tail = values[:, :LANES], values[:, LANES:]
    wide = jnp.concatenate(
        [main, jnp.where(low_lanes(tail.shape), tail, turn(main))], axis=1
    )
    return jnp.where(same, wide, 0.0).astype(BF)


def store_tiles(out_ref, pair, k, tiles):
    for t in range(3):
        block = tiles[t].astype(BF).reshape(out_ref.shape[0], -1, LANES)
        out_ref[:, 3 * pair + t, k] = block


def tri_kernel(dims, col_ref, row_ref, acts_ref, out_ref):
    same = chain_mask(col_ref, row_ref)
    for k, spot in enumerate(channel_spots(dims)):
        left_out, right_out = slot_operands(acts_ref, 0, spot)
        left_in, right_in = slot_operands(acts_ref, 1, spot)
        outgoing = jnp.where(same, mm(left_out, right_out, NT), 0.0)
        incoming = mm(raw_columns(left_in, same), right_in, TN)
        low = low_lanes((outgoing.shape[0], LANES))
        o_lo, o_hi = outgoing[:, :LANES], outgoing[:, LANES:]
        main_o = o_lo + jnp.where(low, turn(o_hi), 0.0)
        tail = jnp.where(low, o_hi, turn(incoming[:, LANES:]))
        store_tiles(out_ref, 0, k, (main_o, incoming[:, :LANES], tail))


def tri_back_kernel(dims, col_ref, row_ref, acts_ref, grad_ref, out_ref):
    same = chain_mask(col_ref, row_ref)
    for k, spot in enumerate(channel_spots(dims)):
        left_out, right_out = slot_operands(acts_ref, 0, spot)
        left_in, right_in = slot_operands(acts_ref, 1, spot)
        grad_out, grad_in = slot_operands(grad_ref, 0, spot)
        raw_out = raw_columns(grad_out, same)
        d_left = mm(raw_out, right_out)
        d_right = mm(raw_out, left_out, TN)
        low = low_lanes((d_left.shape[0], LANES))
        tail = jnp.where(low, d_left[:, LANES:], turn(d_right[:, LANES:]))
        store_tiles(out_ref, 0, k, (d_left[:, :LANES], d_right[:, :LANES], tail))
        d_left = jnp.where(same, mm(right_in, grad_in, NT), 0.0)
        d_right = mm(raw_columns(left_in, same), grad_in)
        l_lo, l_hi = d_left[:, :LANES], d_left[:, LANES:]
        main_l = l_lo + jnp.where(low, turn(l_hi), 0.0)
        tail = jnp.where(low, l_hi, turn(d_right[:, LANES:]))
        store_tiles(out_ref, 1, k, (main_l, d_right[:, :LANES], tail))


def second_kernel(
    share, rows, sum_ref, tri_ref, grad_ref, mask_ref, gx_ref, gt_ref, gh_ref,
    wgate_ref, wzt_ref, wz_ref, wut_ref, wu_ref, wdt_ref, wd_ref,
    out_ref, ds_ref, dlogit_ref, send_ref, gd_ref, gu_ref, gz_ref, gains_ref, gaint_ref, gainh_ref,
    *stage,
):
    @pl.when(pl.program_id(0) == 0)
    def _():
        for acc in (gd_ref, gu_ref, gz_ref, gaint_ref, gainh_ref):
            acc[...] = jnp.zeros_like(acc)
        if stage:
            unship(tri_ref, stage[0], 3, share, rows)

    step, _, residues = sum_ref.shape
    joined = lambda values: jnp.concatenate(list(values), axis=1)
    total = joined(sum_ref[r] for r in range(step))
    mask = joined(mask_ref[r] for r in range(step))
    hat_x, _ = norm_rows(total)
    norm = (hat_x * gx_ref[...]).astype(BF)
    out_gate = jax.nn.sigmoid(mm(wgate_ref[...], norm))
    combined = []
    for r in range(step):
        row = pl.program_id(0) * step + r
        if stage:
            tiles = [get_tile(stage[0], t, row, rows, total.shape[0]) for t in range(3)]
        else:
            tiles = [tri_ref[r, t].astype(F32) for t in range(3)]
        combined.append(jnp.concatenate(unfold_pair(*tiles), axis=0))
    hat_t, inv_t = norm_rows(joined(combined))
    tri_norm = (hat_t * gt_ref[...]).astype(BF)
    tri_proj = mm(wzt_ref[...], tri_norm)
    second = total + out_gate * tri_proj * mask
    hat_h, inv_h = norm_rows(second)
    trans_in = (hat_h * gh_ref[...]).astype(BF)
    act, slope = gelu_parts(mm(wut_ref[...], trans_in))
    act = act.astype(BF)
    result = second + mm(wdt_ref[...], act)
    for r in range(step):
        out_ref[r] = result[:, r * residues : (r + 1) * residues].T.astype(BF)
    grad_low = joined(grad_ref[r].astype(F32).T.astype(BF) for r in range(step))
    gd_ref[...] += mm(act, grad_low, NT)
    d_up = (mm(wd_ref[...], grad_low) * slope).astype(BF)
    gu_ref[...] += mm(d_up, trans_in, NT)
    back = mm(wu_ref[...], d_up)
    prod = back * hat_h
    gainh_ref[...] += sum(prod[:, r * residues : (r + 1) * residues] for r in range(step))
    d_second = grad_low.astype(F32) + norm_rows_back(back * gh_ref[...], hat_h, inv_h)
    gated = d_second * mask * out_gate
    d_tri = gated.astype(BF)
    d_logit = (gated * tri_proj * (1.0 - out_gate)).astype(BF)
    for r in range(step):
        ds_ref[r] = d_second[:, r * residues : (r + 1) * residues]
        dlogit_ref[r] = d_logit[:, r * residues : (r + 1) * residues]
    gz_ref[...] += mm(tri_norm, d_tri, NT)
    back = mm(wz_ref[...], d_tri)
    prod = back * hat_t
    gaint_ref[...] += sum(prod[:, r * residues : (r + 1) * residues] for r in range(step))
    comb = norm_rows_back(back * gt_ref[...], hat_t, inv_t)
    hidden = comb.shape[0] // 2
    for r in range(step):
        row = pl.program_id(0) * step + r
        own = comb[:, r * residues : (r + 1) * residues]
        tiles = fold_pair(own[:hidden], own[hidden:])
        for t in range(3):
            if stage:
                put_tile(stage[1], t, row, rows, tiles[t])
            else:
                send_ref[r, t] = tiles[t].astype(BF)

    @pl.when(pl.program_id(0) == pl.num_programs(0) - 1)
    def _():
        gains_ref[...] = jnp.concatenate([lane_sums(gaint_ref), lane_sums(gainh_ref)], axis=0)
        if stage:
            ship(stage[1], send_ref, 3, share, rows)
            devices = send_ref.shape[0]
            at = 3 * share * rows
            for acc, turned in ((gd_ref, False), (gu_ref, True), (gz_ref, False)):
                part = acc.shape[0] // devices
                block = turn_blocks(acc) if turned else acc[...]
                send_ref[:, at : at + part] = block.reshape(devices, part, LANES).astype(BF)
                at = at + part


def third_kernel(
    share, rows, sum_ref, acts_ref, ds_ref, dlogit_ref, mask_ref, mix_ref, right_ref, gx_ref,
    wt_ref, w_ref, left_ref, outer_ref, carry_ref,
    fg_ref, packed_ref, late_ref, gains_ref,
    gainx_ref, dproj_ref, acc_ref, dmix_ref, dright_ref, gout_ref, *stage,
):
    @pl.when(pl.program_id(0) == 0)
    def _():
        for acc in (dright_ref, acc_ref, gainx_ref):
            acc[...] = jnp.zeros_like(acc)
        if stage:
            unship(acts_ref, stage[0], 6, share, rows)

    hidden = wt_ref.shape[0] // 9
    step, _, residues = sum_ref.shape
    joined = lambda ref: jnp.concatenate([ref[r] for r in range(step)], axis=1)
    hat, inv = norm_rows(joined(sum_ref))
    norm = (hat * gx_ref[...]).astype(BF)
    mask = joined(mask_ref)
    for pair in range(2):
        unfolded = []
        for r in range(step):
            row = pl.program_id(0) * step + r
            tiles = range(3 * pair, 3 * pair + 3)
            if stage:
                tiles = [get_tile(stage[0], t, row, rows, hidden) for t in tiles]
            else:
                tiles = [acts_ref[r, t].astype(F32) for t in tiles]
            unfolded.append(unfold_pair(*tiles))
        for side in range(2):
            block = 2 * pair + side
            value = mm(wt_ref[block * hidden : (block + 1) * hidden], norm)
            gate = mm(wt_ref[(block + 4) * hidden : (block + 5) * hidden], norm)
            sig = jax.nn.sigmoid(gate)
            d_value = jnp.concatenate([both[side] for both in unfolded], axis=1) * mask * sig
            d_gate = d_value * value * (1.0 - sig)
            dproj_ref[block * hidden : (block + 1) * hidden] = d_value.astype(BF)
            dproj_ref[(block + 4) * hidden : (block + 5) * hidden] = d_gate.astype(BF)
    dproj_ref[8 * hidden :] = joined(dlogit_ref)
    d_proj = dproj_ref[...]
    acc_ref[...] += mm(d_proj, norm, NT)
    back = mm(w_ref[...], d_proj)
    prod = back * hat
    gainx_ref[...] += sum(prod[:, r * residues : (r + 1) * residues] for r in range(step))
    first = joined(ds_ref) + norm_rows_back(back * gx_ref[...], hat, inv)
    low = first.astype(BF)
    for r in range(step):
        own = slice(r * residues, (r + 1) * residues)
        fg_ref[r] = first[:, own]
        outer_dim = right_ref.shape[0]
        row = pl.program_id(0) * step + r
        mixed = pl.ds(pl.multiple_of(row * outer_dim, outer_dim), outer_dim)
        dmix_ref[mixed, :] = mm(right_ref[...], low[:, own], NT).astype(BF).astype(F32)
        right = mm(mix_ref[r], low[:, own])
        for half in range(dright_ref.shape[0]):
            dright_ref[half] += right[:, half * LANES : (half + 1) * LANES]

    @pl.when(pl.program_id(0) == pl.num_programs(0) - 1)
    def _():
        gains_ref[...] = lane_sums(gainx_ref)
        outer_dim, count = right_ref.shape[0], left_ref.shape[0]
        d_left = jnp.zeros((count, LANES), F32)
        below = jnp.zeros((LANES - outer_dim, LANES), BF)
        for b in range(outer_dim):
            mixed = dmix_ref[pl.ds(b, count, stride=outer_dim), :].astype(BF)
            weight = outer_ref[pl.ds(b, outer_dim, stride=outer_dim), :].astype(BF)
            d_left += mm(mixed, jnp.concatenate([weight, below], axis=0), NT)
            gout_ref[pl.ds(b, outer_dim, stride=outer_dim), :] = mm(left_ref[...], mixed, TN)
        at = 0
        for half in range(dright_ref.shape[0]):
            spread_rows(packed_ref, at, dright_ref[half].astype(BF))
            at = at + outer_dim
        spread_rows(packed_ref, at, d_left.astype(BF))
        if carry_ref.shape[0] > 1:
            spread_rows(packed_ref, packed_ref.shape[1] - carry_ref.shape[0], carry_ref[...])
        in_rows, outer_rows = acc_ref.shape[0], gout_ref.shape[0]
        late_ref[:in_rows] = turn_blocks(acc_ref).astype(BF)
        late_ref[in_rows : in_rows + outer_rows] = gout_ref[...].astype(BF)
        spare = late_ref.shape[0] - in_rows - outer_rows
        late_ref[in_rows + outer_rows :] = jnp.zeros((spare, LANES), BF)


def last_kernel(xt_ref, fg_ref, ds_ref, gain_ref, w_ref, out_ref):
    for r in range(xt_ref.shape[0]):
        hat, inv = norm_rows(xt_ref[r].astype(F32))
        back = mm(w_ref[...], ds_ref[r])
        out_ref[r] = (fg_ref[r] + norm_rows_back(back * gain_ref[...], hat, inv)).T


def norm_lanes(values):
    centred = values - jnp.mean(values, axis=1, keepdims=True)
    inv = lax.rsqrt(jnp.mean(centred * centred, axis=1, keepdims=True) + EPS)
    return centred * inv, inv


def norm_lanes_back(scaled, hat, inv):
    return inv * (
        scaled
        - jnp.mean(scaled, axis=1, keepdims=True)
        - hat * jnp.mean(scaled * hat, axis=1, keepdims=True)
    )


def head_lanes(heads, width):
    depth = width // heads
    lane = lax.broadcasted_iota(jnp.int32, (heads, width), 1)
    head = lax.broadcasted_iota(jnp.int32, (heads, width), 0)
    return ((lane >= head * depth) & (lane < (head + 1) * depth)).astype(F32)


def rows_by_head(values, lanes):
    spread = values[:, None, :] * lanes[None]
    return spread.reshape(-1, values.shape[1])


def heads_by_row(values, lanes):
    spread = values[None] * lanes[:, None, :]
    return spread.reshape(-1, values.shape[1])


def crop_rows(residues):
    return pl.ds(pl.multiple_of(lax.axis_index("crop") * residues, residues), residues)


def attend_kernel(
    both_ref, own_ref, gain_ref, w_ref, bias_ref, mask_ref,
    norm_ref, gate_ref, qkv_ref, weights_ref, low_ref, gated_ref,
):
    width = own_ref.shape[1]
    residues = mask_ref.shape[2]
    heads = bias_ref.shape[1]
    rows = own_ref.shape[0]
    scale = 1.0 / (width // heads) ** 0.5
    hat, _ = norm_lanes(both_ref[:, :width].astype(F32))
    norm_ref[...] = (hat * gain_ref[...]).astype(BF)
    gate_ref[...] = jax.nn.sigmoid(mm(norm_ref[...], w_ref[:, 3 * width :]))
    qkv_ref[...] = mm(norm_ref[crop_rows(residues), :], w_ref[:, : 3 * width]).astype(BF)
    keys, values = qkv_ref[:, width : 2 * width], qkv_ref[:, 2 * width :]
    hat, _ = norm_lanes(own_ref[...].astype(F32))
    own = (hat * gain_ref[...]).astype(BF)
    query = mm(own, w_ref[:, :width]).astype(BF).astype(F32)
    gate = jax.nn.sigmoid(mm(own, w_ref[:, 3 * width :]))
    lanes = head_lanes(heads, width)
    query = rows_by_head(query, lanes).astype(BF)
    scores = mm(query, keys, NT) * scale + bias_ref[...].reshape(rows * heads, residues)
    mask = jnp.broadcast_to(mask_ref[...], bias_ref.shape).reshape(rows * heads, residues)
    scores = jnp.where(mask > 0.5, scores, -1000000000.0)
    powers = jnp.exp(scores - jnp.max(scores, axis=1, keepdims=True))
    weights = powers / jnp.sum(powers, axis=1, keepdims=True)
    weights_ref[...] = weights
    low = weights.astype(BF)
    low_ref[...] = low
    attn = mm(low, values).reshape(rows, heads, width)
    attn = jnp.sum(attn * lanes[None], axis=1)
    gated_ref[...] = jnp.broadcast_to((gate * attn).astype(BF)[None], gated_ref.shape)


def node_chunks(rows):
    size = min(rows, LANES)
    return [slice(k * size, (k + 1) * size) for k in range(rows // size)]


def gelu_parts(up):
    square = up * up
    curve = jnp.tanh(0.7978845608 * up * (1.0 + 0.044715 * square))
    half = 0.5 * (1.0 + curve)
    slope = half + up * (1.0 - curve * curve) * (0.3989422804 + 0.05351611220 * square)
    return up * half, slope


def node_kernel(
    both_ref, gated_ref, gn_ref, gs_ref, wo_ref, wu_ref, wd_ref, wn_ref, wr_ref,
    mid_ref, next_ref, proj_ref, right_ref, norm_ref,
):
    width = gated_ref.shape[1]
    residues = right_ref.shape[1]
    for rows in node_chunks(gated_ref.shape[0]):
        mid = both_ref[rows, :width].astype(F32) + mm(gated_ref[rows], wo_ref[...])
        mid_ref[rows] = mid
        hat, _ = norm_lanes(mid)
        act, _ = gelu_parts(mm((hat * gn_ref[...]).astype(BF), wu_ref[...]))
        following = mid + mm(act.astype(BF), wd_ref[...])
        next_ref[rows] = following
        hat, _ = norm_lanes(following)
        norm = (hat * gs_ref[...]).astype(BF)
        norm_ref[rows] = norm
        proj_ref[rows] = mm(norm, wn_ref[...]).astype(BF)
    right_ref[...] = mm(wr_ref[...], norm_ref[crop_rows(residues), :], NT).astype(BF)


def sublane_sum(values):
    return jnp.sum(values, axis=0, keepdims=True)


def node_back_kernel(
    outer_dim, got_ref, left_ref, both_ref, mid_ref, next_ref, gated_ref, gate_ref,
    gn_ref, gs_ref, wo_ref, wu_ref, wd_ref, wn_ref,
    gnode_ref, gd_ref, gu_ref, gout_ref, gains_ref, gainn_ref,
    dmid_ref, dattn_ref, dgate_ref, inner_ref,
    proj_ref, norm_ref, act_ref, low_ref, trans_ref, up_ref, midlow_ref,
):
    width = gated_ref.shape[1]
    devices = got_ref.shape[0] // 2
    halves = gated_ref.shape[0] // 2 // LANES
    at = 0
    for crop in range(2):
        for half in range(halves):
            total = jnp.zeros((outer_dim, LANES), F32)
            for d in range(devices):
                part = got_ref[crop * devices + d, half * outer_dim : (half + 1) * outer_dim]
                total += part.astype(F32)
            above = jnp.zeros((outer_dim, LANES), F32)
            below = jnp.zeros((LANES - 2 * outer_dim, LANES), F32)
            turned = jnp.concatenate([above, total, below], axis=0).T
            if left_ref.shape[0] == gated_ref.shape[0]:
                left = left_ref[at : at + LANES].astype(F32)
            else:
                rows = gated_ref.shape[0] // got_ref.shape[0]
                own = slice(halves * outer_dim, halves * outer_dim + rows)
                left = got_ref[at // rows : (at + LANES) // rows, own].astype(F32)
                left = left.reshape(LANES, LANES)
            proj_ref[at : at + LANES] = (turned + left).astype(BF)
            at = at + LANES
    gains, gainn = jnp.zeros((1, width), F32), jnp.zeros((1, width), F32)
    for rows in node_chunks(gated_ref.shape[0]):
        hat, inv = norm_lanes(next_ref[rows])
        norm_ref[rows] = (hat * gs_ref[...]).astype(BF)
        back = mm(proj_ref[rows], wn_ref[...], NT)
        gains += sublane_sum(back * hat)
        d_next = both_ref[rows, width:].astype(F32)
        d_next += norm_lanes_back(back * gs_ref[...], hat, inv)
        low = d_next.astype(BF)
        low_ref[rows] = low
        hat, inv = norm_lanes(mid_ref[rows])
        trans = (hat * gn_ref[...]).astype(BF)
        trans_ref[rows] = trans
        act, slope = gelu_parts(mm(trans, wu_ref[...]))
        act_ref[rows] = act.astype(BF)
        d_up = (mm(low, wd_ref[...], NT) * slope).astype(BF)
        up_ref[rows] = d_up
        back = mm(d_up, wu_ref[...], NT)
        gainn += sublane_sum(back * hat)
        d_mid = d_next + norm_lanes_back(back * gn_ref[...], hat, inv)
        dmid_ref[rows] = d_mid
        low = d_mid.astype(BF)
        midlow_ref[rows] = low
        d_gated = mm(low, wo_ref[...], NT)
        gate = gate_ref[rows]
        product = d_gated * gated_ref[rows].astype(F32)
        inner_ref[rows] = product
        dattn_ref[rows] = (d_gated * gate).astype(BF)
        dgate_ref[rows] = (product * (1.0 - gate)).astype(BF)
    gains_ref[...] = gains
    gainn_ref[...] = gainn
    gnode_ref[...] = mm(proj_ref[...], norm_ref[...], TN)[: 2 * outer_dim]
    gd_ref[...] = mm(act_ref[...], low_ref[...], TN)
    gu_ref[...] = mm(trans_ref[...], up_ref[...], TN)
    gout_ref[...] = mm(gated_ref[...], midlow_ref[...], TN)


def attend_back_kernel(
    own_ref, dattn_ref, inner_ref, qkv_ref, values_ref, weights_ref, column_ref, norm_ref,
    ds_ref, grad_ref, bias_ref,
):
    width = own_ref.shape[1]
    residues = qkv_ref.shape[0]
    rows, _, _ = norm_ref.shape
    heads = ds_ref.shape[0] // rows
    scale = 1.0 / (width // heads) ** 0.5
    lanes = head_lanes(heads, width)
    query, keys = qkv_ref[:, :width], qkv_ref[:, width : 2 * width]
    own = rows_by_head(own_ref[...].astype(F32), lanes).astype(BF)
    d_weights = mm(own, qkv_ref[:, 2 * width :], NT)
    weights = weights_ref[...]
    inner = jnp.sum(d_weights * weights, axis=1, keepdims=True)
    d_scores = (weights * (d_weights - inner)).astype(BF)
    ds_ref[...] = d_scores
    d_query = mm(d_scores, keys).reshape(rows, heads, width)
    d_query = jnp.sum(d_query * lanes[None], axis=1) * scale
    total = jnp.zeros(bias_ref.shape, F32)
    for r in range(rows):
        total += mm(d_scores[r * heads : (r + 1) * heads], norm_ref[r], NT)
    bias_ref[...] = total
    crop = crop_rows(residues)
    d_attn = dattn_ref[crop, :]
    spread = heads_by_row(values_ref[...].astype(F32), lanes).astype(BF)
    ones = heads_by_row(jnp.ones(values_ref.shape, F32), lanes).astype(BF)
    product = inner_ref[crop, :]
    high = product.astype(BF)
    rest = (product - high.astype(F32)).astype(BF)
    inner = mm(high, ones, NT) + mm(rest, ones, NT)
    column = column_ref[...]
    d_column = (column.astype(F32) * (mm(d_attn, spread, NT) - inner)).astype(BF)
    d_key = mm(d_column, query, TN).reshape(heads, rows, width)
    d_key = jnp.sum(d_key * lanes[:, None, :], axis=0) * scale
    d_value = mm(column, d_attn, TN).reshape(heads, rows, width)
    d_value = jnp.sum(d_value * lanes[:, None, :], axis=0)
    at = 0
    for part in (d_query, d_key, d_value):
        for half in range(width // LANES):
            grad_ref[at] = part[:, half * LANES : (half + 1) * LANES].astype(BF)
            at = at + 1


def layout_kernel(parts_ref, qkv_ref, bias_ref, gainx_ref, gains_ref, out_ref):
    total = jnp.zeros(parts_ref.shape[1:], F32)
    for d in range(parts_ref.shape[0]):
        total += parts_ref[d].astype(F32)
    at = 0
    for k in range(qkv_ref.shape[0]):
        spread_rows(out_ref, at, qkv_ref[k])
        at = at + qkv_ref.shape[1]
    spread_rows(out_ref, at, total.astype(BF))
    at = at + total.shape[0]
    small = [bias_ref[...], gainx_ref[...], gains_ref[...]]
    filled = sum(part.shape[0] for part in small)
    spare = out_ref.shape[1] - at - filled
    small = jnp.concatenate(small + [jnp.zeros((spare, LANES), F32)], axis=0)
    spread_rows(out_ref, at, small.astype(BF))


def adam_refs(master_ref, first_ref, second_ref, grad, outs, rate=0.1, decay=0.1):
    found = adam_step(master_ref[...], first_ref[...], second_ref[...], grad, rate, decay)
    for ref, value in zip(outs, found):
        ref[...] = value


def adam_kernel(count, layout, *refs):
    n_pair = 1 if layout else 3
    ins = 4 * count + 9 + n_pair
    outs, sums = refs[ins : ins + 3 * count + 9], refs[ins + 3 * count + 9 :]
    for k in range(count):
        master, first, second, grad = refs[4 * k : 4 * k + 4]
        adam_refs(master, first, second, grad[...], outs[3 * k : 3 * k + 3])
    olds, pair = refs[4 * count : 4 * count + 9], refs[4 * count + 9 : ins]

    @pl.when(pl.program_id(0) == 0)
    def _():
        if layout:
            start, part_up, part_z = layout
            values = unpack_pair(pair[0][:, start:].astype(F32), part_up, part_z)
        else:
            values = [ref[...] for ref in pair]
        for ref, value in zip(sums, values):
            ref[...] = value

    for k in range(3):
        height = olds[3 * k].shape[0]
        start = pl.multiple_of(pl.program_id(0) * height, height)
        at = 3 * (count + k)
        adam_refs(*olds[3 * k : 3 * k + 3], sums[k][pl.ds(start, height), :], outs[at : at + 3])


def across(rows):
    count = rows.shape[0] // LANES
    return jnp.concatenate([rows[k * LANES : (k + 1) * LANES] for k in range(count)], axis=1)


def unpack(take, layout):
    count, late_rows, in_rows, outer_rows, small_rows = layout
    blocks, at = [], 0
    for _ in range(6):
        blocks.append(take(at, at + count).reshape(-1, LANES))
        at = at + count
    late = take(at, at + late_rows)
    late = late.reshape((-1, 2) + late.shape[1:])
    late = jnp.concatenate([late[:, 0], late[:, 1]], axis=0).reshape(-1, LANES)
    at = at + late_rows
    small = jnp.sum(take(at, at + small_rows), axis=0)
    return blocks, (late[in_rows : in_rows + outer_rows], across(late[:in_rows])), small


def unpack_pair(pair, part_up, part_z):
    devices, half_rows, _ = pair.shape
    lower, upper = pair[: devices // 2], pair[devices // 2 :]
    over = 2 * part_up - half_rows
    g_up = jnp.concatenate([lower[:, part_up:], upper[:, :over]], axis=1).reshape(-1, LANES)
    g_down = lower[:, :part_up].reshape(-1, LANES)
    return upper[:, over : over + part_z].reshape(-1, LANES), across(g_up), g_down


def final_kernel(
    layout, dgate_ref, norm_ref, both_ref, dmid_ref, gain_ref, w_ref, gainn_ref, gains_ref, *refs
):
    n_got = 1 if layout else 9
    minor, refs = refs[:6], refs[6:]
    got, refs = refs[:n_got], refs[n_got:]
    olds, refs = refs[:9], refs[9:]
    news, minor_new, (dnode_ref, grad_ref, full_ref), sums = refs[:9], refs[9:15], refs[15:18], refs[18:]
    width = dmid_ref.shape[1]

    @pl.when(pl.program_id(0) == 0)
    def _():
        if layout:
            take = lambda start, stop: got[0][:, start:stop].astype(F32)
            blocks, grads, small = unpack(take, layout)
        else:
            values = [ref[...] for ref in got]
            blocks, grads, small = values[:6], values[6:8], values[8]
        for ref, grad in zip(sums[1:], grads):
            ref[...] = grad
        for k, block in enumerate(blocks):
            grad_ref[:, k * LANES : (k + 1) * LANES] = block.astype(BF)
        grad_ref[:, 3 * width :] = dgate_ref[...]
        sums[0][...] = mm(norm_ref[...], grad_ref[...], TN)
        total = jnp.zeros((1, width), F32)
        for rows in node_chunks(dmid_ref.shape[0]):
            hat, inv = norm_lanes(both_ref[rows, :width].astype(F32))
            back = mm(grad_ref[rows], w_ref[...], NT)
            total += sublane_sum(back * hat)
            full_ref[rows] = dmid_ref[rows] + norm_lanes_back(back * gain_ref[...], hat, inv)
        if dnode_ref.shape[0] == full_ref.shape[0]:
            dnode_ref[...] = full_ref[...]
        else:
            count = dnode_ref.shape[0]
            first = lax.axis_index("crop") * (full_ref.shape[0] // 2)
            first = pl.multiple_of(first + lax.axis_index("row") * count, count)
            dnode_ref[:, 0] = full_ref[pl.ds(first, count), :]
        heads = minor[0].shape[0]
        bias = small[:heads]
        adam_refs(*minor[:3], bias, minor_new[:3])
        spots = width // LANES
        rows_of = lambda line: [line[:, k * LANES : (k + 1) * LANES] for k in range(spots)]
        gain_b = minor[3][spots : spots + 1]
        weight = minor[0][...].astype(BF).astype(F32)
        grad_b = jnp.sum(weight * bias, axis=0, keepdims=True) / gain_b
        lines = rows_of(total) + [grad_b] + rows_of(gainn_ref[...]) + rows_of(gains_ref[...])
        rest = minor[3].shape[0] - len(lines)
        lines.append(small[heads : heads + rest])
        adam_refs(*minor[3:], jnp.concatenate(lines, axis=0), minor_new[3:], 1.0, 0.0)

    for k in range(3):
        height = olds[3 * k].shape[0]
        start = pl.multiple_of(pl.program_id(0) * height, height)
        adam_refs(*olds[3 * k : 3 * k + 3], sums[k][pl.ds(start, height), :], news[3 * k : 3 * k + 3])


def whole(shape):
    return pl.BlockSpec(shape, lambda i: (0,) * len(shape))


def by_row(step, shape):
    return pl.BlockSpec((step,) + shape, lambda i: (i,) + (0,) * len(shape))


def pair_call(kernel, steps, ins, outs, args, scratch=(), flops=0, moved=0, free=(), near=()):
    args = [
        arg if at in free else pltpu.with_memory_space_constraint(arg, pltpu.HBM)
        for at, arg in enumerate(args)
    ]
    shapes = [
        shape if at in near else pltpu.HBM(shape.shape, shape.dtype)
        for at, (_, shape) in enumerate(outs)
    ]
    return pl.pallas_call(
        kernel,
        grid=(steps,),
        in_specs=ins,
        out_specs=[spec for spec, _ in outs],
        out_shape=shapes,
        scratch_shapes=list(scratch),
        compiler_params=pltpu.CompilerParams(vmem_limit_bytes=40 * 1024 * 1024),
        cost_estimate=pl.CostEstimate(flops=flops, bytes_accessed=moved, transcendentals=0),
    )(*args)


def shards(row_devices, *arrays):
    (pair_feats, node_feats, chain_ids, out_grad, node_out_grad) = arrays[:5]
    masters, firsts, seconds = arrays[5:17], arrays[17:29], arrays[29:41]
    w_attend, w_pairbias, w_attout, w_nodeup, w_nodedown = masters[:5]
    w_node, w_outer, w_in, w_z, w_up, w_down, ln_gains = masters[5:]
    count, _, residues, width_z = pair_feats.shape
    width_s = node_feats.shape[2]
    heads = w_pairbias.shape[1]
    outer_dim = w_node.shape[1] // 2
    hidden = (w_in.shape[1] - width_z) // 8
    expand = w_up.shape[1]
    every = 2 * row_devices
    shape_of = jax.ShapeDtypeStruct
    cuts = [width_s, width_z, width_s, width_s, width_z, 2 * hidden, width_z]
    gains, at = [], 0
    for cut in cuts:
        gains.append(ln_gains[at : at + cut])
        at = at + cut
    gain_a, gain_b, gain_n, gain_s, gain_x, gain_t, gain_h = gains
    column = lambda gain: gain.reshape(-1, 1)
    line = lambda gain: gain.reshape(1, -1)
    nodes = 2 * residues
    crop_index, row_index = lax.axis_index("crop"), lax.axis_index("row")
    first_row = row_index * count
    chains = chain_ids[0]
    own_chain = lax.dynamic_slice_in_dim(chains, first_row, count, 0)
    same_own = own_chain[:, None] == chains[None, :]
    mask = same_own.astype(F32)[:, None, :]
    chain_col, chain_row = chains.reshape(-1, 1), chains.reshape(1, -1)

    att_wb, attout_wb = w_attend.astype(BF), w_attout.astype(BF)
    nodeup_wb, nodedown_wb, node_wb = w_nodeup.astype(BF), w_nodedown.astype(BF), w_node.astype(BF)
    outer_wb = w_outer.astype(BF).reshape(outer_dim, outer_dim * width_z)
    bias_wb, in_wb, z_wb = w_pairbias.astype(BF), w_in.astype(BF), w_z.astype(BF)
    up_wb, down_wb = w_up.astype(BF), w_down.astype(BF)
    bias_wt, in_wt, z_wt, up_wt, down_wt = bias_wb.T, in_wb.T, z_wb.T, up_wb.T, down_wb.T

    direct = count % 16 == 0
    step = next(size for size in (4, 2, 1) if count % size == 0)
    steps = count // step
    pairs = count * residues

    node_both = jnp.concatenate([node_feats[:, 0], node_out_grad[:, 0]], axis=1)
    pair_x = pair_feats[:, 0]
    xt, bias_norm, pair_bias = pair_call(
        bias_kernel, steps,
        [by_row(step, (residues, width_z)), whole((width_z, 1)), whole((heads, width_z))],
        [(by_row(step, (width_z, residues)), shape_of((count, width_z, residues), BF)),
         (by_row(step, (width_z, residues)), shape_of((count, width_z, residues), BF)),
         (by_row(step, (heads, residues)), shape_of((count, heads, residues), F32))],
        [pair_x, column(gain_b), bias_wt], free=(0, 1, 2), near=(2,),
        flops=2 * pairs * width_z * heads, moved=4 * pairs * width_z,
    )

    def own_rows(values):
        return lax.dynamic_slice_in_dim(values, crop_index * residues + first_row, count, 0)

    def single(kernel, outs, args, scratch=(), flops=0, far=(), apart=False):
        moved = sum(arg.size * 4 for arg in args)
        return pair_call(
            kernel, 1, [whole(arg.shape) for arg in args],
            [(whole(shape), shape_of(shape, kind)) for shape, kind in outs],
            args, scratch, flops, moved, (0,) if apart else range(len(args)),
            [at for at in range(len(outs)) if at not in far],
        )

    columns = [column(gain) for gain in (gain_x, gain_t, gain_h)]
    ready = [att_wb, attout_wb, nodeup_wb, nodedown_wb, mask]
    node_both, _ = gather_all(
        spread_over(node_both, row_devices), row_devices, [xt, pair_bias] + ready
    )
    node_both = node_both.reshape(nodes, 2 * width_s)
    square = (nodes, width_s)
    att_norm, gate_all, qkv_crop, att_weights, weights_low, gated_own = single(
        attend_kernel,
        [(square, BF), (square, F32), ((residues, 3 * width_s), BF),
         ((count * heads, residues), F32), ((count * heads, residues), BF),
         ((every, count, width_s), BF)],
        [node_both, node_feats[:, 0], line(gain_a), att_wb, pair_bias, mask],
        flops=8 * nodes * width_s * width_s, far=(0, 1, 2, 3),
    )
    weights_cut = weights_low.reshape(count, heads, row_devices, count).transpose(2, 0, 1, 3)
    if direct:
        weights_cut = weights_cut.reshape(row_devices, -1, LANES)
    ready = [weights_cut, node_wb, outer_wb, in_wt, chain_col, columns[0]]
    gated = lax.all_to_all(gated_own, BOTH, split_axis=0, concat_axis=0, tiled=True)
    gated = after(gated, ready).reshape(nodes, width_s)

    node_mid, node_next, node_proj, right_t = single(
        node_kernel,
        [(square, F32), (square, F32), ((nodes, 2 * outer_dim), BF), ((outer_dim, residues), BF)],
        [node_both, gated, line(gain_n), line(gain_s), attout_wb, nodeup_wb, nodedown_wb, node_wb,
         node_wb[:, outer_dim:].T],
        scratch=[pltpu.VMEM(square, BF)], flops=18 * nodes * width_s * width_s, far=(0, 1),
    )
    node_out = own_rows(node_next).astype(BF)[:, None]
    left_vec = own_rows(node_proj[:, :outer_dim])
    outer_mix = mm(left_vec, outer_wb).astype(BF).reshape(count, outer_dim, width_z)

    share = hidden // row_devices
    dims = (share, count) if direct else None

    def sent_block(tiles, extra=0):
        if direct:
            shape = (row_devices, tiles * share * count + extra, LANES)
            return whole(shape), shape_of(shape, BF)
        return by_row(step, (tiles, hidden, LANES)), shape_of((count, tiles, hidden, LANES), BF)

    def stage(tiles):
        return [pltpu.VMEM((tiles * hidden * count, LANES), F32)] if direct else []

    def swap(block):
        return lax.all_to_all(block, "row", split_axis=0, concat_axis=0, tiled=True)

    def to_channels(block):
        if direct:
            return swap(block)
        tiles = block.shape[1]
        cut = block.reshape(count, tiles, row_devices, share, LANES)
        sent = swap(cut.transpose(2, 1, 3, 0, 4))
        return sent.transpose(1, 2, 0, 3, 4).reshape(1, tiles, share, residues, LANES)

    def to_rows(block):
        if direct:
            return swap(block.reshape(row_devices, -1, LANES))
        tiles = block.shape[1]
        cut = block.reshape(tiles, share, row_devices, count, LANES)
        got = swap(cut.transpose(2, 0, 1, 3, 4))
        return got.transpose(3, 1, 0, 2, 4).reshape(count, tiles, hidden, LANES)

    def tri_out(tiles):
        if not direct:
            return tri_block(tiles)
        shape = (row_devices, tiles, share, count, LANES)
        each = share // tri_steps(share)
        block = (row_devices, tiles, each, count, LANES)
        return pl.BlockSpec(block, lambda i: (0, 0, i, 0, 0)), shape_of(shape, BF)

    def tri_block(tiles, extra=0):
        if direct:
            return sent_block(tiles, extra)
        shape = (1, tiles, share, residues, LANES)
        spec = pl.BlockSpec((1, tiles, 1, residues, LANES), lambda i: (0, 0, i, 0, 0))
        return spec, shape_of(shape, BF)

    ride = weights_cut if direct else jnp.zeros((1, 1, LANES), BF)
    extra = ride.shape[1]
    first_sum, acts_own = pair_call(
        functools.partial(first_kernel, share, count), steps,
        [by_row(step, (width_z, residues)), by_row(step, (outer_dim, width_z)),
         whole((outer_dim, residues)), by_row(step, (1, residues)), whole((width_z, 1)),
         whole(in_wt.shape), whole(ride.shape)],
        [(by_row(step, (width_z, residues)), shape_of((count, width_z, residues), F32)),
         sent_block(6, extra)],
        [xt, outer_mix, right_t, mask, column(gain_x), in_wt, ride],
        scratch=stage(6),
        flops=16 * pairs * width_z * hidden, moved=12 * pairs * width_z,
    )

    tri_steps = lambda channels: channels // 2 if direct and channels % 2 == 0 else channels
    chain_specs = [whole((residues, 1)), whole((1, residues))]
    product = 2 * share * residues**3
    ready = [in_wb, z_wb, up_wb, down_wb, z_wt, up_wt, down_wt] + columns
    acts = after(to_channels(acts_own), ready)
    weights_col = acts[:, 6 * share * count :] if direct else swap(weights_cut)
    weights_col = weights_col.reshape(residues, heads * count)
    (tri,) = pair_call(
        functools.partial(tri_kernel, dims), tri_steps(share), chain_specs + [tri_block(6, extra)[0]],
        [tri_out(3)], [chain_col, chain_row, acts], free=(2,),
        flops=2 * product, moved=share * residues * 9 * 256,
    )
    tri_rows = to_rows(tri)

    slab = by_row(step, (width_z, residues))
    second_args = [
        (by_row(step, (width_z, residues)), first_sum),
        (sent_block(3)[0], tri_rows),
        (by_row(step, (residues, width_z)), out_grad[:, 0]),
        (by_row(step, (1, residues)), mask),
    ]
    second_args += [
        (whole(v.shape), v)
        for v in (
            column(gain_x), column(gain_t), column(gain_h),
            in_wt[8 * hidden :], z_wt, z_wb, up_wt, up_wb, down_wt, down_wb,
        )
    ]
    part_up, part_z = expand // row_devices, 2 * hidden // row_devices
    half_rows = part_up + part_up // 2
    carried = 2 * part_up + part_z if direct else 0
    acc_shapes = [
        (expand, width_z), (expand, width_z), (2 * hidden, width_z),
        ((2 * hidden + width_z) // LANES, LANES),
    ]
    pair_out, d_second, d_logit, dtri_own, g_down, g_up_t, g_z, gains_th = pair_call(
        functools.partial(second_kernel, share, count), steps,
        [spec for spec, _ in second_args],
        [(by_row(step, (residues, width_z)), shape_of((count, residues, width_z), BF)),
         (slab, shape_of((count, width_z, residues), F32)),
         (slab, shape_of((count, width_z, residues), BF)),
         sent_block(3, carried)]
        + [(whole(s), shape_of(s, F32)) for s in acc_shapes],
        [arg for _, arg in second_args], free=(1,),
        scratch=[pltpu.VMEM((2 * hidden, residues), F32), pltpu.VMEM((width_z, residues), F32)]
        + stage(3) + stage(3),
        flops=12 * pairs * width_z * expand, moved=20 * pairs * width_z,
    )

    dtri = to_channels(dtri_own)
    if direct:
        grad_parts = dtri[:, 3 * share * count :]
    else:
        turned = g_up_t.reshape(-1, LANES, LANES).transpose(0, 2, 1)
        parts = [g.reshape(row_devices, -1, LANES) for g in (g_down, turned, g_z)]
        grad_parts = swap(jnp.concatenate(parts, axis=1).astype(BF))
    row_sum = jnp.sum(grad_parts.astype(F32), axis=0)
    row_sum = jnp.pad(row_sum, ((0, 2 * half_rows - row_sum.shape[0]), (0, 0)))
    lower, upper = row_sum[:half_rows], row_sum[half_rows:]
    low_crop = crop_index == 0
    theirs = lax.ppermute(jnp.where(low_crop, upper, lower), "crop", [(0, 1), (1, 0)])
    pair_own = (jnp.where(low_crop, lower, upper) + theirs).astype(BF)
    (dacts,) = pair_call(
        functools.partial(tri_back_kernel, dims), tri_steps(share),
        chain_specs + [tri_block(6, extra)[0], tri_block(3, carried)[0]],
        [tri_out(6)], [chain_col, chain_row, acts, dtri], free=(2,),
        flops=4 * product, moved=share * residues * 15 * 256,
    )
    dacts_rows = after(to_rows(dacts), pair_own)

    right_rows = residues // LANES * outer_dim
    left_rows = -(-count // 16) * 16
    carry = pair_own if direct else jnp.zeros((1, LANES), BF)
    packed_rows = right_rows + left_rows + (half_rows if direct else 0)
    in_rows, outer_rows = in_wt.shape[0], w_outer.shape[0]
    late_rows = -(-(in_rows + outer_rows) // (every * 16)) * every * 16
    first_grad, packed, late, gains_x = pair_call(
        functools.partial(third_kernel, share, count), steps,
        [slab, sent_block(6)[0], slab, slab, by_row(step, (1, residues)),
         by_row(step, (outer_dim, width_z)), whole((outer_dim, residues)), whole((width_z, 1)),
         whole(in_wt.shape), whole(in_wb.shape), whole(left_vec.shape), whole(w_outer.shape),
         whole(carry.shape)],
        [(slab, shape_of((count, width_z, residues), F32)),
         (whole((row_devices, packed_rows, LANES)),
          shape_of((row_devices, packed_rows, LANES), BF)),
         (whole((late_rows, LANES)), shape_of((late_rows, LANES), BF)),
         (whole((width_z // LANES, LANES)), shape_of((width_z // LANES, LANES), F32))],
        [first_sum, dacts_rows, d_second, d_logit, mask, outer_mix, right_t, columns[0],
         in_wt, in_wb, left_vec, w_outer, carry],
        free=(1,),
        scratch=[pltpu.VMEM((width_z, residues), F32), pltpu.VMEM((9 * hidden, step * residues), BF),
                 pltpu.VMEM(in_wt.shape, F32), pltpu.VMEM((count * outer_dim, LANES), F32),
                 pltpu.VMEM((residues // LANES, outer_dim, LANES), F32),
                 pltpu.VMEM(w_outer.shape, F32)] + stage(6),
        flops=54 * pairs * width_z * hidden, moved=20 * pairs * width_z,
    )
    late = late.reshape(2, late_rows // 2, LANES)
    odd = row_index % 2 == 1
    theirs = core_exchange(jnp.where(odd, late[0], late[1]), row_devices)
    late = jnp.where(odd, late[1], late[0]).astype(F32) + theirs.astype(F32)
    late = late.astype(BF).reshape(row_devices, -1, LANES)
    got, first_got = gather_all(packed, row_devices, late)
    late_parts = same_core_exchange(after(late, first_got), row_devices)
    left_all = left_vec
    if not direct:
        left_all = got[:, right_rows : right_rows + count].reshape(nodes, LANES)

    wide_node = jnp.pad(node_wb, ((0, 0), (0, LANES - 2 * outer_dim)))
    tall, low_square = (nodes, w_nodeup.shape[1]), pltpu.VMEM(square, BF)
    (g_node, g_nodedown, g_nodeup, g_attout, gain_s_grad, gain_n_grad,
     grad_mid, d_attn, d_gate, inner) = single(
        functools.partial(node_back_kernel, outer_dim),
        [((2 * outer_dim, width_s), F32), (w_nodedown.shape, F32), (w_nodeup.shape, F32),
         (w_attout.shape, F32), ((1, width_s), F32), ((1, width_s), F32),
         (square, F32), (square, BF), (square, BF), (square, F32)],
        [got, left_all, node_both, node_mid, node_next, gated, gate_all,
         line(gain_n), line(gain_s), attout_wb, nodeup_wb, nodedown_wb, wide_node],
        scratch=[pltpu.VMEM((nodes, LANES), BF), low_square, pltpu.VMEM(tall, BF), low_square,
                 low_square, pltpu.VMEM(tall, BF), low_square],
        flops=50 * nodes * width_s * width_s, far=(0, 1, 2, 3, 4, 5, 6, 8), apart=True,
    )

    values_own = lax.dynamic_slice(qkv_crop, (first_row, 2 * width_s), (count, width_s))
    score_grad, qkv_grad, g_bias_t = single(
        attend_back_kernel,
        [((count * heads, residues), BF), ((3 * width_s // LANES, count, LANES), BF),
         ((heads, width_z), F32)],
        [own_rows(d_attn), d_attn, inner, qkv_crop, values_own, att_weights, weights_col,
         bias_norm],
        flops=12 * count * heads * residues * width_s,
    )

    qkv_rows, share_rows = qkv_grad.size // LANES, late_parts.shape[1]
    small_rows = heads + gains_x.shape[0] + gains_th.shape[0]
    small_rows = small_rows + -small_rows % 16
    layout = (count, share_rows, in_rows, outer_rows, small_rows)
    last_shape = (row_devices, qkv_rows + share_rows + small_rows, LANES)
    pieces = [late_parts, qkv_grad, g_bias_t, gains_x, gains_th]
    if direct:
        (last_own,) = single(layout_kernel, [(last_shape, BF)], pieces)
    else:
        small = jnp.concatenate(pieces[2:])
        small = jnp.pad(small, ((0, small_rows - small.shape[0]), (0, 0)))
        late_own = jnp.sum(late_parts.astype(F32), axis=0)
        last_own = [qkv_grad.reshape(-1, LANES).astype(F32), late_own, small]
        last_own = spread_over(jnp.concatenate(last_own).astype(BF), row_devices)

    (pair_grad,) = pair_call(
        last_kernel, steps,
        [slab, slab, by_row(step, (heads, residues)), whole((width_z, 1)), whole((width_z, heads))],
        [(by_row(step, (residues, width_z)), shape_of((count, residues, width_z), F32))],
        [xt, first_grad, score_grad.reshape(count, heads, residues), column(gain_b), bias_wb],
        flops=4 * pairs * width_z * heads, moved=10 * pairs * width_z,
    )

    parts = 2
    split = lambda k: pl.BlockSpec((olds[k].shape[0] // parts, olds[k].shape[1]), lambda i: (i, 0))
    updated = {}

    early = {2: g_attout, 3: g_nodeup, 4: g_nodedown, 5: g_node}
    turned = lambda k, value: value.T if k == 5 else value
    specs, args, outs = [], [], []
    for k, grad in early.items():
        spec = pl.BlockSpec((grad.shape[0] // parts, grad.shape[1]), lambda i: (i, 0))
        specs += [spec] * 4
        args += [turned(k, old[k]) for old in (masters, firsts, seconds)] + [grad]
        outs += [(spec, shape_of(grad.shape, F32))] * 3
    pair_keys = (8, 9, 10)
    for k in pair_keys:
        height, width = masters[k].shape
        spec = pl.BlockSpec((height // parts, width), lambda i: (i, 0))
        specs += [spec] * 3
        args += [masters[k], firsts[k], seconds[k]]
        outs += [(spec, shape_of((height, width), F32))] * 3
    if direct:
        pair_got, pair_layout = [got], (right_rows + left_rows, part_up, part_z)
    else:
        pair_all, _ = gather_all(spread_over(pair_own, row_devices), row_devices)
        pair_got, pair_layout = list(unpack_pair(pair_all.astype(F32), part_up, part_z)), None
    specs += [whole(arg.shape) for arg in pair_got]
    args += pair_got
    found = pair_call(
        functools.partial(adam_kernel, len(early), pair_layout), parts, specs, outs, args,
        scratch=[pltpu.VMEM(masters[k].shape, F32) for k in pair_keys],
        moved=sum(7 * arg.size for arg in args),
    )
    beside = (pair_grad, found[0], node_out)
    last, _ = gather_all(last_own, row_devices, beside)
    for at, k in enumerate(early):
        updated[k] = [turned(k, value) for value in found[3 * at : 3 * at + 3]]
    for at, k in enumerate(pair_keys, len(early)):
        updated[k] = found[3 * at : 3 * at + 3]

    late_keys = (0, 6, 7)
    got_last = [last]
    if not direct:
        blocks, sums, small = unpack(lambda a, b: last[:, a:b].astype(F32), layout)
        got_last = blocks + list(sums) + [small]
    node_shape = (count, 1, width_s) if direct else square
    minor = [old[1].T for old in (masters, firsts, seconds)]
    minor += [old[11].reshape(-1, LANES) for old in (masters, firsts, seconds)]
    fixed = [d_gate, att_norm, node_both, grad_mid, line(gain_a), att_wb, gain_n_grad, gain_s_grad]
    fixed = fixed + minor + got_last
    olds, specs = [], [whole(arg.shape) for arg in fixed]
    for k in late_keys:
        olds += [masters[k], firsts[k], seconds[k]]
    blocked = [split(k) for k in range(len(olds))]
    found = pair_call(
        functools.partial(final_kernel, layout if direct else None), parts, specs + blocked,
        [(spec, shape_of(old.shape, F32)) for spec, old in zip(blocked, olds)]
        + [(whole(value.shape), shape_of(value.shape, F32)) for value in minor]
        + [(whole(node_shape), shape_of(node_shape, F32))],
        fixed + olds,
        scratch=[pltpu.VMEM((nodes, 4 * width_s), BF), pltpu.VMEM(square, F32)]
        + [pltpu.VMEM(masters[k].shape, F32) for k in late_keys],
        flops=16 * nodes * width_s * width_s, moved=sum(7 * old.size for old in olds),
    )
    for at, k in enumerate(late_keys):
        updated[k] = found[3 * at : 3 * at + 3]
    updated[1] = [value.T for value in found[9:12]]
    updated[11] = [value.reshape(-1) for value in found[12:15]]
    node_grad = found[15] if direct else own_rows(found[15])[:, None]
    results = [pair_out[:, None], node_out, pair_grad[:, None], node_grad]
    for k in range(12):
        results.extend(updated[k])
    return tuple(results)


def solution(mesh):
    rows4, rows3 = P("row", "crop", None, None), P("row", "crop", None)
    return jax.shard_map(
        functools.partial(shards, mesh.shape["row"]),
        mesh=mesh,
        in_specs=(rows4, rows3, P("crop", None), rows4, rows3) + (P(),) * 36,
        out_specs=(rows4, rows3, rows4, rows3) + (P(),) * 36,
        check_vma=False,
    )
```

```python
import functools
import jax
import jax.numpy as jnp
from jax import lax
from jax.experimental import pallas as pl
from jax.experimental.pallas import tpu as pltpu
from jax.sharding import PartitionSpec as P

ADAM_STEP = 4
EPS = 1e-05
BF = jnp.bfloat16
F32 = jnp.float32
LANES = 128
HALF = 64
BOTH = ("crop", "row")
NN = (((1,), (0,)), ((), ()))
NT = (((1,), (1,)), ((), ()))
TN = (((0,), (0,)), ((), ()))


def mm(left, right, dims=NN):
    return lax.dot_general(left, right, dims, preferred_element_type=F32)


def adam_step(master, first_old, second_old, grad_total, rate, decay):
    first_new = 0.9 * first_old + 0.1 * grad_total
    second_new = 0.999 * second_old + 0.001 * grad_total * grad_total
    first_hat = first_new / (1.0 - 0.9**ADAM_STEP)
    second_hat = second_new / (1.0 - 0.999**ADAM_STEP)
    master_new = master - rate * (first_hat / (jnp.sqrt(second_hat) + 1e-08) + decay * master)
    return (first_new, second_new, master_new)


def after(value, event):
    return lax.optimization_barrier((value, event))[0]


def spread_over(part, row_devices):
    return jnp.broadcast_to(part[None], (row_devices,) + part.shape)


def same_core_exchange(block, row_devices):
    groups = [[d for d in range(2 * row_devices) if d % 2 == k] for k in range(2)]
    return lax.all_to_all(
        block, BOTH, split_axis=0, concat_axis=0, tiled=True, axis_index_groups=groups
    )


def core_exchange(block, row_devices):
    return lax.ppermute(block, "row", [(d, d ^ 1) for d in range(row_devices)])


def gather_all(spread, row_devices, during=()):
    every = 2 * row_devices
    first = same_core_exchange(spread, row_devices)
    got = after(first, during)
    other = core_exchange(got, row_devices)
    odd = lax.axis_index("row") % 2 == 1
    pair = [jnp.where(odd, other, got), jnp.where(odd, got, other)]
    return jnp.stack(pair, axis=1).reshape((every,) + spread.shape[1:]), first


def norm_rows(values):
    centred = values - jnp.mean(values, axis=0, keepdims=True)
    inv = lax.rsqrt(jnp.mean(centred * centred, axis=0, keepdims=True) + EPS)
    return centred * inv, inv


def norm_rows_back(scaled, hat, inv):
    return inv * (
        scaled
        - jnp.mean(scaled, axis=0, keepdims=True)
        - hat * jnp.mean(scaled * hat, axis=0, keepdims=True)
    )


def turn(values):
    return pltpu.roll(values, HALF, values.ndim - 1)


def low_lanes(shape):
    return lax.broadcasted_iota(jnp.int32, shape, len(shape) - 1) < HALF


def fold_pair(first, second):
    low = low_lanes((first.shape[0], LANES))
    f_lo, f_hi = first[:, :LANES], first[:, LANES:]
    s_lo, s_hi = second[:, :LANES], second[:, LANES:]
    f_turn, s_turn = turn(f_hi), turn(s_hi)
    main_f = f_lo + jnp.where(low, f_turn, 0.0)
    main_s = s_lo + jnp.where(low, s_turn, 0.0)
    return main_f, main_s, jnp.where(low, f_hi, s_turn)


def unfold_pair(main_f, main_s, tail):
    low = low_lanes(tail.shape)
    first = jnp.concatenate([main_f, jnp.where(low, tail, turn(main_f))], axis=1)
    second = jnp.concatenate([main_s, jnp.where(low, turn(tail), turn(main_s))], axis=1)
    return first, second


def put_tile(stage_ref, tile, row, rows, values):
    high = values.shape[0]
    stage_ref[pl.ds(tile * high * rows + row, high, stride=rows), :] = values


def get_tile(stage_ref, tile, row, rows, high):
    return stage_ref[pl.ds(tile * high * rows + row, high, stride=rows), :]


def ship(stage_ref, send_ref, tiles, share, rows):
    devices = send_ref.shape[0]
    span = share * rows
    for t in range(tiles):
        block = stage_ref[t * devices * span : (t + 1) * devices * span]
        send_ref[:, t * span : (t + 1) * span] = block.reshape(devices, span, LANES).astype(BF)


def unship(got_ref, stage_ref, tiles, share, rows):
    devices = got_ref.shape[0]
    span = share * rows
    for t in range(tiles):
        block = got_ref[:, t * span : (t + 1) * span].astype(F32)
        stage_ref[t * devices * span : (t + 1) * devices * span] = block.reshape(-1, LANES)


def lane_sums(ref):
    count = ref.shape[0] // LANES
    cut = [ref[k * LANES : (k + 1) * LANES].T for k in range(count)]
    return jnp.concatenate([jnp.sum(part, axis=0, keepdims=True) for part in cut], axis=0)


def spread_rows(ref, at, rows):
    shape = (ref.shape[0],) + rows.shape
    ref[:, at : at + rows.shape[0]] = jnp.broadcast_to(rows[None], shape)


def turn_blocks(ref):
    count = ref.shape[0] // LANES
    return jnp.concatenate([ref[k * LANES : (k + 1) * LANES].T for k in range(count)], axis=0)


def bias_kernel(x_ref, gain_ref, weight_ref, xt_ref, norm_ref, bias_ref):
    for r in range(x_ref.shape[0]):
        xt = x_ref[r].astype(F32).T
        xt_ref[r] = xt.astype(BF)
        hat, _ = norm_rows(xt)
        norm = (hat * gain_ref[...]).astype(BF)
        norm_ref[r] = norm
        bias_ref[r] = mm(weight_ref[...], norm)


def first_kernel(
    share, rows, xt_ref, mix_ref, right_ref, mask_ref, gain_ref, weight_ref, ride_ref,
    sum_ref, send_ref, *stage,
):
    hidden = weight_ref.shape[0] // 9
    step, _, residues = xt_ref.shape
    columns = [slice(r * residues, (r + 1) * residues) for r in range(step)]
    mixes = [mm(mix_ref[r], right_ref[...], TN) for r in range(step)]
    total = jnp.concatenate([xt_ref[r].astype(F32) + mixes[r] for r in range(step)], axis=1)
    for r in range(step):
        sum_ref[r] = total[:, columns[r]]
    hat, _ = norm_rows(total)
    norm = (hat * gain_ref[...]).astype(BF)
    mask = jnp.concatenate([mask_ref[r] for r in range(step)], axis=1)
    for pair in range(2):
        acts = []
        for block in (2 * pair, 2 * pair + 1):
            value = mm(weight_ref[block * hidden : (block + 1) * hidden], norm)
            gate = mm(weight_ref[(block + 4) * hidden : (block + 5) * hidden], norm)
            acts.append(jax.nn.sigmoid(gate) * value * mask)
        for r in range(step):
            row = pl.program_id(0) * step + r
            tiles = fold_pair(*(act[:, columns[r]] for act in acts))
            for t in range(3):
                if stage:
                    put_tile(stage[0], 3 * pair + t, row, rows, tiles[t])
                else:
                    send_ref[r, 3 * pair + t] = tiles[t].astype(BF)
    if stage:

        @pl.when(pl.program_id(0) == pl.num_programs(0) - 1)
        def _():
            ship(stage[0], send_ref, 6, share, rows)
            send_ref[:, 6 * share * rows :] = ride_ref[...]


def chain_mask(col_ref, row_ref):
    return col_ref[...] == row_ref[...]


def flat_rows(ref, tile, spot):
    block = ref[:, spot(tile)] if spot else ref[:, tile, 0]
    return block.reshape(-1, block.shape[-1])


def slot_operands(ref, pair, spot):
    main_f, main_s, tail = (flat_rows(ref, 3 * pair + t, spot).astype(F32) for t in range(3))
    low = low_lanes(tail.shape)
    zero = jnp.zeros_like(tail)
    first = jnp.concatenate([main_f, jnp.where(low, tail, zero)], axis=1).astype(BF)
    second = jnp.concatenate([main_s, jnp.where(low, turn(tail), zero)], axis=1).astype(BF)
    return first, second


def channel_spots(dims):
    if not dims:
        return [None]
    share, rows = dims
    each = share // pl.num_programs(0)
    first = pl.program_id(0) * each

    def spot_of(channel):
        return lambda tile: pl.ds(pl.multiple_of((tile * share + channel) * rows, rows), rows)

    return [spot_of(first + k) for k in range(each)]


def raw_columns(slots, same):
    values = slots.astype(F32)
    main, tail = values[:, :LANES], values[:, LANES:]
    wide = jnp.concatenate(
        [main, jnp.where(low_lanes(tail.shape), tail, turn(main))], axis=1
    )
    return jnp.where(same, wide, 0.0).astype(BF)


def store_tiles(out_ref, pair, k, tiles):
    for t in range(3):
        block = tiles[t].astype(BF).reshape(out_ref.shape[0], -1, LANES)
        out_ref[:, 3 * pair + t, k] = block


def tri_kernel(dims, col_ref, row_ref, acts_ref, out_ref):
    same = chain_mask(col_ref, row_ref)
    for k, spot in enumerate(channel_spots(dims)):
        left_out, right_out = slot_operands(acts_ref, 0, spot)
        left_in, right_in = slot_operands(acts_ref, 1, spot)
        outgoing = jnp.where(same, mm(left_out, right_out, NT), 0.0)
        incoming = mm(raw_columns(left_in, same), right_in, TN)
        low = low_lanes((outgoing.shape[0], LANES))
        o_lo, o_hi = outgoing[:, :LANES], outgoing[:, LANES:]
        main_o = o_lo + jnp.where(low, turn(o_hi), 0.0)
        tail = jnp.where(low, o_hi, turn(incoming[:, LANES:]))
        store_tiles(out_ref, 0, k, (main_o, incoming[:, :LANES], tail))


def tri_back_kernel(dims, col_ref, row_ref, acts_ref, grad_ref, out_ref):
    same = chain_mask(col_ref, row_ref)
    for k, spot in enumerate(channel_spots(dims)):
        left_out, right_out = slot_operands(acts_ref, 0, spot)
        left_in, right_in = slot_operands(acts_ref, 1, spot)
        grad_out, grad_in = slot_operands(grad_ref, 0, spot)
        raw_out = raw_columns(grad_out, same)
        d_left = mm(raw_out, right_out)
        d_right = mm(raw_out, left_out, TN)
        low = low_lanes((d_left.shape[0], LANES))
        tail = jnp.where(low, d_left[:, LANES:], turn(d_right[:, LANES:]))
        store_tiles(out_ref, 0, k, (d_left[:, :LANES], d_right[:, :LANES], tail))
        d_left = jnp.where(same, mm(right_in, grad_in, NT), 0.0)
        d_right = mm(raw_columns(left_in, same), grad_in)
        l_lo, l_hi = d_left[:, :LANES], d_left[:, LANES:]
        main_l = l_lo + jnp.where(low, turn(l_hi), 0.0)
        tail = jnp.where(low, l_hi, turn(d_right[:, LANES:]))
        store_tiles(out_ref, 1, k, (main_l, d_right[:, :LANES], tail))


def second_kernel(
    share, rows, sum_ref, tri_ref, grad_ref, mask_ref, gx_ref, gt_ref, gh_ref,
    wgate_ref, wzt_ref, wz_ref, wut_ref, wu_ref, wdt_ref, wd_ref,
    out_ref, ds_ref, dlogit_ref, send_ref, gd_ref, gu_ref, gz_ref, gains_ref, gaint_ref, gainh_ref,
    *stage,
):
    @pl.when(pl.program_id(0) == 0)
    def _():
        for acc in (gd_ref, gu_ref, gz_ref, gaint_ref, gainh_ref):
            acc[...] = jnp.zeros_like(acc)
        if stage:
            unship(tri_ref, stage[0], 3, share, rows)

    step, _, residues = sum_ref.shape
    joined = lambda values: jnp.concatenate(list(values), axis=1)
    total = joined(sum_ref[r] for r in range(step))
    mask = joined(mask_ref[r] for r in range(step))
    hat_x, _ = norm_rows(total)
    norm = (hat_x * gx_ref[...]).astype(BF)
    out_gate = jax.nn.sigmoid(mm(wgate_ref[...], norm))
    combined = []
    for r in range(step):
        row = pl.program_id(0) * step + r
        if stage:
            tiles = [get_tile(stage[0], t, row, rows, total.shape[0]) for t in range(3)]
        else:
            tiles = [tri_ref[r, t].astype(F32) for t in range(3)]
        combined.append(jnp.concatenate(unfold_pair(*tiles), axis=0))
    hat_t, inv_t = norm_rows(joined(combined))
    tri_norm = (hat_t * gt_ref[...]).astype(BF)
    tri_proj = mm(wzt_ref[...], tri_norm)
    second = total + out_gate * tri_proj * mask
    hat_h, inv_h = norm_rows(second)
    trans_in = (hat_h * gh_ref[...]).astype(BF)
    act, slope = gelu_parts(mm(wut_ref[...], trans_in))
    act = act.astype(BF)
    result = second + mm(wdt_ref[...], act)
    for r in range(step):
        out_ref[r] = result[:, r * residues : (r + 1) * residues].T.astype(BF)
    grad_low = joined(grad_ref[r].astype(F32).T.astype(BF) for r in range(step))
    gd_ref[...] += mm(act, grad_low, NT)
    d_up = (mm(wd_ref[...], grad_low) * slope).astype(BF)
    gu_ref[...] += mm(d_up, trans_in, NT)
    back = mm(wu_ref[...], d_up)
    prod = back * hat_h
    gainh_ref[...] += sum(prod[:, r * residues : (r + 1) * residues] for r in range(step))
    d_second = grad_low.astype(F32) + norm_rows_back(back * gh_ref[...], hat_h, inv_h)
    gated = d_second * mask * out_gate
    d_tri = gated.astype(BF)
    d_logit = (gated * tri_proj * (1.0 - out_gate)).astype(BF)
    for r in range(step):
        ds_ref[r] = d_second[:, r * residues : (r + 1) * residues]
        dlogit_ref[r] = d_logit[:, r * residues : (r + 1) * residues]
    gz_ref[...] += mm(tri_norm, d_tri, NT)
    back = mm(wz_ref[...], d_tri)
    prod = back * hat_t
    gaint_ref[...] += sum(prod[:, r * residues : (r + 1) * residues] for r in range(step))
    comb = norm_rows_back(back * gt_ref[...], hat_t, inv_t)
    hidden = comb.shape[0] // 2
    for r in range(step):
        row = pl.program_id(0) * step + r
        own = comb[:, r * residues : (r + 1) * residues]
        tiles = fold_pair(own[:hidden], own[hidden:])
        for t in range(3):
            if stage:
                put_tile(stage[1], t, row, rows, tiles[t])
            else:
                send_ref[r, t] = tiles[t].astype(BF)

    @pl.when(pl.program_id(0) == pl.num_programs(0) - 1)
    def _():
        gains_ref[...] = jnp.concatenate([lane_sums(gaint_ref), lane_sums(gainh_ref)], axis=0)
        if stage:
            ship(stage[1], send_ref, 3, share, rows)
            devices = send_ref.shape[0]
            at = 3 * share * rows
            for acc, turned in ((gd_ref, False), (gu_ref, True), (gz_ref, False)):
                part = acc.shape[0] // devices
                block = turn_blocks(acc) if turned else acc[...]
                send_ref[:, at : at + part] = block.reshape(devices, part, LANES).astype(BF)
                at = at + part


def third_kernel(
    share, rows, sum_ref, acts_ref, ds_ref, dlogit_ref, mask_ref, mix_ref, right_ref, gx_ref,
    wt_ref, w_ref, left_ref, outer_ref, carry_ref,
    fg_ref, packed_ref, late_ref, gains_ref,
    gainx_ref, dproj_ref, acc_ref, dmix_ref, dright_ref, gout_ref, *stage,
):
    @pl.when(pl.program_id(0) == 0)
    def _():
        for acc in (dright_ref, acc_ref, gainx_ref):
            acc[...] = jnp.zeros_like(acc)
        if stage:
            unship(acts_ref, stage[0], 6, share, rows)

    hidden = wt_ref.shape[0] // 9
    step, _, residues = sum_ref.shape
    joined = lambda ref: jnp.concatenate([ref[r] for r in range(step)], axis=1)
    hat, inv = norm_rows(joined(sum_ref))
    norm = (hat * gx_ref[...]).astype(BF)
    mask = joined(mask_ref)
    for pair in range(2):
        unfolded = []
        for r in range(step):
            row = pl.program_id(0) * step + r
            tiles = range(3 * pair, 3 * pair + 3)
            if stage:
                tiles = [get_tile(stage[0], t, row, rows, hidden) for t in tiles]
            else:
                tiles = [acts_ref[r, t].astype(F32) for t in tiles]
            unfolded.append(unfold_pair(*tiles))
        for side in range(2):
            block = 2 * pair + side
            value = mm(wt_ref[block * hidden : (block + 1) * hidden], norm)
            gate = mm(wt_ref[(block + 4) * hidden : (block + 5) * hidden], norm)
            sig = jax.nn.sigmoid(gate)
            d_value = jnp.concatenate([both[side] for both in unfolded], axis=1) * mask * sig
            d_gate = d_value * value * (1.0 - sig)
            dproj_ref[block * hidden : (block + 1) * hidden] = d_value.astype(BF)
            dproj_ref[(block + 4) * hidden : (block + 5) * hidden] = d_gate.astype(BF)
    dproj_ref[8 * hidden :] = joined(dlogit_ref)
    d_proj = dproj_ref[...]
    acc_ref[...] += mm(d_proj, norm, NT)
    back = mm(w_ref[...], d_proj)
    prod = back * hat
    gainx_ref[...] += sum(prod[:, r * residues : (r + 1) * residues] for r in range(step))
    first = joined(ds_ref) + norm_rows_back(back * gx_ref[...], hat, inv)
    low = first.astype(BF)
    for r in range(step):
        own = slice(r * residues, (r + 1) * residues)
        fg_ref[r] = first[:, own]
        outer_dim = right_ref.shape[0]
        row = pl.program_id(0) * step + r
        mixed = pl.ds(pl.multiple_of(row * outer_dim, outer_dim), outer_dim)
        dmix_ref[mixed, :] = mm(right_ref[...], low[:, own], NT).astype(BF).astype(F32)
        right = mm(mix_ref[r], low[:, own])
        for half in range(dright_ref.shape[0]):
            dright_ref[half] += right[:, half * LANES : (half + 1) * LANES]

    @pl.when(pl.program_id(0) == pl.num_programs(0) - 1)
    def _():
        gains_ref[...] = lane_sums(gainx_ref)
        outer_dim, count = right_ref.shape[0], left_ref.shape[0]
        d_left = jnp.zeros((count, LANES), F32)
        below = jnp.zeros((LANES - outer_dim, LANES), BF)
        for b in range(outer_dim):
            mixed = dmix_ref[pl.ds(b, count, stride=outer_dim), :].astype(BF)
            weight = outer_ref[pl.ds(b, outer_dim, stride=outer_dim), :].astype(BF)
            d_left += mm(mixed, jnp.concatenate([weight, below], axis=0), NT)
            gout_ref[pl.ds(b, outer_dim, stride=outer_dim), :] = mm(left_ref[...], mixed, TN)
        at = 0
        for half in range(dright_ref.shape[0]):
            spread_rows(packed_ref, at, dright_ref[half].astype(BF))
            at = at + outer_dim
        spread_rows(packed_ref, at, d_left.astype(BF))
        if carry_ref.shape[0] > 1:
            spread_rows(packed_ref, packed_ref.shape[1] - carry_ref.shape[0], carry_ref[...])
        in_rows, outer_rows = acc_ref.shape[0], gout_ref.shape[0]
        late_ref[:in_rows] = turn_blocks(acc_ref).astype(BF)
        late_ref[in_rows : in_rows + outer_rows] = gout_ref[...].astype(BF)
        spare = late_ref.shape[0] - in_rows - outer_rows
        late_ref[in_rows + outer_rows :] = jnp.zeros((spare, LANES), BF)


def last_kernel(xt_ref, fg_ref, ds_ref, gain_ref, w_ref, out_ref):
    for r in range(xt_ref.shape[0]):
        hat, inv = norm_rows(xt_ref[r].astype(F32))
        back = mm(w_ref[...], ds_ref[r])
        out_ref[r] = (fg_ref[r] + norm_rows_back(back * gain_ref[...], hat, inv)).T


def norm_lanes(values):
    centred = values - jnp.mean(values, axis=1, keepdims=True)
    inv = lax.rsqrt(jnp.mean(centred * centred, axis=1, keepdims=True) + EPS)
    return centred * inv, inv


def norm_lanes_back(scaled, hat, inv):
    return inv * (
        scaled
        - jnp.mean(scaled, axis=1, keepdims=True)
        - hat * jnp.mean(scaled * hat, axis=1, keepdims=True)
    )


def head_lanes(heads, width):
    depth = width // heads
    lane = lax.broadcasted_iota(jnp.int32, (heads, width), 1)
    head = lax.broadcasted_iota(jnp.int32, (heads, width), 0)
    return ((lane >= head * depth) & (lane < (head + 1) * depth)).astype(F32)


def rows_by_head(values, lanes):
    spread = values[:, None, :] * lanes[None]
    return spread.reshape(-1, values.shape[1])


def heads_by_row(values, lanes):
    spread = values[None] * lanes[:, None, :]
    return spread.reshape(-1, values.shape[1])


def crop_rows(residues):
    return pl.ds(pl.multiple_of(lax.axis_index("crop") * residues, residues), residues)


def attend_kernel(
    both_ref, own_ref, gain_ref, w_ref, bias_ref, mask_ref,
    norm_ref, gate_ref, qkv_ref, weights_ref, low_ref, gated_ref,
):
    width = own_ref.shape[1]
    residues = mask_ref.shape[2]
    heads = bias_ref.shape[1]
    rows = own_ref.shape[0]
    scale = 1.0 / (width // heads) ** 0.5
    hat, _ = norm_lanes(both_ref[:, :width].astype(F32))
    norm_ref[...] = (hat * gain_ref[...]).astype(BF)
    gate_ref[...] = jax.nn.sigmoid(mm(norm_ref[...], w_ref[:, 3 * width :]))
    qkv_ref[...] = mm(norm_ref[crop_rows(residues), :], w_ref[:, : 3 * width]).astype(BF)
    keys, values = qkv_ref[:, width : 2 * width], qkv_ref[:, 2 * width :]
    hat, _ = norm_lanes(own_ref[...].astype(F32))
    own = (hat * gain_ref[...]).astype(BF)
    query = mm(own, w_ref[:, :width]).astype(BF).astype(F32)
    gate = jax.nn.sigmoid(mm(own, w_ref[:, 3 * width :]))
    lanes = head_lanes(heads, width)
    query = rows_by_head(query, lanes).astype(BF)
    scores = mm(query, keys, NT) * scale + bias_ref[...].reshape(rows * heads, residues)
    mask = jnp.broadcast_to(mask_ref[...], bias_ref.shape).reshape(rows * heads, residues)
    scores = jnp.where(mask > 0.5, scores, -1000000000.0)
    powers = jnp.exp(scores - jnp.max(scores, axis=1, keepdims=True))
    weights = powers / jnp.sum(powers, axis=1, keepdims=True)
    weights_ref[...] = weights
    low = weights.astype(BF)
    low_ref[...] = low
    attn = mm(low, values).reshape(rows, heads, width)
    attn = jnp.sum(attn * lanes[None], axis=1)
    gated_ref[...] = jnp.broadcast_to((gate * attn).astype(BF)[None], gated_ref.shape)


def node_chunks(rows):
    size = min(rows, LANES)
    return [slice(k * size, (k + 1) * size) for k in range(rows // size)]


def gelu_parts(up):
    square = up * up
    curve = jnp.tanh(0.7978845608 * up * (1.0 + 0.044715 * square))
    half = 0.5 * (1.0 + curve)
    slope = half + up * (1.0 - curve * curve) * (0.3989422804 + 0.05351611220 * square)
    return up * half, slope


def node_kernel(
    both_ref, gated_ref, gn_ref, gs_ref, wo_ref, wu_ref, wd_ref, wn_ref, wr_ref,
    mid_ref, next_ref, proj_ref, right_ref, norm_ref,
):
    width = gated_ref.shape[1]
    residues = right_ref.shape[1]
    for rows in node_chunks(gated_ref.shape[0]):
        mid = both_ref[rows, :width].astype(F32) + mm(gated_ref[rows], wo_ref[...])
        mid_ref[rows] = mid
        hat, _ = norm_lanes(mid)
        act, _ = gelu_parts(mm((hat * gn_ref[...]).astype(BF), wu_ref[...]))
        following = mid + mm(act.astype(BF), wd_ref[...])
        next_ref[rows] = following
        hat, _ = norm_lanes(following)
        norm = (hat * gs_ref[...]).astype(BF)
        norm_ref[rows] = norm
        proj_ref[rows] = mm(norm, wn_ref[...]).astype(BF)
    right_ref[...] = mm(wr_ref[...], norm_ref[crop_rows(residues), :], NT).astype(BF)


def sublane_sum(values):
    return jnp.sum(values, axis=0, keepdims=True)


def node_back_kernel(
    outer_dim, got_ref, left_ref, both_ref, mid_ref, next_ref, gated_ref, gate_ref,
    gn_ref, gs_ref, wo_ref, wu_ref, wd_ref, wn_ref,
    gnode_ref, gd_ref, gu_ref, gout_ref, gains_ref, gainn_ref,
    dmid_ref, dattn_ref, dgate_ref, inner_ref,
    proj_ref, norm_ref, act_ref, low_ref, trans_ref, up_ref, midlow_ref,
):
    width = gated_ref.shape[1]
    devices = got_ref.shape[0] // 2
    halves = gated_ref.shape[0] // 2 // LANES
    at = 0
    for crop in range(2):
        for half in range(halves):
            total = jnp.zeros((outer_dim, LANES), F32)
            for d in range(devices):
                part = got_ref[crop * devices + d, half * outer_dim : (half + 1) * outer_dim]
                total += part.astype(F32)
            above = jnp.zeros((outer_dim, LANES), F32)
            below = jnp.zeros((LANES - 2 * outer_dim, LANES), F32)
            turned = jnp.concatenate([above, total, below], axis=0).T
            if left_ref.shape[0] == gated_ref.shape[0]:
                left = left_ref[at : at + LANES].astype(F32)
            else:
                rows = gated_ref.shape[0] // got_ref.shape[0]
                own = slice(halves * outer_dim, halves * outer_dim + rows)
                left = got_ref[at // rows : (at + LANES) // rows, own].astype(F32)
                left = left.reshape(LANES, LANES)
            proj_ref[at : at + LANES] = (turned + left).astype(BF)
            at = at + LANES
    gains, gainn = jnp.zeros((1, width), F32), jnp.zeros((1, width), F32)
    for rows in node_chunks(gated_ref.shape[0]):
        hat, inv = norm_lanes(next_ref[rows])
        norm_ref[rows] = (hat * gs_ref[...]).astype(BF)
        back = mm(proj_ref[rows], wn_ref[...], NT)
        gains += sublane_sum(back * hat)
        d_next = both_ref[rows, width:].astype(F32)
        d_next += norm_lanes_back(back * gs_ref[...], hat, inv)
        low = d_next.astype(BF)
        low_ref[rows] = low
        hat, inv = norm_lanes(mid_ref[rows])
        trans = (hat * gn_ref[...]).astype(BF)
        trans_ref[rows] = trans
        act, slope = gelu_parts(mm(trans, wu_ref[...]))
        act_ref[rows] = act.astype(BF)
        d_up = (mm(low, wd_ref[...], NT) * slope).astype(BF)
        up_ref[rows] = d_up
        back = mm(d_up, wu_ref[...], NT)
        gainn += sublane_sum(back * hat)
        d_mid = d_next + norm_lanes_back(back * gn_ref[...], hat, inv)
        dmid_ref[rows] = d_mid
        low = d_mid.astype(BF)
        midlow_ref[rows] = low
        d_gated = mm(low, wo_ref[...], NT)
        gate = gate_ref[rows]
        product = d_gated * gated_ref[rows].astype(F32)
        inner_ref[rows] = product
        dattn_ref[rows] = (d_gated * gate).astype(BF)
        dgate_ref[rows] = (product * (1.0 - gate)).astype(BF)
    gains_ref[...] = gains
    gainn_ref[...] = gainn
    gnode_ref[...] = mm(proj_ref[...], norm_ref[...], TN)[: 2 * outer_dim]
    gd_ref[...] = mm(act_ref[...], low_ref[...], TN)
    gu_ref[...] = mm(trans_ref[...], up_ref[...], TN)
    gout_ref[...] = mm(gated_ref[...], midlow_ref[...], TN)


def attend_back_kernel(
    own_ref, dattn_ref, inner_ref, qkv_ref, values_ref, weights_ref, column_ref, norm_ref,
    ds_ref, grad_ref, bias_ref,
):
    width = own_ref.shape[1]
    residues = qkv_ref.shape[0]
    rows, _, _ = norm_ref.shape
    heads = ds_ref.shape[0] // rows
    scale = 1.0 / (width // heads) ** 0.5
    lanes = head_lanes(heads, width)
    query, keys = qkv_ref[:, :width], qkv_ref[:, width : 2 * width]
    own = rows_by_head(own_ref[...].astype(F32), lanes).astype(BF)
    d_weights = mm(own, qkv_ref[:, 2 * width :], NT)
    weights = weights_ref[...]
    inner = jnp.sum(d_weights * weights, axis=1, keepdims=True)
    d_scores = (weights * (d_weights - inner)).astype(BF)
    ds_ref[...] = d_scores
    d_query = mm(d_scores, keys).reshape(rows, heads, width)
    d_query = jnp.sum(d_query * lanes[None], axis=1) * scale
    total = jnp.zeros(bias_ref.shape, F32)
    for r in range(rows):
        total += mm(d_scores[r * heads : (r + 1) * heads], norm_ref[r], NT)
    bias_ref[...] = total
    crop = crop_rows(residues)
    d_attn = dattn_ref[crop, :]
    spread = heads_by_row(values_ref[...].astype(F32), lanes).astype(BF)
    ones = heads_by_row(jnp.ones(values_ref.shape, F32), lanes).astype(BF)
    product = inner_ref[crop, :]
    high = product.astype(BF)
    rest = (product - high.astype(F32)).astype(BF)
    inner = mm(high, ones, NT) + mm(rest, ones, NT)
    column = column_ref[...]
    d_column = (column.astype(F32) * (mm(d_attn, spread, NT) - inner)).astype(BF)
    d_key = mm(d_column, query, TN).reshape(heads, rows, width)
    d_key = jnp.sum(d_key * lanes[:, None, :], axis=0) * scale
    d_value = mm(column, d_attn, TN).reshape(heads, rows, width)
    d_value = jnp.sum(d_value * lanes[:, None, :], axis=0)
    at = 0
    for part in (d_query, d_key, d_value):
        for half in range(width // LANES):
            grad_ref[at] = part[:, half * LANES : (half + 1) * LANES].astype(BF)
            at = at + 1


def layout_kernel(parts_ref, qkv_ref, bias_ref, gainx_ref, gains_ref, out_ref):
    total = jnp.zeros(parts_ref.shape[1:], F32)
    for d in range(parts_ref.shape[0]):
        total += parts_ref[d].astype(F32)
    at = 0
    for k in range(qkv_ref.shape[0]):
        spread_rows(out_ref, at, qkv_ref[k])
        at = at + qkv_ref.shape[1]
    spread_rows(out_ref, at, total.astype(BF))
    at = at + total.shape[0]
    small = [bias_ref[...], gainx_ref[...], gains_ref[...]]
    filled = sum(part.shape[0] for part in small)
    spare = out_ref.shape[1] - at - filled
    small = jnp.concatenate(small + [jnp.zeros((spare, LANES), F32)], axis=0)
    spread_rows(out_ref, at, small.astype(BF))


def adam_refs(master_ref, first_ref, second_ref, grad, outs, rate=0.1, decay=0.1):
    found = adam_step(master_ref[...], first_ref[...], second_ref[...], grad, rate, decay)
    for ref, value in zip(outs, found):
        ref[...] = value


def adam_kernel(count, layout, *refs):
    n_pair = 1 if layout else 3
    ins = 4 * count + 9 + n_pair
    outs, sums = refs[ins : ins + 3 * count + 9], refs[ins + 3 * count + 9 :]
    for k in range(count):
        master, first, second, grad = refs[4 * k : 4 * k + 4]
        adam_refs(master, first, second, grad[...], outs[3 * k : 3 * k + 3])
    olds, pair = refs[4 * count : 4 * count + 9], refs[4 * count + 9 : ins]

    @pl.when(pl.program_id(0) == 0)
    def _():
        if layout:
            start, part_up, part_z = layout
            values = unpack_pair(pair[0][:, start:].astype(F32), part_up, part_z)
        else:
            values = [ref[...] for ref in pair]
        for ref, value in zip(sums, values):
            ref[...] = value

    for k in range(3):
        height = olds[3 * k].shape[0]
        start = pl.multiple_of(pl.program_id(0) * height, height)
        at = 3 * (count + k)
        adam_refs(*olds[3 * k : 3 * k + 3], sums[k][pl.ds(start, height), :], outs[at : at + 3])


def across(rows):
    count = rows.shape[0] // LANES
    return jnp.concatenate([rows[k * LANES : (k + 1) * LANES] for k in range(count)], axis=1)


def unpack(take, layout):
    count, late_rows, in_rows, outer_rows, small_rows = layout
    blocks, at = [], 0
    for _ in range(6):
        blocks.append(take(at, at + count).reshape(-1, LANES))
        at = at + count
    late = take(at, at + late_rows)
    late = late.reshape((-1, 2) + late.shape[1:])
    late = jnp.concatenate([late[:, 0], late[:, 1]], axis=0).reshape(-1, LANES)
    at = at + late_rows
    small = jnp.sum(take(at, at + small_rows), axis=0)
    return blocks, (late[in_rows : in_rows + outer_rows], across(late[:in_rows])), small


def unpack_pair(pair, part_up, part_z):
    devices, half_rows, _ = pair.shape
    lower, upper = pair[: devices // 2], pair[devices // 2 :]
    over = 2 * part_up - half_rows
    g_up = jnp.concatenate([lower[:, part_up:], upper[:, :over]], axis=1).reshape(-1, LANES)
    g_down = lower[:, :part_up].reshape(-1, LANES)
    return upper[:, over : over + part_z].reshape(-1, LANES), across(g_up), g_down


def final_kernel(
    layout, dgate_ref, norm_ref, both_ref, dmid_ref, gain_ref, w_ref, gainn_ref, gains_ref, *refs
):
    n_got = 1 if layout else 9
    minor, refs = refs[:6], refs[6:]
    got, refs = refs[:n_got], refs[n_got:]
    olds, refs = refs[:9], refs[9:]
    news, minor_new, (dnode_ref, grad_ref, full_ref), sums = refs[:9], refs[9:15], refs[15:18], refs[18:]
    width = dmid_ref.shape[1]

    @pl.when(pl.program_id(0) == 0)
    def _():
        if layout:
            take = lambda start, stop: got[0][:, start:stop].astype(F32)
            blocks, grads, small = unpack(take, layout)
        else:
            values = [ref[...] for ref in got]
            blocks, grads, small = values[:6], values[6:8], values[8]
        for ref, grad in zip(sums[1:], grads):
            ref[...] = grad
        for k, block in enumerate(blocks):
            grad_ref[:, k * LANES : (k + 1) * LANES] = block.astype(BF)
        grad_ref[:, 3 * width :] = dgate_ref[...]
        sums[0][...] = mm(norm_ref[...], grad_ref[...], TN)
        total = jnp.zeros((1, width), F32)
        for rows in node_chunks(dmid_ref.shape[0]):
            hat, inv = norm_lanes(both_ref[rows, :width].astype(F32))
            back = mm(grad_ref[rows], w_ref[...], NT)
            total += sublane_sum(back * hat)
            full_ref[rows] = dmid_ref[rows] + norm_lanes_back(back * gain_ref[...], hat, inv)
        if dnode_ref.shape[0] == full_ref.shape[0]:
            dnode_ref[...] = full_ref[...]
        else:
            count = dnode_ref.shape[0]
            first = lax.axis_index("crop") * (full_ref.shape[0] // 2)
            first = pl.multiple_of(first + lax.axis_index("row") * count, count)
            dnode_ref[:, 0] = full_ref[pl.ds(first, count), :]
        heads = minor[0].shape[0]
        bias = small[:heads]
        adam_refs(*minor[:3], bias, minor_new[:3])
        spots = width // LANES
        rows_of = lambda line: [line[:, k * LANES : (k + 1) * LANES] for k in range(spots)]
        gain_b = minor[3][spots : spots + 1]
        weight = minor[0][...].astype(BF).astype(F32)
        grad_b = jnp.sum(weight * bias, axis=0, keepdims=True) / gain_b
        lines = rows_of(total) + [grad_b] + rows_of(gainn_ref[...]) + rows_of(gains_ref[...])
        rest = minor[3].shape[0] - len(lines)
        lines.append(small[heads : heads + rest])
        adam_refs(*minor[3:], jnp.concatenate(lines, axis=0), minor_new[3:], 1.0, 0.0)

    for k in range(3):
        height = olds[3 * k].shape[0]
        start = pl.multiple_of(pl.program_id(0) * height, height)
        adam_refs(*olds[3 * k : 3 * k + 3], sums[k][pl.ds(start, height), :], news[3 * k : 3 * k + 3])


def whole(shape):
    return pl.BlockSpec(shape, lambda i: (0,) * len(shape))


def by_row(step, shape):
    return pl.BlockSpec((step,) + shape, lambda i: (i,) + (0,) * len(shape))


def pair_call(kernel, steps, ins, outs, args, scratch=(), flops=0, moved=0, free=(), near=()):
    args = [
        arg if at in free else pltpu.with_memory_space_constraint(arg, pltpu.HBM)
        for at, arg in enumerate(args)
    ]
    shapes = [
        shape if at in near else pltpu.HBM(shape.shape, shape.dtype)
        for at, (_, shape) in enumerate(outs)
    ]
    return pl.pallas_call(
        kernel,
        grid=(steps,),
        in_specs=ins,
        out_specs=[spec for spec, _ in outs],
        out_shape=shapes,
        scratch_shapes=list(scratch),
        compiler_params=pltpu.CompilerParams(vmem_limit_bytes=40 * 1024 * 1024),
        cost_estimate=pl.CostEstimate(flops=flops, bytes_accessed=moved, transcendentals=0),
    )(*args)


def shards(row_devices, *arrays):
    (pair_feats, node_feats, chain_ids, out_grad, node_out_grad) = arrays[:5]
    masters, firsts, seconds = arrays[5:17], arrays[17:29], arrays[29:41]
    w_attend, w_pairbias, w_attout, w_nodeup, w_nodedown = masters[:5]
    w_node, w_outer, w_in, w_z, w_up, w_down, ln_gains = masters[5:]
    count, _, residues, width_z = pair_feats.shape
    width_s = node_feats.shape[2]
    heads = w_pairbias.shape[1]
    outer_dim = w_node.shape[1] // 2
    hidden = (w_in.shape[1] - width_z) // 8
    expand = w_up.shape[1]
    every = 2 * row_devices
    shape_of = jax.ShapeDtypeStruct
    cuts = [width_s, width_z, width_s, width_s, width_z, 2 * hidden, width_z]
    gains, at = [], 0
    for cut in cuts:
        gains.append(ln_gains[at : at + cut])
        at = at + cut
    gain_a, gain_b, gain_n, gain_s, gain_x, gain_t, gain_h = gains
    column = lambda gain: gain.reshape(-1, 1)
    line = lambda gain: gain.reshape(1, -1)
    nodes = 2 * residues
    crop_index, row_index = lax.axis_index("crop"), lax.axis_index("row")
    first_row = row_index * count
    chains = chain_ids[0]
    own_chain = lax.dynamic_slice_in_dim(chains, first_row, count, 0)
    same_own = own_chain[:, None] == chains[None, :]
    mask = same_own.astype(F32)[:, None, :]
    chain_col, chain_row = chains.reshape(-1, 1), chains.reshape(1, -1)

    att_wb, attout_wb = w_attend.astype(BF), w_attout.astype(BF)
    nodeup_wb, nodedown_wb, node_wb = w_nodeup.astype(BF), w_nodedown.astype(BF), w_node.astype(BF)
    outer_wb = w_outer.astype(BF).reshape(outer_dim, outer_dim * width_z)
    bias_wb, in_wb, z_wb = w_pairbias.astype(BF), w_in.astype(BF), w_z.astype(BF)
    up_wb, down_wb = w_up.astype(BF), w_down.astype(BF)
    bias_wt, in_wt, z_wt, up_wt, down_wt = bias_wb.T, in_wb.T, z_wb.T, up_wb.T, down_wb.T

    direct = count % 16 == 0
    step = next(size for size in (4, 2, 1) if count % size == 0)
    steps = count // step
    pairs = count * residues

    node_both = jnp.concatenate([node_feats[:, 0], node_out_grad[:, 0]], axis=1)
    pair_x = pair_feats[:, 0]
    xt, bias_norm, pair_bias = pair_call(
        bias_kernel, steps,
        [by_row(step, (residues, width_z)), whole((width_z, 1)), whole((heads, width_z))],
        [(by_row(step, (width_z, residues)), shape_of((count, width_z, residues), BF)),
         (by_row(step, (width_z, residues)), shape_of((count, width_z, residues), BF)),
         (by_row(step, (heads, residues)), shape_of((count, heads, residues), F32))],
        [pair_x, column(gain_b), bias_wt], free=(0, 1, 2), near=(2,),
        flops=2 * pairs * width_z * heads, moved=4 * pairs * width_z,
    )

    def own_rows(values):
        return lax.dynamic_slice_in_dim(values, crop_index * residues + first_row, count, 0)

    def single(kernel, outs, args, scratch=(), flops=0, far=(), apart=False):
        moved = sum(arg.size * 4 for arg in args)
        return pair_call(
            kernel, 1, [whole(arg.shape) for arg in args],
            [(whole(shape), shape_of(shape, kind)) for shape, kind in outs],
            args, scratch, flops, moved, (0,) if apart else range(len(args)),
            [at for at in range(len(outs)) if at not in far],
        )

    columns = [column(gain) for gain in (gain_x, gain_t, gain_h)]
    ready = [att_wb, attout_wb, nodeup_wb, nodedown_wb, mask]
    node_both, _ = gather_all(
        spread_over(node_both, row_devices), row_devices, [xt, pair_bias] + ready
    )
    node_both = node_both.reshape(nodes, 2 * width_s)
    square = (nodes, width_s)
    att_norm, gate_all, qkv_crop, att_weights, weights_low, gated_own = single(
        attend_kernel,
        [(square, BF), (square, F32), ((residues, 3 * width_s), BF),
         ((count * heads, residues), F32), ((count * heads, residues), BF),
         ((every, count, width_s), BF)],
        [node_both, node_feats[:, 0], line(gain_a), att_wb, pair_bias, mask],
        flops=8 * nodes * width_s * width_s, far=(0, 1, 2, 3),
    )
    weights_cut = weights_low.reshape(count, heads, row_devices, count).transpose(2, 0, 1, 3)
    if direct:
        weights_cut = weights_cut.reshape(row_devices, -1, LANES)
    ready = [weights_cut, node_wb, outer_wb, in_wt, chain_col, columns[0]]
    gated = lax.all_to_all(gated_own, BOTH, split_axis=0, concat_axis=0, tiled=True)
    gated = after(gated, ready).reshape(nodes, width_s)

    node_mid, node_next, node_proj, right_t = single(
        node_kernel,
        [(square, F32), (square, F32), ((nodes, 2 * outer_dim), BF), ((outer_dim, residues), BF)],
        [node_both, gated, line(gain_n), line(gain_s), attout_wb, nodeup_wb, nodedown_wb, node_wb,
         node_wb[:, outer_dim:].T],
        scratch=[pltpu.VMEM(square, BF)], flops=18 * nodes * width_s * width_s, far=(0, 1),
    )
    node_out = own_rows(node_next).astype(BF)[:, None]
    left_vec = own_rows(node_proj[:, :outer_dim])
    outer_mix = mm(left_vec, outer_wb).astype(BF).reshape(count, outer_dim, width_z)

    share = hidden // row_devices
    dims = (share, count) if direct else None

    def sent_block(tiles, extra=0):
        if direct:
            shape = (row_devices, tiles * share * count + extra, LANES)
            return whole(shape), shape_of(shape, BF)
        return by_row(step, (tiles, hidden, LANES)), shape_of((count, tiles, hidden, LANES), BF)

    def stage(tiles):
        return [pltpu.VMEM((tiles * hidden * count, LANES), F32)] if direct else []

    def swap(block):
        return lax.all_to_all(block, "row", split_axis=0, concat_axis=0, tiled=True)

    def to_channels(block):
        if direct:
            return swap(block)
        tiles = block.shape[1]
        cut = block.reshape(count, tiles, row_devices, share, LANES)
        sent = swap(cut.transpose(2, 1, 3, 0, 4))
        return sent.transpose(1, 2, 0, 3, 4).reshape(1, tiles, share, residues, LANES)

    def to_rows(block):
        if direct:
            return swap(block.reshape(row_devices, -1, LANES))
        tiles = block.shape[1]
        cut = block.reshape(tiles, share, row_devices, count, LANES)
        got = swap(cut.transpose(2, 0, 1, 3, 4))
        return got.transpose(3, 1, 0, 2, 4).reshape(count, tiles, hidden, LANES)

    def tri_out(tiles):
        if not direct:
            return tri_block(tiles)
        shape = (row_devices, tiles, share, count, LANES)
        each = share // tri_steps(share)
        block = (row_devices, tiles, each, count, LANES)
        return pl.BlockSpec(block, lambda i: (0, 0, i, 0, 0)), shape_of(shape, BF)

    def tri_block(tiles, extra=0):
        if direct:
            return sent_block(tiles, extra)
        shape = (1, tiles, share, residues, LANES)
        spec = pl.BlockSpec((1, tiles, 1, residues, LANES), lambda i: (0, 0, i, 0, 0))
        return spec, shape_of(shape, BF)

    ride = weights_cut if direct else jnp.zeros((1, 1, LANES), BF)
    extra = ride.shape[1]
    first_sum, acts_own = pair_call(
        functools.partial(first_kernel, share, count), steps,
        [by_row(step, (width_z, residues)), by_row(step, (outer_dim, width_z)),
         whole((outer_dim, residues)), by_row(step, (1, residues)), whole((width_z, 1)),
         whole(in_wt.shape), whole(ride.shape)],
        [(by_row(step, (width_z, residues)), shape_of((count, width_z, residues), F32)),
         sent_block(6, extra)],
        [xt, outer_mix, right_t, mask, column(gain_x), in_wt, ride],
        scratch=stage(6),
        flops=16 * pairs * width_z * hidden, moved=12 * pairs * width_z,
    )

    tri_steps = lambda channels: channels // 2 if direct and channels % 2 == 0 else channels
    chain_specs = [whole((residues, 1)), whole((1, residues))]
    product = 2 * share * residues**3
    ready = [in_wb, z_wb, up_wb, down_wb, z_wt, up_wt, down_wt] + columns
    acts = after(to_channels(acts_own), ready)
    weights_col = acts[:, 6 * share * count :] if direct else swap(weights_cut)
    weights_col = weights_col.reshape(residues, heads * count)
    (tri,) = pair_call(
        functools.partial(tri_kernel, dims), tri_steps(share), chain_specs + [tri_block(6, extra)[0]],
        [tri_out(3)], [chain_col, chain_row, acts], free=(0, 1, 2),
        flops=2 * product, moved=share * residues * 9 * 256,
    )
    tri_rows = to_rows(tri)

    slab = by_row(step, (width_z, residues))
    second_args = [
        (by_row(step, (width_z, residues)), first_sum),
        (sent_block(3)[0], tri_rows),
        (by_row(step, (residues, width_z)), out_grad[:, 0]),
        (by_row(step, (1, residues)), mask),
    ]
    second_args += [
        (whole(v.shape), v)
        for v in (
            column(gain_x), column(gain_t), column(gain_h),
            in_wt[8 * hidden :], z_wt, z_wb, up_wt, up_wb, down_wt, down_wb,
        )
    ]
    part_up, part_z = expand // row_devices, 2 * hidden // row_devices
    half_rows = part_up + part_up // 2
    carried = 2 * part_up + part_z if direct else 0
    acc_shapes = [
        (expand, width_z), (expand, width_z), (2 * hidden, width_z),
        ((2 * hidden + width_z) // LANES, LANES),
    ]
    pair_out, d_second, d_logit, dtri_own, g_down, g_up_t, g_z, gains_th = pair_call(
        functools.partial(second_kernel, share, count), steps,
        [spec for spec, _ in second_args],
        [(by_row(step, (residues, width_z)), shape_of((count, residues, width_z), BF)),
         (slab, shape_of((count, width_z, residues), F32)),
         (slab, shape_of((count, width_z, residues), BF)),
         sent_block(3, carried)]
        + [(whole(s), shape_of(s, F32)) for s in acc_shapes],
        [arg for _, arg in second_args], free=(1,),
        scratch=[pltpu.VMEM((2 * hidden, residues), F32), pltpu.VMEM((width_z, residues), F32)]
        + stage(3) + stage(3),
        flops=12 * pairs * width_z * expand, moved=20 * pairs * width_z,
    )

    dtri = to_channels(dtri_own)
    if direct:
        grad_parts = dtri[:, 3 * share * count :]
    else:
        turned = g_up_t.reshape(-1, LANES, LANES).transpose(0, 2, 1)
        parts = [g.reshape(row_devices, -1, LANES) for g in (g_down, turned, g_z)]
        grad_parts = swap(jnp.concatenate(parts, axis=1).astype(BF))
    row_sum = jnp.sum(grad_parts.astype(F32), axis=0)
    row_sum = jnp.pad(row_sum, ((0, 2 * half_rows - row_sum.shape[0]), (0, 0)))
    lower, upper = row_sum[:half_rows], row_sum[half_rows:]
    low_crop = crop_index == 0
    theirs = lax.ppermute(jnp.where(low_crop, upper, lower), "crop", [(0, 1), (1, 0)])
    pair_own = (jnp.where(low_crop, lower, upper) + theirs).astype(BF)
    (dacts,) = pair_call(
        functools.partial(tri_back_kernel, dims), tri_steps(share),
        chain_specs + [tri_block(6, extra)[0], tri_block(3, carried)[0]],
        [tri_out(6)], [chain_col, chain_row, acts, dtri], free=(0, 1, 2, 3),
        flops=4 * product, moved=share * residues * 15 * 256,
    )
    dacts_rows = after(to_rows(dacts), pair_own)

    right_rows = residues // LANES * outer_dim
    left_rows = -(-count // 16) * 16
    carry = pair_own if direct else jnp.zeros((1, LANES), BF)
    packed_rows = right_rows + left_rows + (half_rows if direct else 0)
    in_rows, outer_rows = in_wt.shape[0], w_outer.shape[0]
    late_rows = -(-(in_rows + outer_rows) // (every * 16)) * every * 16
    first_grad, packed, late, gains_x = pair_call(
        functools.partial(third_kernel, share, count), steps,
        [slab, sent_block(6)[0], slab, slab, by_row(step, (1, residues)),
         by_row(step, (outer_dim, width_z)), whole((outer_dim, residues)), whole((width_z, 1)),
         whole(in_wt.shape), whole(in_wb.shape), whole(left_vec.shape), whole(w_outer.shape),
         whole(carry.shape)],
        [(slab, shape_of((count, width_z, residues), F32)),
         (whole((row_devices, packed_rows, LANES)),
          shape_of((row_devices, packed_rows, LANES), BF)),
         (whole((late_rows, LANES)), shape_of((late_rows, LANES), BF)),
         (whole((width_z // LANES, LANES)), shape_of((width_z // LANES, LANES), F32))],
        [first_sum, dacts_rows, d_second, d_logit, mask, outer_mix, right_t, columns[0],
         in_wt, in_wb, left_vec, w_outer, carry],
        free=(1,),
        scratch=[pltpu.VMEM((width_z, residues), F32), pltpu.VMEM((9 * hidden, step * residues), BF),
                 pltpu.VMEM(in_wt.shape, F32), pltpu.VMEM((count * outer_dim, LANES), F32),
                 pltpu.VMEM((residues // LANES, outer_dim, LANES), F32),
                 pltpu.VMEM(w_outer.shape, F32)] + stage(6),
        flops=54 * pairs * width_z * hidden, moved=20 * pairs * width_z,
    )
    late = late.reshape(2, late_rows // 2, LANES)
    odd = row_index % 2 == 1
    theirs = core_exchange(jnp.where(odd, late[0], late[1]), row_devices)
    late = jnp.where(odd, late[1], late[0]).astype(F32) + theirs.astype(F32)
    late = late.astype(BF).reshape(row_devices, -1, LANES)
    got, first_got = gather_all(packed, row_devices, late)
    late_parts = same_core_exchange(after(late, first_got), row_devices)
    left_all = left_vec
    if not direct:
        left_all = got[:, right_rows : right_rows + count].reshape(nodes, LANES)

    wide_node = jnp.pad(node_wb, ((0, 0), (0, LANES - 2 * outer_dim)))
    tall, low_square = (nodes, w_nodeup.shape[1]), pltpu.VMEM(square, BF)
    (g_node, g_nodedown, g_nodeup, g_attout, gain_s_grad, gain_n_grad,
     grad_mid, d_attn, d_gate, inner) = single(
        functools.partial(node_back_kernel, outer_dim),
        [((2 * outer_dim, width_s), F32), (w_nodedown.shape, F32), (w_nodeup.shape, F32),
         (w_attout.shape, F32), ((1, width_s), F32), ((1, width_s), F32),
         (square, F32), (square, BF), (square, BF), (square, F32)],
        [got, left_all, node_both, node_mid, node_next, gated, gate_all,
         line(gain_n), line(gain_s), attout_wb, nodeup_wb, nodedown_wb, wide_node],
        scratch=[pltpu.VMEM((nodes, LANES), BF), low_square, pltpu.VMEM(tall, BF), low_square,
                 low_square, pltpu.VMEM(tall, BF), low_square],
        flops=50 * nodes * width_s * width_s, far=(0, 1, 2, 3, 4, 5, 6, 8), apart=True,
    )

    values_own = lax.dynamic_slice(qkv_crop, (first_row, 2 * width_s), (count, width_s))
    score_grad, qkv_grad, g_bias_t = single(
        attend_back_kernel,
        [((count * heads, residues), BF), ((3 * width_s // LANES, count, LANES), BF),
         ((heads, width_z), F32)],
        [own_rows(d_attn), d_attn, inner, qkv_crop, values_own, att_weights, weights_col,
         bias_norm],
        flops=12 * count * heads * residues * width_s,
    )

    qkv_rows, share_rows = qkv_grad.size // LANES, late_parts.shape[1]
    small_rows = heads + gains_x.shape[0] + gains_th.shape[0]
    small_rows = small_rows + -small_rows % 16
    layout = (count, share_rows, in_rows, outer_rows, small_rows)
    last_shape = (row_devices, qkv_rows + share_rows + small_rows, LANES)
    pieces = [late_parts, qkv_grad, g_bias_t, gains_x, gains_th]
    if direct:
        (last_own,) = single(layout_kernel, [(last_shape, BF)], pieces)
    else:
        small = jnp.concatenate(pieces[2:])
        small = jnp.pad(small, ((0, small_rows - small.shape[0]), (0, 0)))
        late_own = jnp.sum(late_parts.astype(F32), axis=0)
        last_own = [qkv_grad.reshape(-1, LANES).astype(F32), late_own, small]
        last_own = spread_over(jnp.concatenate(last_own).astype(BF), row_devices)

    (pair_grad,) = pair_call(
        last_kernel, steps,
        [slab, slab, by_row(step, (heads, residues)), whole((width_z, 1)), whole((width_z, heads))],
        [(by_row(step, (residues, width_z)), shape_of((count, residues, width_z), F32))],
        [xt, first_grad, score_grad.reshape(count, heads, residues), column(gain_b), bias_wb],
        flops=4 * pairs * width_z * heads, moved=10 * pairs * width_z,
    )

    parts = 2
    split = lambda k: pl.BlockSpec((olds[k].shape[0] // parts, olds[k].shape[1]), lambda i: (i, 0))
    updated = {}

    early = {2: g_attout, 3: g_nodeup, 4: g_nodedown, 5: g_node}
    turned = lambda k, value: value.T if k == 5 else value
    specs, args, outs = [], [], []
    for k, grad in early.items():
        spec = pl.BlockSpec((grad.shape[0] // parts, grad.shape[1]), lambda i: (i, 0))
        specs += [spec] * 4
        args += [turned(k, old[k]) for old in (masters, firsts, seconds)] + [grad]
        outs += [(spec, shape_of(grad.shape, F32))] * 3
    pair_keys = (8, 9, 10)
    for k in pair_keys:
        height, width = masters[k].shape
        spec = pl.BlockSpec((height // parts, width), lambda i: (i, 0))
        specs += [spec] * 3
        args += [masters[k], firsts[k], seconds[k]]
        outs += [(spec, shape_of((height, width), F32))] * 3
    if direct:
        pair_got, pair_layout = [got], (right_rows + left_rows, part_up, part_z)
    else:
        pair_all, _ = gather_all(spread_over(pair_own, row_devices), row_devices)
        pair_got, pair_layout = list(unpack_pair(pair_all.astype(F32), part_up, part_z)), None
    specs += [whole(arg.shape) for arg in pair_got]
    args += pair_got
    found = pair_call(
        functools.partial(adam_kernel, len(early), pair_layout), parts, specs, outs, args,
        scratch=[pltpu.VMEM(masters[k].shape, F32) for k in pair_keys],
        moved=sum(7 * arg.size for arg in args),
    )
    beside = (pair_grad, found[0], node_out)
    last, _ = gather_all(last_own, row_devices, beside)
    for at, k in enumerate(early):
        updated[k] = [turned(k, value) for value in found[3 * at : 3 * at + 3]]
    for at, k in enumerate(pair_keys, len(early)):
        updated[k] = found[3 * at : 3 * at + 3]

    late_keys = (0, 6, 7)
    got_last = [last]
    if not direct:
        blocks, sums, small = unpack(lambda a, b: last[:, a:b].astype(F32), layout)
        got_last = blocks + list(sums) + [small]
    node_shape = (count, 1, width_s) if direct else square
    minor = [old[1].T for old in (masters, firsts, seconds)]
    minor += [old[11].reshape(-1, LANES) for old in (masters, firsts, seconds)]
    fixed = [d_gate, att_norm, node_both, grad_mid, line(gain_a), att_wb, gain_n_grad, gain_s_grad]
    fixed = fixed + minor + got_last
    olds, specs = [], [whole(arg.shape) for arg in fixed]
    for k in late_keys:
        olds += [masters[k], firsts[k], seconds[k]]
    blocked = [split(k) for k in range(len(olds))]
    found = pair_call(
        functools.partial(final_kernel, layout if direct else None), parts, specs + blocked,
        [(spec, shape_of(old.shape, F32)) for spec, old in zip(blocked, olds)]
        + [(whole(value.shape), shape_of(value.shape, F32)) for value in minor]
        + [(whole(node_shape), shape_of(node_shape, F32))],
        fixed + olds,
        scratch=[pltpu.VMEM((nodes, 4 * width_s), BF), pltpu.VMEM(square, F32)]
        + [pltpu.VMEM(masters[k].shape, F32) for k in late_keys],
        flops=16 * nodes * width_s * width_s, moved=sum(7 * old.size for old in olds),
    )
    for at, k in enumerate(late_keys):
        updated[k] = found[3 * at : 3 * at + 3]
    updated[1] = [value.T for value in found[9:12]]
    updated[11] = [value.reshape(-1) for value in found[12:15]]
    node_grad = found[15] if direct else own_rows(found[15])[:, None]
    results = [pair_out[:, None], node_out, pair_grad[:, None], node_grad]
    for k in range(12):
        results.extend(updated[k])
    return tuple(results)


def solution(mesh):
    rows4, rows3 = P("row", "crop", None, None), P("row", "crop", None)
    return jax.shard_map(
        functools.partial(shards, mesh.shape["row"]),
        mesh=mesh,
        in_specs=(rows4, rows3, P("crop", None), rows4, rows3) + (P(),) * 36,
        out_specs=(rows4, rows3, rows4, rows3) + (P(),) * 36,
        check_vma=False,
    )
```
